32 devices in a mesh: row: 4 (over y, x), col: 8 (over z, core).
Axes of the slice: x: 2, y: 2, z: 4, core: 2. Of those that a mesh axis runs over, the one named last changes fastest.
Arguments:
- features: float32 [2, 64, 512, 128], P(None, 'row', 'col'), may hold values from -6 to 6
- cotangent: float32 [2, 64, 512, 128], P(None, 'row', 'col'), may hold values from -6 to 6
- conv_kernel: float32 [7, 7, 128], P(None, None, ('row', 'col')), may hold values from -0.875 to 0.875
- conv_bias: float32 [128], P(('row', 'col')), may hold values from -3 to 3
- norm_gain: float32 [128], P(('row', 'col')), may hold values from 0.1 to 1.9
- norm_shift: float32 [128], P(('row', 'col')), may hold values from -2 to 2
- w_in: float32 [128, 512], P(None, ('row', 'col')), may hold values from -0.5 to 0.5
- in_bias: float32 [512], P(('row', 'col')), may hold values from -3 to 3
- w_out: float32 [512, 128], P(('row', 'col')), may hold values from -0.25 to 0.25
- out_bias: float32 [128], P(('row', 'col')), may hold values from -3 to 3
- layer_scale: float32 [128], P(('row', 'col')), may hold values from 0.5 to 1.5
Outputs:
- features_grad: float32 [2, 64, 512, 128], P(None, 'row', 'col')
- kernel_grad: float32 [7, 7, 128], P(None, None, ('row', 'col'))
- conv_bias_grad: float32 [128], P(('row', 'col'))
- gain_grad: float32 [128], P(('row', 'col'))
- shift_grad: float32 [128], P(('row', 'col'))
- w_in_grad: float32 [128, 512], P(None, ('row', 'col'))
- in_bias_grad: float32 [512], P(('row', 'col'))
- w_out_grad: float32 [512, 128], P(('row', 'col'))
- out_bias_grad: float32 [128], P(('row', 'col'))
- scale_grad: float32 [128], P(('row', 'col'))
The draws below stay inside these ranges and needn't reach their ends.
All inputs are finite; a program needn't handle non-finite values.
Results may differ from the reference program's by a relative error of at most 0.0003.
Values sent between devices are 32-bit elements; how exact they have to be, the bound alone decides.
No kernel may reach another device: no remote copies, remote signals or barrier semaphores. Data moves between devices by JAX's collectives and lax.ppermute only.
A program may use at most 64 MiB of HBM per device.

```python
import math
import jax
import jax.numpy as jnp
from jax import lax

C = 128
HID = 512
K = 7
BATCH = 2
IMG_H = 64
IMG_W = 512


def block_levels(rng, dims, shards, least, largest):
    factor_of, own = 1.0, jax.random.fold_in(rng, 6)
    for dim, shards_of in shards:
        steps = jnp.exp(jax.random.uniform(jax.random.fold_in(own, dim), (shards_of,), jnp.float32, least / len(shards), largest / len(shards)))
        factor_of = factor_of * jnp.repeat(steps, dims[dim] // shards_of).reshape([-1 if axis == dim else 1 for axis in range(len(dims))])
    return factor_of


def normal_values(own_key, shape, scale, reach, split=(), dtype=jnp.bfloat16):
    level = block_levels(own_key, shape, split, -0.22, 0.18) if split else 1.0
    array = jax.random.normal(own_key, shape, jnp.float32) * scale * level
    return jnp.minimum(jnp.maximum(array, -reach), reach).astype(dtype)


def setup_inputs(seed: int = 0) -> dict:
    keys = jax.random.split(jax.random.key(seed), 12)
    features = normal_values(keys[0], (BATCH, IMG_H, IMG_W, C), 1.0, 6.0, ((1, 4), (2, 8)), jnp.float32)
    cotangent = normal_values(keys[1], (BATCH, IMG_H, IMG_W, C), 1.0, 6.0, ((1, 4), (2, 8)), jnp.float32)
    conv_kernel = normal_values(keys[2], (K, K, C), (K * K) ** -0.5, 0.875, ((2, 32),), jnp.float32)
    conv_bias = normal_values(keys[3], (C,), 0.5, 3.0, ((0, 32),), jnp.float32)
    norm_gain = jnp.clip(1.0 + 0.18 * jax.random.normal(keys[4], (C,), jnp.float32), 0.1, 1.9)
    norm_shift = normal_values(keys[5], (C,), 0.3, 2.0, ((0, 32),), jnp.float32)
    w_in = normal_values(keys[6], (C, HID), C ** -0.5, 0.5, ((1, 32),), jnp.float32)
    in_bias = normal_values(keys[7], (HID,), 0.5, 3.0, ((0, 32),), jnp.float32)
    w_out = normal_values(keys[8], (HID, C), HID ** -0.5, 0.25, ((0, 32),), jnp.float32)
    out_bias = normal_values(keys[9], (C,), 0.5, 3.0, ((0, 32),), jnp.float32)
    layer_scale = jnp.clip(0.5 + 1.0 * jax.random.uniform(keys[10], (C,), jnp.float32) ** block_levels(keys[10], (C,), ((0, 32),), -0.2, 0.2), 0.5, 1.5)
    return {"features": features, "cotangent": cotangent, "conv_kernel": conv_kernel, "conv_bias": conv_bias, "norm_gain": norm_gain, "norm_shift": norm_shift, "w_in": w_in, "in_bias": in_bias, "w_out": w_out, "out_bias": out_bias, "layer_scale": layer_scale}


norm_eps = 1e-06

def depthwise(field, kernel):
    return lax.conv_general_dilated(field, kernel[:, :, None, :], (1, 1), 'VALID', dimension_numbers=('NHWC', 'HWIO', 'NHWC'), feature_group_count=field.shape[-1], precision=lax.Precision.HIGHEST)

def mixing(conv_out, norm_gain, norm_shift, w_in, in_bias, w_out, out_bias, layer_scale):
    mean = lax.optimization_barrier(jnp.mean(conv_out, -1, keepdims=True))
    centred = conv_out - mean
    variance = lax.optimization_barrier(jnp.mean(centred * centred, -1, keepdims=True))
    normed = centred * lax.rsqrt(variance + norm_eps)
    lin = normed * norm_gain + norm_shift
    act = jnp.einsum('bhwc,ck->bhwk', lin, w_in, precision=lax.Precision.HIGHEST) + in_bias
    hidden = jax.nn.gelu(act, approximate=False)
    branch = jnp.einsum('bhwk,kc->bhwc', hidden, w_out, precision=lax.Precision.HIGHEST) + out_bias
    return branch * layer_scale

def reference(features, cotangent, conv_kernel, conv_bias, norm_gain, norm_shift, w_in, in_bias, w_out, out_bias, layer_scale):
    margin = K // 2
    padded = jnp.pad(features, ((0, 0), (margin, margin), (margin, margin), (0, 0)))
    conv_out = depthwise(padded, conv_kernel) + conv_bias
    params = (norm_gain, norm_shift, w_in, in_bias, w_out, out_bias, layer_scale)
    block = math.gcd(IMG_H, 16)
    count = IMG_H // block
    conv_blocks = jnp.moveaxis(conv_out.reshape(BATCH, count, block, IMG_W, C), 1, 0)
    cot_blocks = jnp.moveaxis(cotangent.reshape(BATCH, count, block, IMG_W, C), 1, 0)

    def step(carry, pair):
        conv_piece, cot_piece = pair
        outcome, pullback = jax.vjp(mixing, conv_piece, *params)
        grads = pullback(cot_piece)
        carry = tuple((total + part for total, part in zip(carry, grads[1:])))
        return (carry, grads[0])
    start = tuple((jnp.zeros_like(p) for p in params))
    totals, dconv_blocks = lax.scan(step, start, (conv_blocks, cot_blocks))
    d_conv = jnp.moveaxis(dconv_blocks, 0, 1).reshape(BATCH, IMG_H, IMG_W, C)
    conv_value, conv_pull = jax.vjp(depthwise, padded, conv_kernel)
    d_padded, kernel_grad = conv_pull(d_conv)
    features_grad = cotangent + d_padded[:, margin:-margin, margin:-margin]
    factor = 1.0 / math.sqrt(BATCH * IMG_H * IMG_W)
    bias_grad = lax.optimization_barrier(jnp.sum(d_conv, axis=(0, 1, 2)))
    gain_g, shift_g, win_g, inb_g, wout_g, outb_g, scale_g = totals
    return (features_grad, kernel_grad * factor, bias_grad * factor, gain_g * factor, shift_g * factor, win_g * factor, inb_g * factor, wout_g * factor, outb_g * factor, scale_g * factor)
```

```python
import functools
import math

import jax
import jax.numpy as jnp
from jax import lax
from jax.experimental import pallas as pl
from jax.experimental.pallas import tpu as pltpu
from jax.sharding import PartitionSpec as P

norm_eps = 1e-06
inverse_root_twopi = 0.3989422804014327
half_log2e = 0.7213475204444817
tail_p = 0.275
tail_c = (
    0.1178092510180382,
    0.04211149421929024,
    0.3339322641039753,
    -0.33099338058058636,
    0.45199870802757525,
    -0.11485833206946416,
)
AXES = ("row", "col")
LANES = 128
LEFT = 8
NN = (((1,), (0,)), ((), ()))
NT = (((1,), (1,)), ((), ()))
f32, bf16 = jnp.float32, jnp.bfloat16
VMEM_LIMIT = 48 * 1024 * 1024


def ceil8(n):
    return (n + 7) // 8 * 8


def call(body, outs, scratch=(), flops=0, size=0):
    return pl.pallas_call(
        body,
        out_shape=outs,
        scratch_shapes=list(scratch),
        compiler_params=pltpu.CompilerParams(vmem_limit_bytes=VMEM_LIMIT),
        cost_estimate=pl.CostEstimate(flops=flops, bytes_accessed=size, transcendentals=0),
    )


def shape(*dims):
    return jax.ShapeDtypeStruct(dims, f32)


def device_index(mesh_shape):
    return lax.axis_index("row") * mesh_shape["col"] + lax.axis_index("col")


def split(x):
    high = x.astype(bf16)
    return high, (x - high.astype(f32)).astype(bf16)


def dot(a, b, dims):
    return lax.dot_general(a, b, dims, preferred_element_type=f32)


def exchange_order(x, unit, count, me):
    rows = x.shape[0]
    index = lax.broadcasted_iota(jnp.int32, x.shape, 0)
    step = unit
    bit = 1
    while bit < count:
        up = pltpu.roll(x, step, 0)
        down = pltpu.roll(x, rows - step, 0)
        swapped = jnp.where((index & step) != 0, up, down)
        x = jnp.where((me & bit) != 0, swapped, x)
        step *= 2
        bit *= 2
    return x


def pack_body(ms, kernel_ref, cb, ng, ns, ob, ls, win_ref, ib, wout_ref, out_ref):
    taps_i, cs, taps_j = kernel_ref.shape
    hs = win_ref.shape[0]
    taps = taps_i * taps_j
    out_ref[...] = jnp.zeros_like(out_ref)
    out_ref[0:hs, :] = win_ref[...]
    out_ref[hs : 2 * hs, :] = wout_ref[...]
    base = 2 * hs
    for i in range(taps_i):
        out_ref[base : base + cs, i * taps_j : (i + 1) * taps_j] = kernel_ref[i]
    for n, ref in enumerate((cb, ng, ns, ob, ls)):
        column = jnp.broadcast_to(ref[...], (8, cs)).T
        out_ref[base : base + cs, taps + n : taps + n + 1] = column[:, 0:1]
    out_ref[base + cs : base + cs + 1, 0:hs] = ib[...]


def depthwise_block(read, weight, rows, taps_i, taps_j, start):
    acc = start
    for j in range(taps_j):
        w = [weight(i, j) for i in range(taps_i)]
        for r in range(rows + taps_i - 1):
            s = read(r, j)
            for i in range(taps_i):
                p = r - i
                if 0 <= p < rows:
                    term = w[i] * s
                    acc[p] = term if acc[p] is None else acc[p] + term
    return acc


def fill(dst, inner, top, bottom, left, right):
    batch, rows, cols, _ = inner.shape
    m = top.shape[1]
    for b in range(batch):
        dst[b, m : m + rows, LEFT : LEFT + cols, :] = inner[b]
        dst[b, 0:m, LEFT : LEFT + cols, :] = top[b]
        dst[b, m + rows : m + rows + m, LEFT : LEFT + cols, :] = bottom[b]
        dst[b, :, LEFT - m : LEFT, :] = left[b]
        dst[b, :, LEFT + cols : LEFT + cols + m, :] = right[b]


def small_columns(slots_ref, hs, cs, count, me, order, scratch):
    base = 2 * hs
    for s in range(count):
        scratch[order[s] * cs : (order[s] + 1) * cs, :] = slots_ref[s, base : base + cs, :]
    return exchange_order(scratch[...], cs, count, me)


def mix_body(
    ms, order, factor, taps_i, taps_j, tile,
    feat, top, bottom, left, right, slots_ref, cot_ref,
    src_ref, dconv_ref, edge_top, edge_bottom, grads_ref, chan_ref, small_ref,
    conv_scr, cols_scr, kb_scr, win_scr, wout_scr, w1_scr, w2_scr, w4_scr, bias_scr,
    gw1_scr, gw2_scr, gb_scr, gg_scr, gs_scr, gc_scr, cot_sum,
):
    batch, rows, cols, C = feat.shape
    count = slots_ref.shape[0]
    cs = C // count
    taps = taps_i * taps_j
    m = taps_i // 2
    hid = win_scr.shape[0]
    hs = hid // count
    me = device_index(ms)

    fill(src_ref, feat, top, bottom, left, right)
    columns = small_columns(slots_ref, hs, cs, count, me, order, cols_scr)
    cols_scr[...] = columns
    rows_form = columns.T
    small_ref[...] = rows_form
    for t in range(taps):
        kb_scr[t] = jnp.broadcast_to(rows_form[t : t + 1, :], (8, C))
    conv_bias = jnp.broadcast_to(rows_form[taps : taps + 1, :], (8, C))

    for s in range(count):
        win_scr[s * hs : (s + 1) * hs, :] = slots_ref[s, 0:hs, :]
        wout_scr[s * hs : (s + 1) * hs, :] = slots_ref[s, hs : 2 * hs, :]
    for s in range(count):
        cols_bias = jnp.broadcast_to(slots_ref[s, 2 * hs + cs : 2 * hs + cs + 1, :], (LANES, LANES)).T
        bias_scr[s * hs : (s + 1) * hs, :] = cols_bias[0:hs, :]

    scale_row = rows_form[taps + 4 : taps + 5, :]
    wh, wl = split(win_scr[...])
    w1_scr[:, 0:C] = wh
    w1_scr[:, C : 2 * C] = wl
    w1_scr[:, 2 * C : 3 * C] = wh
    oh, ol = split(wout_scr[...] * scale_row)
    w2_scr[:, 0:C] = oh
    w2_scr[:, C : 2 * C] = ol
    w2_scr[:, 2 * C : 3 * C] = oh
    th, tl = split(win_scr[...].T)
    w4_scr[0:C, :] = th
    w4_scr[C : 2 * C, :] = tl

    def conv_step(b, _):
        for q in range(0, cols, 8):
            acc = depthwise_block(
                lambda r, j: src_ref[b, r, LEFT - m + q + j : LEFT - m + q + j + 8, :],
                lambda i, j: kb_scr[i * taps_j + j],
                rows, taps_i, taps_j, [conv_bias] * rows,
            )
            for p in range(rows):
                conv_scr[b, p, q : q + 8, :] = acc[p]
        return 0

    lax.fori_loop(0, batch, conv_step, 0)

    for ref in (gw1_scr, gw2_scr, gb_scr, gg_scr, gs_scr, gc_scr, cot_sum):
        ref[...] = jnp.zeros_like(ref)
    tile_rows = tile // cols
    per_image = rows // tile_rows
    gain = cols_scr[:, taps + 1 : taps + 2]
    shift = cols_scr[:, taps + 2 : taps + 3]

    def lanes_sum(x):
        total = x[:, 0:LANES]
        for k in range(LANES, x.shape[1], LANES):
            total = total + x[:, k : k + LANES]
        return total

    def step(t, _):
        b = t // per_image
        p0 = (t % per_image) * tile_rows
        x = conv_scr[b, pl.ds(p0, tile_rows)].reshape(tile, C).T
        mean = jnp.mean(x, axis=0, keepdims=True)
        centred = x - mean
        variance = jnp.mean(centred * centred, axis=0, keepdims=True)
        inverse = lax.rsqrt(variance + norm_eps)
        normed = centred * inverse
        lin = normed * gain + shift
        lh, ll = split(lin)
        cot = cot_ref[b, pl.ds(p0, tile_rows)].reshape(tile, C)
        ch, cl = split(cot)
        act = dot(w1_scr[...], jnp.concatenate([lh, lh, ll], axis=0), NN)
        d_hid = dot(w2_scr[...], jnp.concatenate([ch, ch, cl], axis=1), NT)
        bias = bias_scr[...]
        act = act + jnp.concatenate([bias] * (tile // LANES), axis=1)
        e = jnp.exp2((act * act) * (-half_log2e))
        d = 1.0 + tail_p * jnp.abs(act)
        r = pltpu.reciprocal(d, approx=True)
        r = r * (2.0 - d * r)
        q = tail_c[5] * r + tail_c[4]
        for k in (3, 2, 1, 0):
            q = q * r + tail_c[k]
        q = q * r * e
        phi = jnp.where(act > 0, 1.0 - q, q)
        hidden = act * phi
        d_act = d_hid * (phi + act * e * inverse_root_twopi)
        hh, hl = split(hidden)
        dh, dl = split(d_act)
        gb_scr[...] += lanes_sum(d_act)
        both = dot(w4_scr[...], dh, NN)
        d_lin = both[0:C] + both[C : 2 * C] + dot(w4_scr[0:C, :], dl, NN)
        gw1_scr[...] += dot(dh, jnp.concatenate([lh, ll], axis=0), NT)
        gw1_scr[:, 0:C] += dot(dl, lh, NT)
        gw2_scr[...] += dot(hh, jnp.concatenate([ch, cl], axis=1), NN)
        gw2_scr[:, 0:C] += dot(hl, ch, NN)
        gg_scr[...] += lanes_sum(d_lin * normed)
        gs_scr[...] += lanes_sum(d_lin)
        d_norm = d_lin * gain
        d_conv = inverse * (
            d_norm
            - jnp.mean(d_norm, axis=0, keepdims=True)
            - normed * jnp.mean(d_norm * normed, axis=0, keepdims=True)
        )
        gc_scr[...] += lanes_sum(d_conv)
        dconv_ref[b, pl.ds(p0, tile_rows)] = d_conv.T.reshape(tile_rows, cols, C)
        cot_sum[...] += jnp.sum(cot.reshape(tile // 8, 8, C), axis=0)
        return 0

    lax.fori_loop(0, batch * per_image, step, 0)

    edge_top[...] = dconv_ref[:, 0:m]
    edge_bottom[...] = dconv_ref[:, rows - m : rows]

    h = gw2_scr[:, 0:C] + gw2_scr[:, C : 2 * C]
    gw1 = (gw1_scr[:, 0:C] + gw1_scr[:, C : 2 * C]) * factor
    gw2 = h * (scale_row * factor)
    gb = (jnp.sum(gb_scr[...].T, axis=0, keepdims=True)) * factor
    for s in range(count):
        grads_ref[s, 0:hs, :] = gw1[s * hs : (s + 1) * hs, :]
        grads_ref[s, hs : 2 * hs, :] = gw2[s * hs : (s + 1) * hs, :]
    total = jnp.sum(cot_sum[...], axis=0, keepdims=True)
    outb = rows_form[taps + 3 : taps + 4, :]
    scale_grad = jnp.sum(h * wout_scr[...], axis=0, keepdims=True) + outb * total
    chan_ref[...] = jnp.zeros_like(chan_ref)
    chan_ref[0:1, 0:C] = jnp.sum(gc_scr[...].T, axis=0, keepdims=True) * factor
    chan_ref[1:2, 0:C] = jnp.sum(gg_scr[...].T, axis=0, keepdims=True) * factor
    chan_ref[2:3, 0:C] = jnp.sum(gs_scr[...].T, axis=0, keepdims=True) * factor
    chan_ref[3:4, 0:C] = total * scale_row * factor
    chan_ref[4:5, 0:C] = scale_grad * factor
    chan_ref[5:6, :] = gb


def kernel_grad_body(ms, order, factor, taps_i, taps_j, count, src_ref, dconv_ref, chan_ref, out_ref, acc_scr, rows_scr):
    batch, rows, cols, C = dconv_ref.shape
    m = taps_i // 2
    taps = taps_i * taps_j
    cs = C // count
    me = device_index(ms)
    acc_scr[...] = jnp.zeros_like(acc_scr)

    def step(b, _):
        for j in range(taps_j):
            acc = [acc_scr[i * taps_j + j] for i in range(taps_i)]
            for q in range(0, cols, 8):
                d = [dconv_ref[b, p, q : q + 8, :] for p in range(rows)]
                for r in range(rows + taps_i - 1):
                    s = src_ref[b, r, LEFT - m + q + j : LEFT - m + q + j + 8, :]
                    for i in range(taps_i):
                        p = r - i
                        if 0 <= p < rows:
                            acc[i] = acc[i] + d[p] * s
            for i in range(taps_i):
                acc_scr[i * taps_j + j] = acc[i]
        return 0

    lax.fori_loop(0, batch, step, 0)
    rows_scr[...] = jnp.zeros_like(rows_scr)
    for t in range(taps):
        rows_scr[t : t + 1, :] = jnp.sum(acc_scr[t], axis=0, keepdims=True) * factor
    rows_scr[taps : taps + 5, :] = chan_ref[0:5, 0:C]
    columns = exchange_order(rows_scr[...].T, cs, count, me)
    out_ref[...] = jnp.zeros_like(out_ref)
    hs = chan_ref.shape[1] // count
    for s in range(count):
        out_ref[s, 0:cs, :] = columns[order[s] * cs : (order[s] + 1) * cs, :]
        out_ref[s, cs : cs + 1, 0:hs] = chan_ref[5:6, s * hs : (s + 1) * hs]


def features_grad_body(taps_i, taps_j, inner, top, bottom, left, right, small_ref, cot_ref, out_ref, ext_scr, kb_scr):
    batch, rows, cols, C = inner.shape
    m = taps_i // 2
    taps = taps_i * taps_j
    fill(ext_scr, inner, top, bottom, left, right)
    for t in range(taps):
        kb_scr[t] = jnp.broadcast_to(small_ref[t : t + 1, :], (8, C))

    def step(b, _):
        for q in range(0, cols, 8):
            acc = depthwise_block(
                lambda r, j: ext_scr[b, r, LEFT - m + q + j : LEFT - m + q + j + 8, :],
                lambda i, j: kb_scr[taps - 1 - (i * taps_j + j)],
                rows, taps_i, taps_j, [cot_ref[b, p, q : q + 8, :] for p in range(rows)],
            )
            for p in range(rows):
                out_ref[b, p, q : q + 8, :] = acc[p]
        return 0

    lax.fori_loop(0, batch, step, 0)


def finish_body(taps_i, taps_j, cs, hs, *refs):
    parts, outs = refs[:-9], refs[-9:]
    total = parts[0][...]
    for part in parts[1:]:
        total = total + part[...]
    kernel_out, cb, ng, ns, win_out, ib, wout_out, ob, ls = outs
    taps = taps_i * taps_j
    win_out[...] = total[0:hs, :]
    wout_out[...] = total[hs : 2 * hs, :]
    small = total[2 * hs : 2 * hs + 8, :]
    for i in range(taps_i):
        kernel_out[i] = small[0:cs, i * taps_j : (i + 1) * taps_j]
    flipped = small.T
    for n, ref in enumerate((cb, ng, ns, ob, ls)):
        ref[...] = flipped[taps + n : taps + n + 1, 0:cs]
    ib[...] = small[cs : cs + 1, 0:hs]


def shifted(x, axis, step):
    count = lax.axis_size(axis)
    pairs = [(i, i + step) for i in range(count) if 0 <= i + step < count]
    return lax.ppermute(x, axis, pairs)


def flip(x, mask, count):
    return lax.ppermute(x, AXES, [(i, i ^ mask) for i in range(count)])


def groups_of(ms):
    bits_col = ms["col"].bit_length() - 1
    bits_row = ms["row"].bit_length() - 1
    col = [1 << k for k in range(bits_col)]
    row = [1 << (k + bits_col) for k in range(bits_row)]
    rest = col[1:]
    out = [rest[k : k + 2] for k in range(0, len(rest), 2)]
    out += [row[k : k + 2] for k in range(0, len(row), 2)]
    return out + [col[:1]]


def masks(group):
    out = [0]
    for bit in group:
        out += [bit ^ x for x in out]
    return out


def per_device(ms, features, cotangent, conv_kernel, conv_bias, norm_gain, norm_shift, w_in, in_bias, w_out, out_bias, layer_scale):
    batch, rows, cols, C = features.shape
    taps_i, taps_j, cs = conv_kernel.shape
    hs = w_out.shape[0]
    count = ms["row"] * ms["col"]
    hid = hs * count
    m = taps_i // 2
    taps = taps_i * taps_j
    cells = batch * rows * cols * count
    factor = 1.0 / math.sqrt(cells)
    slot = 2 * hs + 8
    wide = ceil8(LEFT + cols + m)

    block = call(functools.partial(pack_body, ms), shape(slot, LANES), size=100000)(
        conv_kernel.transpose(0, 2, 1),
        *(v.reshape(1, cs) for v in (conv_bias, norm_gain, norm_shift, out_bias, layer_scale)),
        w_in.T, in_bias.reshape(1, hs), w_out,
    )
    top = shifted(features[:, rows - m :], "row", 1)
    bottom = shifted(features[:, :m], "row", -1)
    slots = block[None]
    groups = groups_of(ms)
    order = [0]
    for group in groups:
        order = [mask ^ x for mask in masks(group) for x in order]
        slots = jnp.concatenate([slots] + [flip(slots, mask, count) for mask in masks(group)[1:]])

    def sides(top, inner, bottom):
        low = jnp.concatenate([x[:, :, cols - m :] for x in (top, inner, bottom)], axis=1)
        high = jnp.concatenate([x[:, :, :m] for x in (top, inner, bottom)], axis=1)
        return shifted(low, "col", 1), shifted(high, "col", -1)

    left, right = sides(top, features, bottom)
    tile = 4 * cols
    vm = pltpu.VMEM
    src, dconv, edge_top, edge_bottom, grads, chan, small = call(
        functools.partial(mix_body, ms, order, factor, taps_i, taps_j, tile),
        (
            shape(batch, rows + 2 * m, wide, C),
            shape(batch, rows, cols, C),
            shape(batch, m, cols, C),
            shape(batch, m, cols, C),
            shape(count, 2 * hs, C),
            shape(8, hid),
            shape(LANES, C),
        ),
        scratch=(
            vm((batch, rows, cols, C), f32),
            vm((C, LANES), f32),
            vm((taps, 8, C), f32),
            vm((hid, C), f32),
            vm((hid, C), f32),
            vm((hid, 3 * C), bf16),
            vm((hid, 3 * C), bf16),
            vm((2 * C, hid), bf16),
            vm((hid, LANES), f32),
            vm((hid, 2 * C), f32),
            vm((hid, 2 * C), f32),
            vm((hid, LANES), f32),
            vm((C, LANES), f32),
            vm((C, LANES), f32),
            vm((C, LANES), f32),
            vm((8, C), f32),
        ),
        flops=12 * 10**9,
        size=8 * 10**6,
    )(features, top, bottom, left, right, slots, cotangent)

    d_top = shifted(edge_bottom, "row", 1)
    d_bottom = shifted(edge_top, "row", -1)
    smalls = call(
        functools.partial(kernel_grad_body, ms, order, factor, taps_i, taps_j, count),
        shape(count, 8, LANES),
        scratch=(vm((taps, 8, C), f32), vm((LANES, C), f32)),
        flops=4 * 10**9,
        size=4 * 10**6,
    )(src, dconv, chan)

    d_left, d_right = sides(d_top, dconv, d_bottom)

    parts = [jnp.concatenate([grads, smalls], axis=1)]
    for group in groups[::-1]:
        whole = parts[0]
        for part in parts[1:]:
            whole = whole + part
        order = masks(group)
        step = whole.shape[0] // len(order)
        parts = [whole[:step]]
        parts += [flip(whole[k * step : (k + 1) * step], mask, count) for k, mask in enumerate(order) if k]

    features_grad = call(
        functools.partial(features_grad_body, taps_i, taps_j),
        shape(batch, rows, cols, C),
        scratch=(vm((batch, rows + 2 * m, wide, C), f32), vm((taps, 8, C), f32)),
        flops=4 * 10**9,
        size=4 * 10**6,
    )(dconv, d_top, d_bottom, d_left, d_right, small, cotangent)

    outs = call(
        functools.partial(finish_body, taps_i, taps_j, cs, hs),
        (
            shape(taps_i, cs, taps_j),
            *(shape(1, cs) for _ in range(3)),
            shape(hs, C),
            shape(1, hs),
            shape(hs, C),
            *(shape(1, cs) for _ in range(2)),
        ),
        size=100000,
    )(*(p.reshape(slot, LANES) for p in parts))
    kernel_grad, cb, ng, ns, win, ib, wout, ob, ls = outs
    return (
        features_grad,
        kernel_grad.transpose(0, 2, 1),
        cb.reshape(cs),
        ng.reshape(cs),
        ns.reshape(cs),
        win.T,
        ib.reshape(hs),
        wout,
        ob.reshape(cs),
        ls.reshape(cs),
    )


def solution(mesh):
    both = P(AXES)
    tiles = P(None, "row", "col", None)
    in_specs = (
        tiles, tiles, P(None, None, AXES), both, both, both, P(None, AXES), both, P(AXES, None), both, both,
    )
    out_specs = (
        tiles, P(None, None, AXES), both, both, both, P(None, AXES), both, P(AXES, None), both, both,
    )
    return jax.shard_map(
        functools.partial(per_device, dict(mesh.shape)),
        mesh=mesh, in_specs=in_specs, out_specs=out_specs, check_vma=False,
    )
```

```python
import functools
import math

import jax
import jax.numpy as jnp
from jax import lax
from jax.experimental import pallas as pl
from jax.experimental.pallas import tpu as pltpu
from jax.sharding import PartitionSpec as P

norm_eps = 1e-06
inverse_root_twopi = 0.3989422804014327
half_log2e = 0.7213475204444817
tail_p = 0.275
tail_c = (
    0.1178092510180382,
    0.04211149421929024,
    0.3339322641039753,
    -0.33099338058058636,
    0.45199870802757525,
    -0.11485833206946416,
)
AXES = ("row", "col")
LANES = 128
LEFT = 8
NN = (((1,), (0,)), ((), ()))
NT = (((1,), (1,)), ((), ()))
f32, bf16 = jnp.float32, jnp.bfloat16


def ceil8(n):
    return (n + 7) // 8 * 8


def call(body, outs, scratch=(), flops=0, size=0, limit=8, **more):
    return pl.pallas_call(
        body,
        out_shape=outs,
        scratch_shapes=list(scratch),
        compiler_params=pltpu.CompilerParams(vmem_limit_bytes=limit * 1024 * 1024),
        **more,
        cost_estimate=pl.CostEstimate(flops=flops, bytes_accessed=size, transcendentals=0),
    )


def shape(*dims):
    return jax.ShapeDtypeStruct(dims, f32)


def device_index(mesh_shape):
    return lax.axis_index("row") * mesh_shape["col"] + lax.axis_index("col")


def split(x):
    high = x.astype(bf16)
    return high, (x - high.astype(f32)).astype(bf16)


def dot(a, b, dims):
    return lax.dot_general(a, b, dims, preferred_element_type=f32)


def exchange_order(x, unit, count, me):
    rows = x.shape[0]
    index = lax.broadcasted_iota(jnp.int32, x.shape, 0)
    step = unit
    bit = 1
    while bit < count:
        up = pltpu.roll(x, step, 0)
        down = pltpu.roll(x, rows - step, 0)
        swapped = jnp.where((index & step) != 0, up, down)
        x = jnp.where((me & bit) != 0, swapped, x)
        step *= 2
        bit *= 2
    return x


def pairs(count, second):
    if not second:
        return [(i, i ^ 1) for i in range(count)]
    return [(i, (i + 1 if i % 2 else i - 1) % count) for i in range(count)]


def both_pairs(a, b, axis):
    count = lax.axis_size(axis)
    return lax.ppermute(a, axis, pairs(count, False)), lax.ppermute(b, axis, pairs(count, True))


def side(ms, axis):
    i = lax.axis_index(axis)
    even = i % 2 == 0
    return even, jnp.where(even, i > 0, i < ms[axis] - 1)


def start_body(ms, feat, kernel_hbm, cb, ng, ns, ob, ls, win_hbm, ib, wout_hbm, out_ref, row_a, row_b, col_a, col_b,
               kernel_scr, v0, v1, v2, v3, v4, ib_scr, win_scr, wout_scr, low, high, sems):
    batch, rows, cols, C = feat.shape
    taps_i, cs, taps_j = kernel_hbm.shape
    hs = win_hbm.shape[0]
    taps = taps_i * taps_j
    m = taps_i // 2
    even_r, _ = side(ms, "row")
    even_c, _ = side(ms, "col")
    far = jnp.where(even_r, rows - m, 0)
    near = jnp.where(even_r, 0, rows - m)
    vectors = (v0, v1, v2, v3, v4)
    moves = [(kernel_hbm, kernel_scr), (win_hbm, win_scr), (wout_hbm, wout_scr), (ib, ib_scr)]
    moves += list(zip((cb, ng, ns, ob, ls), vectors))
    moves += [(feat.at[:, pl.ds(far, m)], row_a), (feat.at[:, pl.ds(near, m)], row_b)]
    moves += [(feat.at[:, :, 0:8], low), (feat.at[:, :, cols - 8 : cols], high)]
    copies = [pltpu.make_async_copy(src, dst, sems.at[n]) for n, (src, dst) in enumerate(moves)]
    for copy in copies:
        copy.start()
    out_ref[...] = jnp.zeros_like(out_ref)
    for copy in copies:
        copy.wait()
    out_ref[0:hs, :] = win_scr[...]
    out_ref[hs : 2 * hs, :] = wout_scr[...]
    base = 2 * hs
    for i in range(taps_i):
        out_ref[base : base + cs, i * taps_j : (i + 1) * taps_j] = kernel_scr[i]
    for n, ref in enumerate(vectors):
        column = jnp.broadcast_to(ref[...], (8, cs)).T
        out_ref[base : base + cs, taps + n : taps + n + 1] = column[:, 0:1]
    out_ref[base + cs : base + cs + 1, 0:hs] = ib_scr[...]
    first, last = low[:, :, 0:m], high[:, :, 8 - m : 8]
    col_a[...] = jnp.where(even_c, last, first)
    col_b[...] = jnp.where(even_c, first, last)


def sides_body(ms, edge_a, edge_b, got_a, got_b, out_a, out_b):
    batch, rows, m, C = edge_a.shape
    cols = got_a.shape[2]
    even_r, true_r = side(ms, "row")
    even_c, _ = side(ms, "col")
    out_a[:, m : m + rows] = edge_a[...]
    out_b[:, m : m + rows] = edge_b[...]
    for got, end, keep in ((got_a, even_r, None), (got_b, jnp.logical_not(even_r), true_r)):
        at = jnp.where(end, rows + m, 0)
        x = got[...]
        if keep is not None:
            x = jnp.where(keep, x, 0.0)
        last, first = x[:, :, cols - m :], x[:, :, 0:m]
        out_a[:, pl.ds(at, m)] = jnp.where(even_c, last, first)
        out_b[:, pl.ds(at, m)] = jnp.where(even_c, first, last)


def depthwise_block(read, weight, rows, taps_i, taps_j, start):
    acc = start
    for j in range(taps_j):
        w = [weight(i, j) for i in range(taps_i)]
        for r in range(rows + taps_i - 1):
            s = read(r, j)
            for i in range(taps_i):
                p = r - i
                if 0 <= p < rows:
                    term = w[i] * s
                    acc[p] = term if acc[p] is None else acc[p] + term
    return acc


def fill(ms, dst, inner, row_a, row_b, col_a, col_b):
    batch, rows, cols, _ = inner.shape
    m = row_a.shape[1]
    even_r, true_r = side(ms, "row")
    even_c, true_c = side(ms, "col")
    at_a = jnp.where(even_r, rows + m, 0)
    at_b = jnp.where(even_r, 0, rows + m)
    for b in range(batch):
        dst[b, m : m + rows, LEFT : LEFT + cols, :] = inner[b]
        dst[b, pl.ds(at_a, m), LEFT : LEFT + cols, :] = row_a[b]
        dst[b, pl.ds(at_b, m), LEFT : LEFT + cols, :] = jnp.where(true_r, row_b[b], 0.0)
        x, y = col_a[b], jnp.where(true_c, col_b[b], 0.0)
        dst[b, :, LEFT - m : LEFT, :] = jnp.where(even_c, y, x)
        dst[b, :, LEFT + cols : LEFT + cols + m, :] = jnp.where(even_c, x, y)


def small_columns(slots_ref, hs, cs, count, me, order, scratch):
    base = 2 * hs
    for s in range(count):
        scratch[order[s] * cs : (order[s] + 1) * cs, :] = slots_ref[s, base : base + cs, :]
    return exchange_order(scratch[...], cs, count, me)


def mix_body(
    ms, order, factor, taps_i, taps_j, tile,
    feat, got_ra, got_rb, got_ca, got_cb, slots_ref, cot_ref,
    src_ref, dconv_ref, row_a, row_b, col_a, col_b, grads_ref, chan_ref, small_ref,
    conv_scr, cols_scr, kb_scr, win_scr, wout_scr, w1_scr, w2_scr, w4_scr, bias_scr,
    gw1_scr, gw2_scr, gb_scr, gg_scr, gs_scr, gc_scr, cot_sum,
):
    batch, rows, cols, C = feat.shape
    count = slots_ref.shape[0]
    cs = C // count
    taps = taps_i * taps_j
    m = taps_i // 2
    hid = win_scr.shape[0]
    hs = hid // count
    me = device_index(ms)

    fill(ms, src_ref, feat, got_ra, got_rb, got_ca, got_cb)
    columns = small_columns(slots_ref, hs, cs, count, me, order, cols_scr)
    cols_scr[...] = columns
    rows_form = columns.T
    small_ref[...] = rows_form
    for t in range(taps):
        kb_scr[t] = jnp.broadcast_to(rows_form[t : t + 1, :], (8, C))
    conv_bias = jnp.broadcast_to(rows_form[taps : taps + 1, :], (8, C))

    for s in range(count):
        win_scr[s * hs : (s + 1) * hs, :] = slots_ref[s, 0:hs, :]
        wout_scr[s * hs : (s + 1) * hs, :] = slots_ref[s, hs : 2 * hs, :]
    for s in range(count):
        cols_bias = jnp.broadcast_to(slots_ref[s, 2 * hs + cs : 2 * hs + cs + 1, :], (LANES, LANES)).T
        bias_scr[s * hs : (s + 1) * hs, :] = cols_bias[0:hs, :]

    scale_row = rows_form[taps + 4 : taps + 5, :]
    wh, wl = split(win_scr[...])
    w1_scr[:, 0:C] = wh
    w1_scr[:, C : 2 * C] = wl
    w1_scr[:, 2 * C : 3 * C] = wh
    oh, ol = split(wout_scr[...] * scale_row)
    w2_scr[:, 0:C] = oh
    w2_scr[:, C : 2 * C] = ol
    w2_scr[:, 2 * C : 3 * C] = oh
    th, tl = split(win_scr[...].T)
    w4_scr[0:C, :] = th
    w4_scr[C : 2 * C, :] = tl

    def conv_step(b, _):
        for q in range(0, cols, 8):
            acc = depthwise_block(
                lambda r, j: src_ref[b, r, LEFT - m + q + j : LEFT - m + q + j + 8, :],
                lambda i, j: kb_scr[i * taps_j + j],
                rows, taps_i, taps_j, [conv_bias] * rows,
            )
            for p in range(rows):
                conv_scr[b, p, q : q + 8, :] = acc[p]
        return 0

    lax.fori_loop(0, batch, conv_step, 0)

    for ref in (gw1_scr, gw2_scr, gb_scr, gg_scr, gs_scr, gc_scr, cot_sum):
        ref[...] = jnp.zeros_like(ref)
    tile_rows = tile // cols
    per_image = rows // tile_rows
    gain = cols_scr[:, taps + 1 : taps + 2]
    shift = cols_scr[:, taps + 2 : taps + 3]

    def lanes_sum(x):
        total = x[:, 0:LANES]
        for k in range(LANES, x.shape[1], LANES):
            total = total + x[:, k : k + LANES]
        return total

    def step(t, _):
        b = t // per_image
        p0 = (t % per_image) * tile_rows
        x = conv_scr[b, pl.ds(p0, tile_rows)].reshape(tile, C).T
        mean = jnp.mean(x, axis=0, keepdims=True)
        centred = x - mean
        variance = jnp.mean(centred * centred, axis=0, keepdims=True)
        inverse = lax.rsqrt(variance + norm_eps)
        normed = centred * inverse
        lin = normed * gain + shift
        lh, ll = split(lin)
        cot = cot_ref[b, pl.ds(p0, tile_rows)].reshape(tile, C)
        ch, cl = split(cot)
        act = dot(w1_scr[...], jnp.concatenate([lh, lh, ll], axis=0), NN)
        d_hid = dot(w2_scr[...], jnp.concatenate([ch, ch, cl], axis=1), NT)
        bias = bias_scr[...]
        act = act + jnp.concatenate([bias] * (tile // LANES), axis=1)
        e = jnp.exp2((act * act) * (-half_log2e))
        d = 1.0 + tail_p * jnp.abs(act)
        r = pltpu.reciprocal(d, approx=True)
        r = r * (2.0 - d * r)
        q = tail_c[5] * r + tail_c[4]
        for k in (3, 2, 1, 0):
            q = q * r + tail_c[k]
        q = q * r * e
        phi = jnp.where(act > 0, 1.0 - q, q)
        hidden = act * phi
        d_act = d_hid * (phi + act * e * inverse_root_twopi)
        hh, hl = split(hidden)
        dh, dl = split(d_act)
        gb_scr[...] += lanes_sum(d_act)
        both = dot(w4_scr[...], dh, NN)
        d_lin = both[0:C] + both[C : 2 * C] + dot(w4_scr[0:C, :], dl, NN)
        gw1_scr[...] += dot(dh, jnp.concatenate([lh, ll], axis=0), NT)
        gw1_scr[:, 0:C] += dot(dl, lh, NT)
        gw2_scr[...] += dot(hh, jnp.concatenate([ch, cl], axis=1), NN)
        gw2_scr[:, 0:C] += dot(hl, ch, NN)
        gg_scr[...] += lanes_sum(d_lin * normed)
        gs_scr[...] += lanes_sum(d_lin)
        d_norm = d_lin * gain
        d_conv = inverse * (
            d_norm
            - jnp.mean(d_norm, axis=0, keepdims=True)
            - normed * jnp.mean(d_norm * normed, axis=0, keepdims=True)
        )
        gc_scr[...] += lanes_sum(d_conv)
        dconv_ref[b, pl.ds(p0, tile_rows)] = d_conv.T.reshape(tile_rows, cols, C)
        cot_sum[...] += jnp.sum(cot.reshape(tile // 8, 8, C), axis=0)
        return 0

    lax.fori_loop(0, batch * per_image, step, 0)

    even_r, _ = side(ms, "row")
    even_c, _ = side(ms, "col")
    row_a[...] = dconv_ref[:, pl.ds(jnp.where(even_r, rows - m, 0), m)]
    row_b[...] = dconv_ref[:, pl.ds(jnp.where(even_r, 0, rows - m), m)]
    first, last = dconv_ref[:, :, 0:m], dconv_ref[:, :, cols - m : cols]
    col_a[...] = jnp.where(even_c, last, first)
    col_b[...] = jnp.where(even_c, first, last)

    h = gw2_scr[:, 0:C] + gw2_scr[:, C : 2 * C]
    gw1 = (gw1_scr[:, 0:C] + gw1_scr[:, C : 2 * C]) * factor
    gw2 = h * (scale_row * factor)
    gb = (jnp.sum(gb_scr[...].T, axis=0, keepdims=True)) * factor
    for s in range(count):
        grads_ref[s, 0:hs, :] = gw1[s * hs : (s + 1) * hs, :]
        grads_ref[s, hs : 2 * hs, :] = gw2[s * hs : (s + 1) * hs, :]
    total = jnp.sum(cot_sum[...], axis=0, keepdims=True)
    outb = rows_form[taps + 3 : taps + 4, :]
    scale_grad = jnp.sum(h * wout_scr[...], axis=0, keepdims=True) + outb * total
    chan_ref[...] = jnp.zeros_like(chan_ref)
    chan_ref[0:1, 0:C] = jnp.sum(gc_scr[...].T, axis=0, keepdims=True) * factor
    chan_ref[1:2, 0:C] = jnp.sum(gg_scr[...].T, axis=0, keepdims=True) * factor
    chan_ref[2:3, 0:C] = jnp.sum(gs_scr[...].T, axis=0, keepdims=True) * factor
    chan_ref[3:4, 0:C] = total * scale_row * factor
    chan_ref[4:5, 0:C] = scale_grad * factor
    chan_ref[5:6, :] = gb


def kernel_grad_body(ms, order, factor, taps_i, taps_j, count, src_ref, dconv_ref, chan_ref, out_ref, acc_scr, rows_scr):
    batch, rows, cols, C = dconv_ref.shape
    m = taps_i // 2
    taps = taps_i * taps_j
    cs = C // count
    me = device_index(ms)
    acc_scr[...] = jnp.zeros_like(acc_scr)

    def step(b, _):
        for j in range(taps_j):
            acc = [acc_scr[i * taps_j + j] for i in range(taps_i)]
            for q in range(0, cols, 8):
                d = [dconv_ref[b, p, q : q + 8, :] for p in range(rows)]
                for r in range(rows + taps_i - 1):
                    s = src_ref[b, r, LEFT - m + q + j : LEFT - m + q + j + 8, :]
                    for i in range(taps_i):
                        p = r - i
                        if 0 <= p < rows:
                            acc[i] = acc[i] + d[p] * s
            for i in range(taps_i):
                acc_scr[i * taps_j + j] = acc[i]
        return 0

    lax.fori_loop(0, batch, step, 0)
    rows_scr[...] = jnp.zeros_like(rows_scr)
    for t in range(taps):
        rows_scr[t : t + 1, :] = jnp.sum(acc_scr[t], axis=0, keepdims=True) * factor
    rows_scr[taps : taps + 5, :] = chan_ref[0:5, 0:C]
    columns = exchange_order(rows_scr[...].T, cs, count, me)
    out_ref[...] = jnp.zeros_like(out_ref)
    hs = chan_ref.shape[1] // count
    for s in range(count):
        out_ref[s, 0:cs, :] = columns[order[s] * cs : (order[s] + 1) * cs, :]
        out_ref[s, cs : cs + 1, 0:hs] = chan_ref[5:6, s * hs : (s + 1) * hs]


def features_grad_body(ms, taps_i, taps_j, inner, got_ra, got_rb, got_ca, got_cb, small_ref, cot_ref, out_ref, ext_scr, kb_scr):
    batch, rows, cols, C = inner.shape
    m = taps_i // 2
    taps = taps_i * taps_j
    fill(ms, ext_scr, inner, got_ra, got_rb, got_ca, got_cb)
    for t in range(taps):
        kb_scr[t] = jnp.broadcast_to(small_ref[t : t + 1, :], (8, C))

    def step(b, _):
        for q in range(0, cols, 8):
            acc = depthwise_block(
                lambda r, j: ext_scr[b, r, LEFT - m + q + j : LEFT - m + q + j + 8, :],
                lambda i, j: kb_scr[taps - 1 - (i * taps_j + j)],
                rows, taps_i, taps_j, [cot_ref[b, p, q : q + 8, :] for p in range(rows)],
            )
            for p in range(rows):
                out_ref[b, p, q : q + 8, :] = acc[p]
        return 0

    lax.fori_loop(0, batch, step, 0)


def finish_body(taps_i, taps_j, cs, hs, *refs):
    parts, outs = refs[:-9], refs[-9:]
    total = parts[0][...]
    for part in parts[1:]:
        total = total + part[...]
    kernel_out, cb, ng, ns, win_out, ib, wout_out, ob, ls = outs
    taps = taps_i * taps_j
    win_out[...] = total[0:hs, :]
    wout_out[...] = total[hs : 2 * hs, :]
    small = total[2 * hs : 2 * hs + 8, :]
    for i in range(taps_i):
        kernel_out[i] = small[0:cs, i * taps_j : (i + 1) * taps_j]
    flipped = small.T
    for n, ref in enumerate((cb, ng, ns, ob, ls)):
        ref[...] = flipped[taps + n : taps + n + 1, 0:cs]
    ib[...] = small[cs : cs + 1, 0:hs]


def flip(x, mask, count):
    return lax.ppermute(x, AXES, [(i, i ^ mask) for i in range(count)])


def groups_of(ms):
    bits_col = ms["col"].bit_length() - 1
    bits_row = ms["row"].bit_length() - 1
    col = [1 << k for k in range(bits_col)]
    row = [1 << (k + bits_col) for k in range(bits_row)]
    rest = col[1:]
    out = [rest[k : k + 2] for k in range(0, len(rest), 2)]
    out += [row[k : k + 2] for k in range(0, len(row), 2)]
    return out + [col[:1]]


def masks(group):
    out = [0]
    for bit in group:
        out += [bit ^ x for x in out]
    return out


def per_device(ms, features, cotangent, conv_kernel, conv_bias, norm_gain, norm_shift, w_in, in_bias, w_out, out_bias, layer_scale):
    batch, rows, cols, C = features.shape
    taps_i, taps_j, cs = conv_kernel.shape
    hs = w_out.shape[0]
    count = ms["row"] * ms["col"]
    hid = hs * count
    m = taps_i // 2
    taps = taps_i * taps_j
    cells = batch * rows * cols * count
    factor = 1.0 / math.sqrt(cells)
    slot = 2 * hs + 8
    wide = ceil8(LEFT + cols + m)

    vm = pltpu.VMEM
    vectors = [v.reshape(1, cs) for v in (conv_bias, norm_gain, norm_shift, out_bias, layer_scale)]
    block, row_a, row_b, col_a, col_b = call(
        functools.partial(start_body, ms),
        (
            shape(slot, LANES),
            *(shape(batch, m, cols, C) for _ in range(2)),
            *(shape(batch, rows, m, C) for _ in range(2)),
        ),
        scratch=(
            vm((taps_i, cs, taps_j), f32),
            *(vm((1, cs), f32) for _ in range(5)),
            vm((1, hs), f32),
            vm((hs, C), f32),
            vm((hs, C), f32),
            vm((batch, rows, 8, C), f32),
            vm((batch, rows, 8, C), f32),
            pltpu.SemaphoreType.DMA((13,)),
        ),
        size=10**6,
        in_specs=[pl.BlockSpec(memory_space=pltpu.HBM)] * 10,
    )(features, conv_kernel.transpose(0, 2, 1), *vectors, w_in.T, in_bias.reshape(1, hs), w_out)

    def sides(edge_a, edge_b, got_a, got_b):
        out = call(
            functools.partial(sides_body, ms),
            tuple(shape(batch, rows + 2 * m, m, C) for _ in range(2)),
            size=10**6,
        )(edge_a, edge_b, got_a, got_b)
        return both_pairs(*out, "col")

    got_ra, got_rb = both_pairs(row_a, row_b, "row")
    slots = block[None]
    groups = groups_of(ms)
    order = [0]
    for group in groups:
        order = [mask ^ x for mask in masks(group) for x in order]
        slots = jnp.concatenate([slots] + [flip(slots, mask, count) for mask in masks(group)[1:]])

    got_ca, got_cb = sides(col_a, col_b, got_ra, got_rb)
    tile = 4 * cols
    src, dconv, d_row_a, d_row_b, d_col_a, d_col_b, grads, chan, small = call(
        functools.partial(mix_body, ms, order, factor, taps_i, taps_j, tile),
        (
            shape(batch, rows + 2 * m, wide, C),
            shape(batch, rows, cols, C),
            *(shape(batch, m, cols, C) for _ in range(2)),
            *(shape(batch, rows, m, C) for _ in range(2)),
            shape(count, 2 * hs, C),
            shape(8, hid),
            shape(LANES, C),
        ),
        scratch=(
            vm((batch, rows, cols, C), f32),
            vm((C, LANES), f32),
            vm((taps, 8, C), f32),
            vm((hid, C), f32),
            vm((hid, C), f32),
            vm((hid, 3 * C), bf16),
            vm((hid, 3 * C), bf16),
            vm((2 * C, hid), bf16),
            vm((hid, LANES), f32),
            vm((hid, 2 * C), f32),
            vm((hid, 2 * C), f32),
            vm((hid, LANES), f32),
            vm((C, LANES), f32),
            vm((C, LANES), f32),
            vm((C, LANES), f32),
            vm((8, C), f32),
        ),
        flops=12 * 10**9,
        size=8 * 10**6,
        limit=24,
    )(features, got_ra, got_rb, got_ca, got_cb, slots, cotangent)

    d_got_ra, d_got_rb = both_pairs(d_row_a, d_row_b, "row")
    smalls = call(
        functools.partial(kernel_grad_body, ms, order, factor, taps_i, taps_j, count),
        shape(count, 8, LANES),
        scratch=(vm((taps, 8, C), f32), vm((LANES, C), f32)),
        flops=4 * 10**9,
        size=4 * 10**6,
    )(src, dconv, chan)

    d_got_ca, d_got_cb = sides(d_col_a, d_col_b, d_got_ra, d_got_rb)

    parts = [jnp.concatenate([grads, smalls], axis=1)]
    for group in groups[::-1]:
        whole = parts[0]
        for part in parts[1:]:
            whole = whole + part
        order = masks(group)
        step = whole.shape[0] // len(order)
        parts = [whole[:step]]
        parts += [flip(whole[k * step : (k + 1) * step], mask, count) for k, mask in enumerate(order) if k]

    features_grad = call(
        functools.partial(features_grad_body, ms, taps_i, taps_j),
        shape(batch, rows, cols, C),
        scratch=(vm((batch, rows + 2 * m, wide, C), f32), vm((taps, 8, C), f32)),
        flops=4 * 10**9,
        size=4 * 10**6,
    )(dconv, d_got_ra, d_got_rb, d_got_ca, d_got_cb, small, cotangent)

    outs = call(
        functools.partial(finish_body, taps_i, taps_j, cs, hs),
        (
            shape(taps_i, cs, taps_j),
            *(shape(1, cs) for _ in range(3)),
            shape(hs, C),
            shape(1, hs),
            shape(hs, C),
            *(shape(1, cs) for _ in range(2)),
        ),
        size=100000,
    )(*(p.reshape(slot, LANES) for p in parts))
    kernel_grad, cb, ng, ns, win, ib, wout, ob, ls = outs
    return (
        features_grad,
        kernel_grad.transpose(0, 2, 1),
        cb.reshape(cs),
        ng.reshape(cs),
        ns.reshape(cs),
        win.T,
        ib.reshape(hs),
        wout,
        ob.reshape(cs),
        ls.reshape(cs),
    )


def solution(mesh):
    both = P(AXES)
    tiles = P(None, "row", "col", None)
    in_specs = (
        tiles, tiles, P(None, None, AXES), both, both, both, P(None, AXES), both, P(AXES, None), both, both,
    )
    out_specs = (
        tiles, P(None, None, AXES), both, both, both, P(None, AXES), both, P(AXES, None), both, both,
    )
    return jax.shard_map(
        functools.partial(per_device, dict(mesh.shape)),
        mesh=mesh, in_specs=in_specs, out_specs=out_specs, check_vma=False,
    )
```

```python
import functools
import math

import jax
import jax.numpy as jnp
from jax import lax
from jax.experimental import pallas as pl
from jax.experimental.pallas import tpu as pltpu
from jax.sharding import PartitionSpec as P

norm_eps = 1e-06
inverse_root_twopi = 0.3989422804014327
half_log2e = 0.7213475204444817
tail_p = 0.275
tail_c = (
    0.1178092510180382,
    0.04211149421929024,
    0.3339322641039753,
    -0.33099338058058636,
    0.45199870802757525,
    -0.11485833206946416,
)
AXES = ("row", "col")
LANES = 128
LEFT = 8
NN = (((1,), (0,)), ((), ()))
NT = (((1,), (1,)), ((), ()))
f32, bf16 = jnp.float32, jnp.bfloat16


def ceil8(n):
    return (n + 7) // 8 * 8


def call(body, outs, scratch=(), flops=0, size=0, limit=8, **more):
    return pl.pallas_call(
        body,
        out_shape=outs,
        scratch_shapes=list(scratch),
        compiler_params=pltpu.CompilerParams(vmem_limit_bytes=limit and limit * 1024 * 1024),
        **more,
        cost_estimate=pl.CostEstimate(flops=flops, bytes_accessed=size, transcendentals=0),
    )


def shape(*dims):
    return jax.ShapeDtypeStruct(dims, f32)


def device_index(mesh_shape):
    return lax.axis_index("row") * mesh_shape["col"] + lax.axis_index("col")


def split(x):
    high = x.astype(bf16)
    return high, (x - high.astype(f32)).astype(bf16)


def dot(a, b, dims):
    return lax.dot_general(a, b, dims, preferred_element_type=f32)


def exchange_order(x, unit, count, me):
    rows = x.shape[0]
    index = lax.broadcasted_iota(jnp.int32, x.shape, 0)
    step = unit
    bit = 1
    while bit < count:
        up = pltpu.roll(x, step, 0)
        down = pltpu.roll(x, rows - step, 0)
        swapped = jnp.where((index & step) != 0, up, down)
        x = jnp.where((me & bit) != 0, swapped, x)
        step *= 2
        bit *= 2
    return x


def pairs(count, second):
    if not second:
        return [(i, i ^ 1) for i in range(count)]
    return [(i, (i + 1 if i % 2 else i - 1) % count) for i in range(count)]


def both_pairs(a, b, axis):
    count = lax.axis_size(axis)
    return lax.ppermute(a, axis, pairs(count, False)), lax.ppermute(b, axis, pairs(count, True))


def side(ms, axis):
    i = lax.axis_index(axis)
    even = i % 2 == 0
    return even, jnp.where(even, i > 0, i < ms[axis] - 1)


def start_body(ms, feat, kernel_hbm, cb, ng, ns, ob, ls, win_hbm, ib, wout_hbm, out_ref, row_a, row_b, col_a, col_b,
               kernel_scr, v0, v1, v2, v3, v4, ib_scr, win_scr, wout_scr, low, high, sems):
    batch, rows, cols, C = feat.shape
    taps_i, cs, taps_j = kernel_hbm.shape
    hs = win_hbm.shape[0]
    taps = taps_i * taps_j
    m = taps_i // 2
    even_r, _ = side(ms, "row")
    even_c, _ = side(ms, "col")
    far = jnp.where(even_r, rows - m, 0)
    near = jnp.where(even_r, 0, rows - m)
    vectors = (v0, v1, v2, v3, v4)
    moves = [(kernel_hbm, kernel_scr), (win_hbm, win_scr), (wout_hbm, wout_scr), (ib, ib_scr)]
    moves += list(zip((cb, ng, ns, ob, ls), vectors))
    moves += [(feat.at[:, pl.ds(far, m)], row_a), (feat.at[:, pl.ds(near, m)], row_b)]
    moves += [(feat.at[:, :, 0:8], low), (feat.at[:, :, cols - 8 : cols], high)]
    copies = [pltpu.make_async_copy(src, dst, sems.at[n]) for n, (src, dst) in enumerate(moves)]
    for copy in copies:
        copy.start()
    out_ref[...] = jnp.zeros_like(out_ref)
    for copy in copies:
        copy.wait()
    out_ref[0:hs, :] = win_scr[...]
    out_ref[hs : 2 * hs, :] = wout_scr[...]
    base = 2 * hs
    for i in range(taps_i):
        out_ref[base : base + cs, i * taps_j : (i + 1) * taps_j] = kernel_scr[i]
    for n, ref in enumerate(vectors):
        column = jnp.broadcast_to(ref[...], (8, cs)).T
        out_ref[base : base + cs, taps + n : taps + n + 1] = column[:, 0:1]
    out_ref[base + cs : base + cs + 1, 0:hs] = ib_scr[...]
    first, last = low[:, :, 0:m], high[:, :, 8 - m : 8]
    col_a[...] = jnp.where(even_c, last, first)
    col_b[...] = jnp.where(even_c, first, last)


def with_corners(ms, edge_a, edge_b, got_a, got_b, out_a, out_b):
    batch, rows, m, C = edge_a.shape
    cols = got_a.shape[2]
    even_r, true_r = side(ms, "row")
    even_c, _ = side(ms, "col")
    out_a[:, m : m + rows] = edge_a[...]
    out_b[:, m : m + rows] = edge_b[...]
    for got, end, keep in ((got_a, even_r, None), (got_b, jnp.logical_not(even_r), true_r)):
        at = jnp.where(end, rows + m, 0)
        x = got[...]
        if keep is not None:
            x = jnp.where(keep, x, 0.0)
        last, first = x[:, :, cols - m :], x[:, :, 0:m]
        out_a[:, pl.ds(at, m)] = jnp.where(even_c, last, first)
        out_b[:, pl.ds(at, m)] = jnp.where(even_c, first, last)


def lay_out(parts, out):
    n = 0
    for part in parts:
        out[n : n + part.shape[0]] = part[...]
        n += part.shape[0]


def first_join_body(ms, edge_a, edge_b, got_a, got_b, *refs):
    parts, (slots, out_a, out_b) = refs[:-3], refs[-3:]
    lay_out(parts, slots)
    with_corners(ms, edge_a, edge_b, got_a, got_b, out_a, out_b)


def join_body(waits, *refs):
    lay_out(refs[waits:-1], refs[-1])


def back_join_body(ms, edge_a, edge_b, got_a, got_b, large, large_got, small, small_got, *refs):
    out_a, out_b = refs[-2:]
    rows = large.shape[1]
    n = 0
    for out in refs[:-2]:
        count = out.shape[0]
        out[:, 0:rows] = large[n : n + count] + large_got[n : n + count]
        out[:, rows:] = small[n : n + count] + small_got[n : n + count]
        n += count
    with_corners(ms, edge_a, edge_b, got_a, got_b, out_a, out_b)


def depthwise_block(read, weight, rows, taps_i, taps_j, start):
    acc = start
    for j in range(taps_j):
        w = [weight(i, j) for i in range(taps_i)]
        for r in range(rows + taps_i - 1):
            s = read(r, j)
            for i in range(taps_i):
                p = r - i
                if 0 <= p < rows:
                    term = w[i] * s
                    acc[p] = term if acc[p] is None else acc[p] + term
    return acc


def fill(ms, dst, inner, row_a, row_b, col_a, col_b):
    batch, rows, cols, _ = inner.shape
    m = row_a.shape[1]
    even_r, true_r = side(ms, "row")
    even_c, true_c = side(ms, "col")
    at_a = jnp.where(even_r, rows + m, 0)
    at_b = jnp.where(even_r, 0, rows + m)
    for b in range(batch):
        dst[b, m : m + rows, LEFT : LEFT + cols, :] = inner[b]
        dst[b, pl.ds(at_a, m), LEFT : LEFT + cols, :] = row_a[b]
        dst[b, pl.ds(at_b, m), LEFT : LEFT + cols, :] = jnp.where(true_r, row_b[b], 0.0)
        x, y = col_a[b], jnp.where(true_c, col_b[b], 0.0)
        dst[b, :, LEFT - m : LEFT, :] = jnp.where(even_c, y, x)
        dst[b, :, LEFT + cols : LEFT + cols + m, :] = jnp.where(even_c, x, y)


def small_columns(slots_ref, hs, cs, count, me, order, scratch):
    base = 2 * hs
    for s in range(count):
        scratch[order[s] * cs : (order[s] + 1) * cs, :] = slots_ref[s, base : base + cs, :]
    return exchange_order(scratch[...], cs, count, me)


def mix_body(
    ms, order, factor, taps_i, taps_j, tile,
    feat, got_ra, got_rb, got_ca, got_cb, slots_ref, cot_ref,
    src_ref, dconv_ref, row_a, row_b, col_a, col_b, grads_ref, chan_ref, small_ref,
    conv_scr, cols_scr, kb_scr, win_scr, wout_scr, w1_scr, w2_scr, w4_scr, bias_scr,
    gw1_scr, gw2_scr, gb_scr, gg_scr, gs_scr, gc_scr, cot_sum,
):
    batch, rows, cols, C = feat.shape
    count = slots_ref.shape[0]
    cs = C // count
    taps = taps_i * taps_j
    m = taps_i // 2
    hid = win_scr.shape[0]
    hs = hid // count
    me = device_index(ms)

    fill(ms, src_ref, feat, got_ra, got_rb, got_ca, got_cb)
    columns = small_columns(slots_ref, hs, cs, count, me, order, cols_scr)
    cols_scr[...] = columns
    rows_form = columns.T
    small_ref[...] = rows_form
    for t in range(taps):
        kb_scr[t] = jnp.broadcast_to(rows_form[t : t + 1, :], (8, C))
    conv_bias = jnp.broadcast_to(rows_form[taps : taps + 1, :], (8, C))

    for s in range(count):
        win_scr[s * hs : (s + 1) * hs, :] = slots_ref[s, 0:hs, :]
        wout_scr[s * hs : (s + 1) * hs, :] = slots_ref[s, hs : 2 * hs, :]
    for s in range(count):
        cols_bias = jnp.broadcast_to(slots_ref[s, 2 * hs + cs : 2 * hs + cs + 1, :], (LANES, LANES)).T
        bias_scr[s * hs : (s + 1) * hs, :] = cols_bias[0:hs, :]

    scale_row = rows_form[taps + 4 : taps + 5, :]
    wh, wl = split(win_scr[...])
    w1_scr[:, 0:C] = wh
    w1_scr[:, C : 2 * C] = wl
    w1_scr[:, 2 * C : 3 * C] = wh
    oh, ol = split(wout_scr[...] * scale_row)
    w2_scr[:, 0:C] = oh
    w2_scr[:, C : 2 * C] = ol
    w2_scr[:, 2 * C : 3 * C] = oh
    th, tl = split(win_scr[...].T)
    w4_scr[0:C, :] = th
    w4_scr[C : 2 * C, :] = tl

    def conv_step(b, _):
        for q in range(0, cols, 8):
            acc = depthwise_block(
                lambda r, j: src_ref[b, r, LEFT - m + q + j : LEFT - m + q + j + 8, :],
                lambda i, j: kb_scr[i * taps_j + j],
                rows, taps_i, taps_j, [conv_bias] * rows,
            )
            for p in range(rows):
                conv_scr[b, p, q : q + 8, :] = acc[p]
        return 0

    lax.fori_loop(0, batch, conv_step, 0)

    for ref in (gw1_scr, gw2_scr, gb_scr, gg_scr, gs_scr, gc_scr, cot_sum):
        ref[...] = jnp.zeros_like(ref)
    tile_rows = tile // cols
    per_image = rows // tile_rows
    gain = cols_scr[:, taps + 1 : taps + 2]
    shift = cols_scr[:, taps + 2 : taps + 3]

    def lanes_sum(x):
        total = x[:, 0:LANES]
        for k in range(LANES, x.shape[1], LANES):
            total = total + x[:, k : k + LANES]
        return total

    def step(t, _):
        b = t // per_image
        p0 = (t % per_image) * tile_rows
        x = conv_scr[b, pl.ds(p0, tile_rows)].reshape(tile, C).T
        mean = jnp.mean(x, axis=0, keepdims=True)
        centred = x - mean
        variance = jnp.mean(centred * centred, axis=0, keepdims=True)
        inverse = lax.rsqrt(variance + norm_eps)
        normed = centred * inverse
        lin = normed * gain + shift
        lh, ll = split(lin)
        cot = cot_ref[b, pl.ds(p0, tile_rows)].reshape(tile, C)
        ch, cl = split(cot)
        act = dot(w1_scr[...], jnp.concatenate([lh, lh, ll], axis=0), NN)
        d_hid = dot(w2_scr[...], jnp.concatenate([ch, ch, cl], axis=1), NT)
        bias = bias_scr[...]
        act = act + jnp.concatenate([bias] * (tile // LANES), axis=1)
        e = jnp.exp2((act * act) * (-half_log2e))
        d = 1.0 + tail_p * jnp.abs(act)
        r = pltpu.reciprocal(d, approx=True)
        r = r * (2.0 - d * r)
        q = tail_c[5] * r + tail_c[4]
        for k in (3, 2, 1, 0):
            q = q * r + tail_c[k]
        q = q * r * e
        phi = jnp.where(act > 0, 1.0 - q, q)
        hidden = act * phi
        d_act = d_hid * (phi + act * e * inverse_root_twopi)
        hh, hl = split(hidden)
        dh, dl = split(d_act)
        gb_scr[...] += lanes_sum(d_act)
        both = dot(w4_scr[...], dh, NN)
        d_lin = both[0:C] + both[C : 2 * C] + dot(w4_scr[0:C, :], dl, NN)
        gw1_scr[...] += dot(dh, jnp.concatenate([lh, ll], axis=0), NT)
        gw1_scr[:, 0:C] += dot(dl, lh, NT)
        gw2_scr[...] += dot(hh, jnp.concatenate([ch, cl], axis=1), NN)
        gw2_scr[:, 0:C] += dot(hl, ch, NN)
        gg_scr[...] += lanes_sum(d_lin * normed)
        gs_scr[...] += lanes_sum(d_lin)
        d_norm = d_lin * gain
        d_conv = inverse * (
            d_norm
            - jnp.mean(d_norm, axis=0, keepdims=True)
            - normed * jnp.mean(d_norm * normed, axis=0, keepdims=True)
        )
        gc_scr[...] += lanes_sum(d_conv)
        dconv_ref[b, pl.ds(p0, tile_rows)] = d_conv.T.reshape(tile_rows, cols, C)
        cot_sum[...] += jnp.sum(cot.reshape(tile // 8, 8, C), axis=0)
        return 0

    lax.fori_loop(0, batch * per_image, step, 0)

    even_r, _ = side(ms, "row")
    even_c, _ = side(ms, "col")
    row_a[...] = dconv_ref[:, pl.ds(jnp.where(even_r, rows - m, 0), m)]
    row_b[...] = dconv_ref[:, pl.ds(jnp.where(even_r, 0, rows - m), m)]
    first, last = dconv_ref[:, :, 0:m], dconv_ref[:, :, cols - m : cols]
    col_a[...] = jnp.where(even_c, last, first)
    col_b[...] = jnp.where(even_c, first, last)

    h = gw2_scr[:, 0:C] + gw2_scr[:, C : 2 * C]
    gw1 = (gw1_scr[:, 0:C] + gw1_scr[:, C : 2 * C]) * factor
    gw2 = h * (scale_row * factor)
    gb = (jnp.sum(gb_scr[...].T, axis=0, keepdims=True)) * factor
    for s in range(count):
        grads_ref[s, 0:hs, :] = gw1[s * hs : (s + 1) * hs, :]
        grads_ref[s, hs : 2 * hs, :] = gw2[s * hs : (s + 1) * hs, :]
    total = jnp.sum(cot_sum[...], axis=0, keepdims=True)
    outb = rows_form[taps + 3 : taps + 4, :]
    scale_grad = jnp.sum(h * wout_scr[...], axis=0, keepdims=True) + outb * total
    chan_ref[...] = jnp.zeros_like(chan_ref)
    chan_ref[0:1, 0:C] = jnp.sum(gc_scr[...].T, axis=0, keepdims=True) * factor
    chan_ref[1:2, 0:C] = jnp.sum(gg_scr[...].T, axis=0, keepdims=True) * factor
    chan_ref[2:3, 0:C] = jnp.sum(gs_scr[...].T, axis=0, keepdims=True) * factor
    chan_ref[3:4, 0:C] = total * scale_row * factor
    chan_ref[4:5, 0:C] = scale_grad * factor
    chan_ref[5:6, :] = gb


def kernel_grad_body(ms, order, factor, taps_i, taps_j, count, src_ref, dconv_ref, chan_ref, out_ref, acc_scr, rows_scr):
    batch, rows, cols, C = dconv_ref.shape
    m = taps_i // 2
    taps = taps_i * taps_j
    cs = C // count
    me = device_index(ms)
    acc_scr[...] = jnp.zeros_like(acc_scr)

    def step(b, _):
        for j in range(taps_j):
            acc = [acc_scr[i * taps_j + j] for i in range(taps_i)]
            for q in range(0, cols, 8):
                d = [dconv_ref[b, p, q : q + 8, :] for p in range(rows)]
                for r in range(rows + taps_i - 1):
                    s = src_ref[b, r, LEFT - m + q + j : LEFT - m + q + j + 8, :]
                    for i in range(taps_i):
                        p = r - i
                        if 0 <= p < rows:
                            acc[i] = acc[i] + d[p] * s
            for i in range(taps_i):
                acc_scr[i * taps_j + j] = acc[i]
        return 0

    lax.fori_loop(0, batch, step, 0)
    rows_scr[...] = jnp.zeros_like(rows_scr)
    for t in range(taps):
        rows_scr[t : t + 1, :] = jnp.sum(acc_scr[t], axis=0, keepdims=True) * factor
    rows_scr[taps : taps + 5, :] = chan_ref[0:5, 0:C]
    columns = exchange_order(rows_scr[...].T, cs, count, me)
    out_ref[...] = jnp.zeros_like(out_ref)
    hs = chan_ref.shape[1] // count
    for s in range(count):
        out_ref[s, 0:cs, :] = columns[order[s] * cs : (order[s] + 1) * cs, :]
        out_ref[s, cs : cs + 1, 0:hs] = chan_ref[5:6, s * hs : (s + 1) * hs]


def features_grad_body(ms, taps_i, taps_j, inner, got_ra, got_rb, got_ca, got_cb, small_ref, cot_ref, out_ref, ext_scr, kb_scr):
    batch, rows, cols, C = inner.shape
    m = taps_i // 2
    taps = taps_i * taps_j
    fill(ms, ext_scr, inner, got_ra, got_rb, got_ca, got_cb)
    for t in range(taps):
        kb_scr[t] = jnp.broadcast_to(small_ref[t : t + 1, :], (8, C))

    def step(b, _):
        for q in range(0, cols, 8):
            acc = depthwise_block(
                lambda r, j: ext_scr[b, r, LEFT - m + q + j : LEFT - m + q + j + 8, :],
                lambda i, j: kb_scr[taps - 1 - (i * taps_j + j)],
                rows, taps_i, taps_j, [cot_ref[b, p, q : q + 8, :] for p in range(rows)],
            )
            for p in range(rows):
                out_ref[b, p, q : q + 8, :] = acc[p]
        return 0

    lax.fori_loop(0, batch, step, 0)


def finish_body(taps_i, taps_j, cs, hs, *refs):
    parts, outs = refs[:-9], refs[-9:]
    total = parts[0][...]
    for part in parts[1:]:
        total = total + part[...]
    kernel_out, cb, ng, ns, win_out, ib, wout_out, ob, ls = outs
    taps = taps_i * taps_j
    win_out[...] = total[0:hs, :]
    wout_out[...] = total[hs : 2 * hs, :]
    small = total[2 * hs : 2 * hs + 8, :]
    for i in range(taps_i):
        kernel_out[i] = small[0:cs, i * taps_j : (i + 1) * taps_j]
    flipped = small.T
    for n, ref in enumerate((cb, ng, ns, ob, ls)):
        ref[...] = flipped[taps + n : taps + n + 1, 0:cs]
    ib[...] = small[cs : cs + 1, 0:hs]


def flip(x, mask, count):
    return lax.ppermute(x, AXES, [(i, i ^ mask) for i in range(count)])


def groups_of(ms):
    bits_col = ms["col"].bit_length() - 1
    bits_row = ms["row"].bit_length() - 1
    col = [1 << k for k in range(bits_col)]
    row = [1 << (k + bits_col) for k in range(bits_row)]
    rest = col[1:]
    out = [rest[k : k + 2] for k in range(0, len(rest), 2)]
    out += [row[k : k + 2] for k in range(0, len(row), 2)]
    return out + [col[:1]]


def masks(group):
    out = [0]
    for bit in group:
        out += [bit ^ x for x in out]
    return out


def per_device(ms, features, cotangent, conv_kernel, conv_bias, norm_gain, norm_shift, w_in, in_bias, w_out, out_bias, layer_scale):
    batch, rows, cols, C = features.shape
    taps_i, taps_j, cs = conv_kernel.shape
    hs = w_out.shape[0]
    count = ms["row"] * ms["col"]
    hid = hs * count
    m = taps_i // 2
    taps = taps_i * taps_j
    cells = batch * rows * cols * count
    factor = 1.0 / math.sqrt(cells)
    slot = 2 * hs + 8
    wide = ceil8(LEFT + cols + m)

    vm = pltpu.VMEM
    vectors = [v.reshape(1, cs) for v in (conv_bias, norm_gain, norm_shift, out_bias, layer_scale)]
    block, row_a, row_b, col_a, col_b = call(
        functools.partial(start_body, ms),
        (
            shape(slot, LANES),
            *(shape(batch, m, cols, C) for _ in range(2)),
            *(shape(batch, rows, m, C) for _ in range(2)),
        ),
        scratch=(
            vm((taps_i, cs, taps_j), f32),
            *(vm((1, cs), f32) for _ in range(5)),
            vm((1, hs), f32),
            vm((hs, C), f32),
            vm((hs, C), f32),
            vm((batch, rows, 8, C), f32),
            vm((batch, rows, 8, C), f32),
            pltpu.SemaphoreType.DMA((13,)),
        ),
        size=10**6,
        limit=None,
        in_specs=[pl.BlockSpec(memory_space=pl.ANY)] * 10,
    )(features, conv_kernel.transpose(0, 2, 1), *vectors, w_in.T, in_bias.reshape(1, hs), w_out)

    edges = tuple(shape(batch, rows + 2 * m, m, C) for _ in range(2))
    anywhere, in_vmem = pl.BlockSpec(memory_space=pl.ANY), pl.BlockSpec(memory_space=pltpu.VMEM)
    groups = groups_of(ms)
    order = [0]
    got_ra, got_rb = both_pairs(row_a, row_b, "row")
    slots = block[None]
    for n, group in enumerate(groups):
        parts = [slots] + [flip(slots, mask, count) for mask in masks(group)[1:]]
        order = [mask ^ x for mask in masks(group) for x in order]
        slots = shape(len(order), slot, LANES)
        if n == 0:
            slots, edge_a, edge_b = call(functools.partial(first_join_body, ms), (slots, *edges))(
                col_a, col_b, got_ra, got_rb, *parts
            )
            got_ca, got_cb = both_pairs(edge_a, edge_b, "col")
        else:
            waits = (got_ca, got_cb) if n == 1 else ()
            slots = call(
                functools.partial(join_body, len(waits)), slots,
                in_specs=[anywhere] * len(waits) + [in_vmem] * len(parts),
            )(*waits, *parts)
    tile = 4 * cols
    src, dconv, d_row_a, d_row_b, d_col_a, d_col_b, grads, chan, small = call(
        functools.partial(mix_body, ms, order, factor, taps_i, taps_j, tile),
        (
            shape(batch, rows + 2 * m, wide, C),
            shape(batch, rows, cols, C),
            *(shape(batch, m, cols, C) for _ in range(2)),
            *(shape(batch, rows, m, C) for _ in range(2)),
            shape(count, 2 * hs, C),
            shape(8, hid),
            shape(LANES, C),
        ),
        scratch=(
            vm((batch, rows, cols, C), f32),
            vm((C, LANES), f32),
            vm((taps, 8, C), f32),
            vm((hid, C), f32),
            vm((hid, C), f32),
            vm((hid, 3 * C), bf16),
            vm((hid, 3 * C), bf16),
            vm((2 * C, hid), bf16),
            vm((hid, LANES), f32),
            vm((hid, 2 * C), f32),
            vm((hid, 2 * C), f32),
            vm((hid, LANES), f32),
            vm((C, LANES), f32),
            vm((C, LANES), f32),
            vm((C, LANES), f32),
            vm((8, C), f32),
        ),
        flops=12 * 10**9,
        size=8 * 10**6,
        limit=24,
    )(features, got_ra, got_rb, got_ca, got_cb, slots, cotangent)

    d_got_ra, d_got_rb = both_pairs(d_row_a, d_row_b, "row")
    last = groups[-1][0]
    half = count // 2
    large_got = flip(grads[half:], last, count)
    smalls = call(
        functools.partial(kernel_grad_body, ms, order, factor, taps_i, taps_j, count),
        shape(count, 8, LANES),
        scratch=(vm((taps, 8, C), f32), vm((LANES, C), f32)),
        flops=4 * 10**9,
        size=4 * 10**6,
    )(src, dconv, chan)
    small_got = flip(smalls[half:], last, count)
    ways = len(masks(groups[-2]))
    *parts, edge_a, edge_b = call(
        functools.partial(back_join_body, ms),
        (*(shape(half // ways, slot, LANES) for _ in range(ways)), *edges),
    )(d_col_a, d_col_b, d_got_ra, d_got_rb, grads, large_got, smalls, small_got)
    d_got_ca, d_got_cb = both_pairs(edge_a, edge_b, "col")
    for n, group in reversed(list(enumerate(groups[:-1]))):
        parts = [parts[0]] + [flip(part, mask, count) for part, mask in zip(parts[1:], masks(group)[1:])]
        if n:
            whole = parts[0]
            for part in parts[1:]:
                whole = whole + part
            ways = len(masks(groups[n - 1]))
            step = whole.shape[0] // ways
            parts = [whole[k * step : (k + 1) * step] for k in range(ways)]

    features_grad = call(
        functools.partial(features_grad_body, ms, taps_i, taps_j),
        shape(batch, rows, cols, C),
        scratch=(vm((batch, rows + 2 * m, wide, C), f32), vm((taps, 8, C), f32)),
        flops=4 * 10**9,
        size=4 * 10**6,
    )(dconv, d_got_ra, d_got_rb, d_got_ca, d_got_cb, small, cotangent)

    outs = call(
        functools.partial(finish_body, taps_i, taps_j, cs, hs),
        (
            shape(taps_i, cs, taps_j),
            *(shape(1, cs) for _ in range(3)),
            shape(hs, C),
            shape(1, hs),
            shape(hs, C),
            *(shape(1, cs) for _ in range(2)),
        ),
        size=100000,
    )(*(p.reshape(slot, LANES) for p in parts))
    kernel_grad, cb, ng, ns, win, ib, wout, ob, ls = outs
    return (
        features_grad,
        kernel_grad.transpose(0, 2, 1),
        cb.reshape(cs),
        ng.reshape(cs),
        ns.reshape(cs),
        win.T,
        ib.reshape(hs),
        wout,
        ob.reshape(cs),
        ls.reshape(cs),
    )


def solution(mesh):
    both = P(AXES)
    tiles = P(None, "row", "col", None)
    in_specs = (
        tiles, tiles, P(None, None, AXES), both, both, both, P(None, AXES), both, P(AXES, None), both, both,
    )
    out_specs = (
        tiles, P(None, None, AXES), both, both, both, P(None, AXES), both, P(AXES, None), both, both,
    )
    return jax.shard_map(
        functools.partial(per_device, dict(mesh.shape)),
        mesh=mesh, in_specs=in_specs, out_specs=out_specs, check_vma=False,
    )
```

```python
import functools
import math

import jax
import jax.numpy as jnp
from jax import lax
from jax.experimental import pallas as pl
from jax.experimental.pallas import tpu as pltpu
from jax.sharding import PartitionSpec as P

norm_eps = 1e-06
inverse_root_twopi = 0.3989422804014327
half_log2e = 0.7213475204444817
tail_p = 0.275
tail_c = (
    0.1178092510180382,
    0.04211149421929024,
    0.3339322641039753,
    -0.33099338058058636,
    0.45199870802757525,
    -0.11485833206946416,
)
AXES = ("row", "col")
LANES = 128
LEFT = 8
NN = (((1,), (0,)), ((), ()))
NT = (((1,), (1,)), ((), ()))
f32, bf16 = jnp.float32, jnp.bfloat16


def ceil8(n):
    return (n + 7) // 8 * 8


def call(body, outs, scratch=(), flops=0, size=0, limit=8, **more):
    return pl.pallas_call(
        body,
        out_shape=outs,
        scratch_shapes=list(scratch),
        compiler_params=pltpu.CompilerParams(vmem_limit_bytes=limit and limit * 1024 * 1024),
        **more,
        cost_estimate=pl.CostEstimate(flops=flops, bytes_accessed=size, transcendentals=0),
    )


def shape(*dims):
    return jax.ShapeDtypeStruct(dims, f32)


def device_index(mesh_shape):
    return lax.axis_index("row") * mesh_shape["col"] + lax.axis_index("col")


def split(x):
    high = x.astype(bf16)
    return high, (x - high.astype(f32)).astype(bf16)


def dot(a, b, dims):
    return lax.dot_general(a, b, dims, preferred_element_type=f32)


def exchange_order(x, unit, count, me):
    rows = x.shape[0]
    index = lax.broadcasted_iota(jnp.int32, x.shape, 0)
    step = unit
    bit = 1
    while bit < count:
        up = pltpu.roll(x, step, 0)
        down = pltpu.roll(x, rows - step, 0)
        swapped = jnp.where((index & step) != 0, up, down)
        x = jnp.where((me & bit) != 0, swapped, x)
        step *= 2
        bit *= 2
    return x


def pairs(count, second):
    if not second:
        return [(i, i ^ 1) for i in range(count)]
    return [(i, (i + 1 if i % 2 else i - 1) % count) for i in range(count)]


def both_pairs(a, b, axis):
    count = lax.axis_size(axis)
    return lax.ppermute(a, axis, pairs(count, False)), lax.ppermute(b, axis, pairs(count, True))


def side(ms, axis):
    i = lax.axis_index(axis)
    even = i % 2 == 0
    return even, jnp.where(even, i > 0, i < ms[axis] - 1)


def start_body(ms, feat, kernel_hbm, cb, ng, ns, ob, ls, win_hbm, ib, wout_hbm, out_ref, row_a, row_b,
               kernel_scr, v0, v1, v2, v3, v4, ib_scr, win_scr, wout_scr, sems):
    batch, rows, cols, C = feat.shape
    taps_i, cs, taps_j = kernel_hbm.shape
    hs = win_hbm.shape[0]
    taps = taps_i * taps_j
    m = taps_i // 2
    even_r, _ = side(ms, "row")
    far = jnp.where(even_r, rows - m, 0)
    near = jnp.where(even_r, 0, rows - m)
    vectors = (v0, v1, v2, v3, v4)
    moves = [(kernel_hbm, kernel_scr), (win_hbm, win_scr), (wout_hbm, wout_scr), (ib, ib_scr)]
    moves += list(zip((cb, ng, ns, ob, ls), vectors))
    moves += [(feat.at[:, pl.ds(far, m)], row_a), (feat.at[:, pl.ds(near, m)], row_b)]
    copies = [pltpu.make_async_copy(src, dst, sems.at[n]) for n, (src, dst) in enumerate(moves)]
    for copy in copies:
        copy.start()
    out_ref[...] = jnp.zeros_like(out_ref)
    for copy in copies:
        copy.wait()
    out_ref[0:hs, :] = win_scr[...]
    out_ref[hs : 2 * hs, :] = wout_scr[...]
    base = 2 * hs
    for i in range(taps_i):
        out_ref[base : base + cs, i * taps_j : (i + 1) * taps_j] = kernel_scr[i]
    for n, ref in enumerate(vectors):
        column = jnp.broadcast_to(ref[...], (8, cs)).T
        out_ref[base : base + cs, taps + n : taps + n + 1] = column[:, 0:1]
    out_ref[base + cs : base + cs + 1, 0:hs] = ib_scr[...]


def with_corners(ms, edge_a, edge_b, got_a, got_b, out_a, out_b):
    batch, rows, m, C = edge_a.shape
    cols = got_a.shape[2]
    even_r, true_r = side(ms, "row")
    even_c, _ = side(ms, "col")
    out_a[:, m : m + rows] = edge_a[...]
    out_b[:, m : m + rows] = edge_b[...]
    for got, end, keep in ((got_a, even_r, None), (got_b, jnp.logical_not(even_r), true_r)):
        at = jnp.where(end, rows + m, 0)
        x = got[...]
        if keep is not None:
            x = jnp.where(keep, x, 0.0)
        last, first = x[:, :, cols - m :], x[:, :, 0:m]
        out_a[:, pl.ds(at, m)] = jnp.where(even_c, last, first)
        out_b[:, pl.ds(at, m)] = jnp.where(even_c, first, last)


def first_join_body(ms, inner, got_a, got_b, slots, out_slots, out_a, out_b, edge_a, edge_b):
    cols, m = inner.shape[2], got_a.shape[1]
    even_c, _ = side(ms, "col")
    first, last = inner[:, :, 0:m], inner[:, :, cols - m :]
    edge_a[...] = jnp.where(even_c, last, first)
    edge_b[...] = jnp.where(even_c, first, last)
    with_corners(ms, edge_a, edge_b, got_a, got_b, out_a, out_b)
    out_slots[...] = slots[...]


def back_join_body(ms, edge_a, edge_b, got_a, got_b, large, large_got, small, small_got, *refs):
    out_a, out_b = refs[-2:]
    rows = large.shape[1]
    n = 0
    for out in refs[:-2]:
        count = out.shape[0]
        out[:, 0:rows] = large[n : n + count] + large_got[n : n + count]
        out[:, rows:] = small[n : n + count] + small_got[n : n + count]
        n += count
    with_corners(ms, edge_a, edge_b, got_a, got_b, out_a, out_b)


def depthwise_block(read, weight, rows, taps_i, taps_j, start):
    acc = start
    for j in range(taps_j):
        w = [weight(i, j) for i in range(taps_i)]
        for r in range(rows + taps_i - 1):
            s = read(r, j)
            for i in range(taps_i):
                p = r - i
                if 0 <= p < rows:
                    term = w[i] * s
                    acc[p] = term if acc[p] is None else acc[p] + term
    return acc


def slot_for(distance, order):
    at = jnp.int32(0)
    bit = 1
    while bit < len(order):
        at = at + jnp.where((distance & bit) != 0, order.index(bit), 0)
        bit *= 2
    return at


def fill(ms, dst, inner, row_a, row_b, col_a, col_b):
    batch, rows, cols, _ = inner.shape
    m = row_a.shape[1]
    even_r, true_r = side(ms, "row")
    even_c, true_c = side(ms, "col")
    at_a = jnp.where(even_r, rows + m, 0)
    at_b = jnp.where(even_r, 0, rows + m)
    for b in range(batch):
        dst[b, m : m + rows, LEFT : LEFT + cols, :] = inner[b]
        dst[b, pl.ds(at_a, m), LEFT : LEFT + cols, :] = row_a[b]
        dst[b, pl.ds(at_b, m), LEFT : LEFT + cols, :] = jnp.where(true_r, row_b[b], 0.0)
        x, y = col_a[b], jnp.where(true_c, col_b[b], 0.0)
        dst[b, :, LEFT - m : LEFT, :] = jnp.where(even_c, y, x)
        dst[b, :, LEFT + cols : LEFT + cols + m, :] = jnp.where(even_c, x, y)


def mix_body(
    ms, order, holders, factor, taps_i, taps_j, tile,
    feat, got_ra, got_rb, got_ca, got_cb, slots_ref, cot_ref,
    src_ref, dconv_ref, row_a, row_b, col_a, col_b, grads_ref, chan_ref, small_ref,
    conv_scr, cols_scr, kb_scr, win_scr, wout_scr, w1_scr, w2_scr, w4_scr, bias_scr,
    gw1_scr, gw2_scr, gb_scr, gg_scr, gs_scr, gc_scr, cot_sum,
):
    batch, rows, cols, C = feat.shape
    count = slots_ref.shape[0]
    cs = C // count
    taps = taps_i * taps_j
    m = taps_i // 2
    hid = win_scr.shape[0]
    hs = hid // count
    me = device_index(ms)

    fill(ms, src_ref, feat, got_ra, got_rb, got_ca, got_cb)
    base = 2 * hs
    for s, dev in enumerate(holders):
        cols_scr[dev * cs : (dev + 1) * cs, :] = slots_ref[s, base : base + cs, :]
        win_scr[dev * hs : (dev + 1) * hs, :] = slots_ref[s, 0:hs, :]
        wout_scr[dev * hs : (dev + 1) * hs, :] = slots_ref[s, hs : 2 * hs, :]
        spread = jnp.broadcast_to(slots_ref[s, base + cs : base + cs + 1, :], (LANES, LANES)).T
        bias_scr[dev * hs : (dev + 1) * hs, :] = spread[0:hs, :]
    rows_form = cols_scr[...].T
    small_ref[...] = rows_form
    for t in range(taps):
        kb_scr[t] = jnp.broadcast_to(rows_form[t : t + 1, :], (8, C))
    conv_bias = jnp.broadcast_to(rows_form[taps : taps + 1, :], (8, C))

    scale_row = rows_form[taps + 4 : taps + 5, :]
    wh, wl = split(win_scr[...])
    w1_scr[:, 0:C] = wh
    w1_scr[:, C : 2 * C] = wl
    w1_scr[:, 2 * C : 3 * C] = wh
    oh, ol = split(wout_scr[...] * scale_row)
    w2_scr[:, 0:C] = oh
    w2_scr[:, C : 2 * C] = ol
    w2_scr[:, 2 * C : 3 * C] = oh
    th, tl = split(win_scr[...].T)
    w4_scr[0:C, :] = th
    w4_scr[C : 2 * C, :] = tl

    def conv_step(b, _):
        for q in range(0, cols, 8):
            acc = depthwise_block(
                lambda r, j: src_ref[b, r, LEFT - m + q + j : LEFT - m + q + j + 8, :],
                lambda i, j: kb_scr[i * taps_j + j],
                rows, taps_i, taps_j, [conv_bias] * rows,
            )
            for p in range(rows):
                conv_scr[b, p, q : q + 8, :] = acc[p]
        return 0

    lax.fori_loop(0, batch, conv_step, 0)

    for ref in (gw1_scr, gw2_scr, gb_scr, gg_scr, gs_scr, gc_scr, cot_sum):
        ref[...] = jnp.zeros_like(ref)
    tile_rows = tile // cols
    per_image = rows // tile_rows
    gain = cols_scr[:, taps + 1 : taps + 2]
    shift = cols_scr[:, taps + 2 : taps + 3]

    def lanes_sum(x):
        total = x[:, 0:LANES]
        for k in range(LANES, x.shape[1], LANES):
            total = total + x[:, k : k + LANES]
        return total

    def step(t, _):
        b = t // per_image
        p0 = (t % per_image) * tile_rows
        x = conv_scr[b, pl.ds(p0, tile_rows)].reshape(tile, C).T
        mean = jnp.mean(x, axis=0, keepdims=True)
        centred = x - mean
        variance = jnp.mean(centred * centred, axis=0, keepdims=True)
        inverse = lax.rsqrt(variance + norm_eps)
        normed = centred * inverse
        lin = normed * gain + shift
        lh, ll = split(lin)
        cot = cot_ref[b, pl.ds(p0, tile_rows)].reshape(tile, C)
        ch, cl = split(cot)
        act = dot(w1_scr[...], jnp.concatenate([lh, lh, ll], axis=0), NN)
        d_hid = dot(w2_scr[...], jnp.concatenate([ch, ch, cl], axis=1), NT)
        bias = bias_scr[...]
        act = act + jnp.concatenate([bias] * (tile // LANES), axis=1)
        e = jnp.exp2((act * act) * (-half_log2e))
        d = 1.0 + tail_p * jnp.abs(act)
        r = pltpu.reciprocal(d, approx=True)
        r = r * (2.0 - d * r)
        q = tail_c[5] * r + tail_c[4]
        for k in (3, 2, 1, 0):
            q = q * r + tail_c[k]
        q = q * r * e
        phi = jnp.where(act > 0, 1.0 - q, q)
        hidden = act * phi
        d_act = d_hid * (phi + act * e * inverse_root_twopi)
        hh, hl = split(hidden)
        dh, dl = split(d_act)
        gb_scr[...] += lanes_sum(d_act)
        both = dot(w4_scr[...], dh, NN)
        d_lin = both[0:C] + both[C : 2 * C] + dot(w4_scr[0:C, :], dl, NN)
        gw1_scr[...] += dot(dh, jnp.concatenate([lh, ll], axis=0), NT)
        gw1_scr[:, 0:C] += dot(dl, lh, NT)
        gw2_scr[...] += dot(hh, jnp.concatenate([ch, cl], axis=1), NN)
        gw2_scr[:, 0:C] += dot(hl, ch, NN)
        gg_scr[...] += lanes_sum(d_lin * normed)
        gs_scr[...] += lanes_sum(d_lin)
        d_norm = d_lin * gain
        d_conv = inverse * (
            d_norm
            - jnp.mean(d_norm, axis=0, keepdims=True)
            - normed * jnp.mean(d_norm * normed, axis=0, keepdims=True)
        )
        gc_scr[...] += lanes_sum(d_conv)
        dconv_ref[b, pl.ds(p0, tile_rows)] = d_conv.T.reshape(tile_rows, cols, C)
        cot_sum[...] += jnp.sum(cot.reshape(tile // 8, 8, C), axis=0)
        return 0

    lax.fori_loop(0, batch * per_image, step, 0)

    even_r, _ = side(ms, "row")
    even_c, _ = side(ms, "col")
    row_a[...] = dconv_ref[:, pl.ds(jnp.where(even_r, rows - m, 0), m)]
    row_b[...] = dconv_ref[:, pl.ds(jnp.where(even_r, 0, rows - m), m)]
    first, last = dconv_ref[:, :, 0:m], dconv_ref[:, :, cols - m : cols]
    col_a[...] = jnp.where(even_c, last, first)
    col_b[...] = jnp.where(even_c, first, last)

    h = gw2_scr[:, 0:C] + gw2_scr[:, C : 2 * C]
    gw1_scr[:, 0:C] = (gw1_scr[:, 0:C] + gw1_scr[:, C : 2 * C]) * factor
    gw2_scr[:, 0:C] = h * (scale_row * factor)
    gb = (jnp.sum(gb_scr[...].T, axis=0, keepdims=True)) * factor
    for dev in range(count):
        at = slot_for(me ^ dev, order)
        grads_ref[at, 0:hs, :] = gw1_scr[dev * hs : (dev + 1) * hs, 0:C]
        grads_ref[at, hs : 2 * hs, :] = gw2_scr[dev * hs : (dev + 1) * hs, 0:C]
    total = jnp.sum(cot_sum[...], axis=0, keepdims=True)
    outb = rows_form[taps + 3 : taps + 4, :]
    scale_grad = jnp.sum(h * wout_scr[...], axis=0, keepdims=True) + outb * total
    chan_ref[...] = jnp.zeros_like(chan_ref)
    chan_ref[0:1, 0:C] = jnp.sum(gc_scr[...].T, axis=0, keepdims=True) * factor
    chan_ref[1:2, 0:C] = jnp.sum(gg_scr[...].T, axis=0, keepdims=True) * factor
    chan_ref[2:3, 0:C] = jnp.sum(gs_scr[...].T, axis=0, keepdims=True) * factor
    chan_ref[3:4, 0:C] = total * scale_row * factor
    chan_ref[4:5, 0:C] = scale_grad * factor
    chan_ref[5:6, :] = gb


def kernel_grad_body(ms, order, factor, taps_i, taps_j, count, src_ref, dconv_ref, chan_ref, out_ref, acc_scr, rows_scr):
    batch, rows, cols, C = dconv_ref.shape
    m = taps_i // 2
    taps = taps_i * taps_j
    cs = C // count
    me = device_index(ms)
    acc_scr[...] = jnp.zeros_like(acc_scr)

    def step(b, _):
        for j in range(taps_j):
            acc = [acc_scr[i * taps_j + j] for i in range(taps_i)]
            for q in range(0, cols, 8):
                d = [dconv_ref[b, p, q : q + 8, :] for p in range(rows)]
                for r in range(rows + taps_i - 1):
                    s = src_ref[b, r, LEFT - m + q + j : LEFT - m + q + j + 8, :]
                    for i in range(taps_i):
                        p = r - i
                        if 0 <= p < rows:
                            acc[i] = acc[i] + d[p] * s
            for i in range(taps_i):
                acc_scr[i * taps_j + j] = acc[i]
        return 0

    lax.fori_loop(0, batch, step, 0)
    rows_scr[...] = jnp.zeros_like(rows_scr)
    for t in range(taps):
        rows_scr[t : t + 1, :] = jnp.sum(acc_scr[t], axis=0, keepdims=True) * factor
    rows_scr[taps : taps + 5, :] = chan_ref[0:5, 0:C]
    columns = exchange_order(rows_scr[...].T, cs, count, me)
    out_ref[...] = jnp.zeros_like(out_ref)
    hs = chan_ref.shape[1] // count
    for s in range(count):
        out_ref[s, 0:cs, :] = columns[order[s] * cs : (order[s] + 1) * cs, :]
    for dev in range(count):
        out_ref[slot_for(me ^ dev, order), cs : cs + 1, 0:hs] = chan_ref[5:6, dev * hs : (dev + 1) * hs]


def features_grad_body(ms, taps_i, taps_j, inner, got_ra, got_rb, got_ca, got_cb, small_ref, cot_ref, out_ref, ext_scr, kb_scr):
    batch, rows, cols, C = inner.shape
    m = taps_i // 2
    taps = taps_i * taps_j
    fill(ms, ext_scr, inner, got_ra, got_rb, got_ca, got_cb)
    for t in range(taps):
        kb_scr[t] = jnp.broadcast_to(small_ref[t : t + 1, :], (8, C))

    def step(b, _):
        for q in range(0, cols, 8):
            acc = depthwise_block(
                lambda r, j: ext_scr[b, r, LEFT - m + q + j : LEFT - m + q + j + 8, :],
                lambda i, j: kb_scr[taps - 1 - (i * taps_j + j)],
                rows, taps_i, taps_j, [cot_ref[b, p, q : q + 8, :] for p in range(rows)],
            )
            for p in range(rows):
                out_ref[b, p, q : q + 8, :] = acc[p]
        return 0

    lax.fori_loop(0, batch, step, 0)


def finish_body(taps_i, taps_j, cs, hs, *refs):
    parts, outs = refs[:-9], refs[-9:]
    total = parts[0][...]
    for part in parts[1:]:
        total = total + part[...]
    kernel_out, cb, ng, ns, win_out, ib, wout_out, ob, ls = outs
    taps = taps_i * taps_j
    win_out[...] = total[0:hs, :]
    wout_out[...] = total[hs : 2 * hs, :]
    small = total[2 * hs : 2 * hs + 8, :]
    for i in range(taps_i):
        kernel_out[i] = small[0:cs, i * taps_j : (i + 1) * taps_j]
    flipped = small.T
    for n, ref in enumerate((cb, ng, ns, ob, ls)):
        ref[...] = flipped[taps + n : taps + n + 1, 0:cs]
    ib[...] = small[cs : cs + 1, 0:hs]


def flip(x, mask, count):
    return lax.ppermute(x, AXES, [(i, i ^ mask) for i in range(count)])


def groups_of(ms):
    bits_col = ms["col"].bit_length() - 1
    bits_row = ms["row"].bit_length() - 1
    col = [1 << k for k in range(bits_col)]
    row = [1 << (k + bits_col) for k in range(bits_row)]
    rest = col[1:]
    out = [rest[k : k + 2] for k in range(0, len(rest), 2)]
    out += [row[k : k + 2] for k in range(0, len(row), 2)]
    return out + [col[:1]]


def masks(group):
    out = [0]
    for bit in group:
        out += [bit ^ x for x in out]
    return out


def per_device(ms, features, cotangent, conv_kernel, conv_bias, norm_gain, norm_shift, w_in, in_bias, w_out, out_bias, layer_scale):
    batch, rows, cols, C = features.shape
    taps_i, taps_j, cs = conv_kernel.shape
    hs = w_out.shape[0]
    count = ms["row"] * ms["col"]
    hid = hs * count
    m = taps_i // 2
    taps = taps_i * taps_j
    cells = batch * rows * cols * count
    factor = 1.0 / math.sqrt(cells)
    slot = 2 * hs + 8
    wide = ceil8(LEFT + cols + m)

    vm = pltpu.VMEM
    vectors = [v.reshape(1, cs) for v in (conv_bias, norm_gain, norm_shift, out_bias, layer_scale)]
    block, row_a, row_b = call(
        functools.partial(start_body, ms),
        (
            shape(slot, LANES),
            *(shape(batch, m, cols, C) for _ in range(2)),
        ),
        scratch=(
            vm((taps_i, cs, taps_j), f32),
            *(vm((1, cs), f32) for _ in range(5)),
            vm((1, hs), f32),
            vm((hs, C), f32),
            vm((hs, C), f32),
            pltpu.SemaphoreType.DMA((11,)),
        ),
        size=10**6,
        limit=None,
        in_specs=[pl.BlockSpec(memory_space=pl.ANY)] * 10,
    )(features, conv_kernel.transpose(0, 2, 1), *vectors, w_in.T, in_bias.reshape(1, hs), w_out)

    edges = tuple(shape(batch, rows + 2 * m, m, C) for _ in range(2))
    groups = groups_of(ms)
    order = [0]
    for group in groups:
        order = [mask ^ x for mask in masks(group) for x in order]
    got_ra, got_rb = both_pairs(row_a, row_b, "row")
    slots = lax.all_gather(block, "row")
    slots, edge_a, edge_b = call(
        functools.partial(first_join_body, ms),
        (shape(*slots.shape), *edges),
        scratch=[vm((batch, rows, m, C), f32) for _ in range(2)],
    )(features, got_ra, got_rb, slots)
    got_ca, got_cb = both_pairs(edge_a, edge_b, "col")
    holders = [r * ms["col"] + c for c in range(ms["col"]) for r in range(ms["row"])]
    slots = lax.all_gather(slots, "col").reshape(count, slot, LANES)
    tile = 4 * cols
    src, dconv, d_row_a, d_row_b, d_col_a, d_col_b, grads, chan, small = call(
        functools.partial(mix_body, ms, order, holders, factor, taps_i, taps_j, tile),
        (
            shape(batch, rows + 2 * m, wide, C),
            shape(batch, rows, cols, C),
            *(shape(batch, m, cols, C) for _ in range(2)),
            *(shape(batch, rows, m, C) for _ in range(2)),
            shape(count, 2 * hs, C),
            shape(8, hid),
            shape(LANES, C),
        ),
        scratch=(
            vm((batch, rows, cols, C), f32),
            vm((C, LANES), f32),
            vm((taps, 8, C), f32),
            vm((hid, C), f32),
            vm((hid, C), f32),
            vm((hid, 3 * C), bf16),
            vm((hid, 3 * C), bf16),
            vm((2 * C, hid), bf16),
            vm((hid, LANES), f32),
            vm((hid, 2 * C), f32),
            vm((hid, 2 * C), f32),
            vm((hid, LANES), f32),
            vm((C, LANES), f32),
            vm((C, LANES), f32),
            vm((C, LANES), f32),
            vm((8, C), f32),
        ),
        flops=12 * 10**9,
        size=8 * 10**6,
        limit=24,
    )(features, got_ra, got_rb, got_ca, got_cb, slots, cotangent)

    d_got_ra, d_got_rb = both_pairs(d_row_a, d_row_b, "row")
    last = groups[-1][0]
    half = count // 2
    large_got = flip(grads[half:], last, count)
    smalls = call(
        functools.partial(kernel_grad_body, ms, order, factor, taps_i, taps_j, count),
        shape(count, 8, LANES),
        scratch=(vm((taps, 8, C), f32), vm((LANES, C), f32)),
        flops=4 * 10**9,
        size=4 * 10**6,
    )(src, dconv, chan)
    small_got = flip(smalls[half:], last, count)
    ways = len(masks(groups[-2]))
    *parts, edge_a, edge_b = call(
        functools.partial(back_join_body, ms),
        (*(shape(half // ways, slot, LANES) for _ in range(ways)), *edges),
    )(d_col_a, d_col_b, d_got_ra, d_got_rb, grads, large_got, smalls, small_got)
    d_got_ca, d_got_cb = both_pairs(edge_a, edge_b, "col")
    for n, group in reversed(list(enumerate(groups[:-1]))):
        parts = [parts[0]] + [flip(part, mask, count) for part, mask in zip(parts[1:], masks(group)[1:])]
        if n:
            whole = parts[0]
            for part in parts[1:]:
                whole = whole + part
            ways = len(masks(groups[n - 1]))
            step = whole.shape[0] // ways
            parts = [whole[k * step : (k + 1) * step] for k in range(ways)]

    features_grad = call(
        functools.partial(features_grad_body, ms, taps_i, taps_j),
        shape(batch, rows, cols, C),
        scratch=(vm((batch, rows + 2 * m, wide, C), f32), vm((taps, 8, C), f32)),
        flops=4 * 10**9,
        size=4 * 10**6,
    )(dconv, d_got_ra, d_got_rb, d_got_ca, d_got_cb, small, cotangent)

    outs = call(
        functools.partial(finish_body, taps_i, taps_j, cs, hs),
        (
            shape(taps_i, cs, taps_j),
            *(shape(1, cs) for _ in range(3)),
            shape(hs, C),
            shape(1, hs),
            shape(hs, C),
            *(shape(1, cs) for _ in range(2)),
        ),
        size=100000,
    )(*(p.reshape(slot, LANES) for p in parts))
    kernel_grad, cb, ng, ns, win, ib, wout, ob, ls = outs
    return (
        features_grad,
        kernel_grad.transpose(0, 2, 1),
        cb.reshape(cs),
        ng.reshape(cs),
        ns.reshape(cs),
        win.T,
        ib.reshape(hs),
        wout,
        ob.reshape(cs),
        ls.reshape(cs),
    )


def solution(mesh):
    both = P(AXES)
    tiles = P(None, "row", "col", None)
    in_specs = (
        tiles, tiles, P(None, None, AXES), both, both, both, P(None, AXES), both, P(AXES, None), both, both,
    )
    out_specs = (
        tiles, P(None, None, AXES), both, both, both, P(None, AXES), both, P(AXES, None), both, both,
    )
    return jax.shard_map(
        functools.partial(per_device, dict(mesh.shape)),
        mesh=mesh, in_specs=in_specs, out_specs=out_specs, check_vma=False,
    )
```

```python
import functools
import math

import jax
import jax.numpy as jnp
from jax import lax
from jax.experimental import pallas as pl
from jax.experimental.pallas import tpu as pltpu
from jax.sharding import PartitionSpec as P

norm_eps = 1e-06
inverse_root_twopi = 0.3989422804014327
half_log2e = 0.7213475204444817
tail_p = 0.275
tail_c = (
    0.1178092510180382,
    0.04211149421929024,
    0.3339322641039753,
    -0.33099338058058636,
    0.45199870802757525,
    -0.11485833206946416,
)
AXES = ("row", "col")
LANES = 128
LEFT = 8
NN = (((1,), (0,)), ((), ()))
NT = (((1,), (1,)), ((), ()))
f32, bf16 = jnp.float32, jnp.bfloat16


def ceil8(n):
    return (n + 7) // 8 * 8


def call(body, outs, scratch=(), flops=0, size=0, limit=8, **more):
    return pl.pallas_call(
        body,
        out_shape=outs,
        scratch_shapes=list(scratch),
        compiler_params=pltpu.CompilerParams(vmem_limit_bytes=limit and limit * 1024 * 1024),
        **more,
        cost_estimate=pl.CostEstimate(flops=flops, bytes_accessed=size, transcendentals=0),
    )


def shape(*dims):
    return jax.ShapeDtypeStruct(dims, f32)


def device_index(mesh_shape):
    return lax.axis_index("row") * mesh_shape["col"] + lax.axis_index("col")


def split(x):
    high = x.astype(bf16)
    return high, (x - high.astype(f32)).astype(bf16)


def dot(a, b, dims):
    return lax.dot_general(a, b, dims, preferred_element_type=f32)


def exchange_order(x, unit, count, me):
    rows = x.shape[0]
    index = lax.broadcasted_iota(jnp.int32, x.shape, 0)
    step = unit
    bit = 1
    while bit < count:
        up = pltpu.roll(x, step, 0)
        down = pltpu.roll(x, rows - step, 0)
        swapped = jnp.where((index & step) != 0, up, down)
        x = jnp.where((me & bit) != 0, swapped, x)
        step *= 2
        bit *= 2
    return x


def pairs(count, second):
    if not second:
        return [(i, i ^ 1) for i in range(count)]
    return [(i, (i + 1 if i % 2 else i - 1) % count) for i in range(count)]


def both_pairs(a, b, axis):
    count = lax.axis_size(axis)
    return lax.ppermute(a, axis, pairs(count, False)), lax.ppermute(b, axis, pairs(count, True))


def side(ms, axis):
    i = lax.axis_index(axis)
    even = i % 2 == 0
    return even, jnp.where(even, i > 0, i < ms[axis] - 1)


def start_body(ms, feat, kernel_hbm, cb, ng, ns, ob, ls, win_hbm, ib, wout_hbm, out_ref, row_a, row_b,
               kernel_scr, v0, v1, v2, v3, v4, ib_scr, win_scr, wout_scr, sems):
    batch, rows, cols, C = feat.shape
    taps_i, cs, taps_j = kernel_hbm.shape
    hs = win_hbm.shape[0]
    taps = taps_i * taps_j
    m = taps_i // 2
    even_r, _ = side(ms, "row")
    far = jnp.where(even_r, rows - m, 0)
    near = jnp.where(even_r, 0, rows - m)
    vectors = (v0, v1, v2, v3, v4)
    moves = [(kernel_hbm, kernel_scr), (win_hbm, win_scr), (wout_hbm, wout_scr), (ib, ib_scr)]
    moves += list(zip((cb, ng, ns, ob, ls), vectors))
    moves += [(feat.at[:, pl.ds(far, m)], row_a), (feat.at[:, pl.ds(near, m)], row_b)]
    copies = [pltpu.make_async_copy(src, dst, sems.at[n]) for n, (src, dst) in enumerate(moves)]
    for copy in copies:
        copy.start()
    out_ref[...] = jnp.zeros_like(out_ref)
    for copy in copies:
        copy.wait()
    out_ref[0:hs, :] = win_scr[...]
    out_ref[hs : 2 * hs, :] = wout_scr[...]
    base = 2 * hs
    for i in range(taps_i):
        out_ref[base : base + cs, i * taps_j : (i + 1) * taps_j] = kernel_scr[i]
    for n, ref in enumerate(vectors):
        column = jnp.broadcast_to(ref[...], (8, cs)).T
        out_ref[base : base + cs, taps + n : taps + n + 1] = column[:, 0:1]
    out_ref[base + cs : base + cs + 1, 0:hs] = ib_scr[...]


def with_corners(ms, edge_a, edge_b, got_a, got_b, out_a, out_b):
    batch, rows, m, C = edge_a.shape
    cols = got_a.shape[2]
    even_r, true_r = side(ms, "row")
    even_c, _ = side(ms, "col")
    out_a[:, m : m + rows] = edge_a[...]
    out_b[:, m : m + rows] = edge_b[...]
    for got, end, keep in ((got_a, even_r, None), (got_b, jnp.logical_not(even_r), true_r)):
        at = jnp.where(end, rows + m, 0)
        x = got[...]
        if keep is not None:
            x = jnp.where(keep, x, 0.0)
        last, first = x[:, :, cols - m :], x[:, :, 0:m]
        out_a[:, pl.ds(at, m)] = jnp.where(even_c, last, first)
        out_b[:, pl.ds(at, m)] = jnp.where(even_c, first, last)


def lay_out(parts, out, n=0):
    for part in parts:
        out[n : n + part.shape[0]] = part[...]
        n += part.shape[0]


def first_join_body(ms, own_hbm, inner, got_a, got_b, *refs):
    parts, (slots, out_a, out_b, edge_a, edge_b, sem) = refs[:-6], refs[-6:]
    copy = pltpu.make_async_copy(own_hbm, slots.at[0:1], sem)
    copy.start()
    cols, m = inner.shape[2], got_a.shape[1]
    even_c, _ = side(ms, "col")
    first, last = inner[:, :, 0:m], inner[:, :, cols - m :]
    edge_a[...] = jnp.where(even_c, last, first)
    edge_b[...] = jnp.where(even_c, first, last)
    with_corners(ms, edge_a, edge_b, got_a, got_b, out_a, out_b)
    lay_out(parts, slots, 1)
    copy.wait()


def join_body(waits, *refs):
    lay_out(refs[waits:-1], refs[-1])


def back_join_body(ms, edge_a, edge_b, got_a, got_b, large, large_got, small, small_got, *refs):
    out_a, out_b = refs[-2:]
    rows = large.shape[1]
    n = 0
    for out in refs[:-2]:
        count = out.shape[0]
        out[:, 0:rows] = large[n : n + count] + large_got[n : n + count]
        out[:, rows:] = small[n : n + count] + small_got[n : n + count]
        n += count
    with_corners(ms, edge_a, edge_b, got_a, got_b, out_a, out_b)


def depthwise_block(read, weight, rows, taps_i, taps_j, start):
    acc = start
    for j in range(taps_j):
        w = [weight(i, j) for i in range(taps_i)]
        for r in range(rows + taps_i - 1):
            s = read(r, j)
            for i in range(taps_i):
                p = r - i
                if 0 <= p < rows:
                    term = w[i] * s
                    acc[p] = term if acc[p] is None else acc[p] + term
    return acc


def fill(ms, dst, inner, row_a, row_b, col_a, col_b):
    batch, rows, cols, _ = inner.shape
    m = row_a.shape[1]
    even_r, true_r = side(ms, "row")
    even_c, true_c = side(ms, "col")
    at_a = jnp.where(even_r, rows + m, 0)
    at_b = jnp.where(even_r, 0, rows + m)
    for b in range(batch):
        dst[b, m : m + rows, LEFT : LEFT + cols, :] = inner[b]
        dst[b, pl.ds(at_a, m), LEFT : LEFT + cols, :] = row_a[b]
        dst[b, pl.ds(at_b, m), LEFT : LEFT + cols, :] = jnp.where(true_r, row_b[b], 0.0)
        x, y = col_a[b], jnp.where(true_c, col_b[b], 0.0)
        dst[b, :, LEFT - m : LEFT, :] = jnp.where(even_c, y, x)
        dst[b, :, LEFT + cols : LEFT + cols + m, :] = jnp.where(even_c, x, y)


def small_columns(slots_ref, hs, cs, count, me, order, scratch):
    base = 2 * hs
    for s in range(count):
        scratch[order[s] * cs : (order[s] + 1) * cs, :] = slots_ref[s, base : base + cs, :]
    return exchange_order(scratch[...], cs, count, me)


def mix_body(
    ms, order, factor, taps_i, taps_j, tile,
    feat, got_ra, got_rb, got_ca, got_cb, slots_ref, cot_ref,
    src_ref, dconv_ref, row_a, row_b, col_a, col_b, grads_ref, chan_ref, small_ref,
    conv_scr, cols_scr, kb_scr, win_scr, wout_scr, w1_scr, w2_scr, w4_scr, bias_scr,
    gw1_scr, gw2_scr, gb_scr, gg_scr, gs_scr, gc_scr, cot_sum,
):
    batch, rows, cols, C = feat.shape
    count = slots_ref.shape[0]
    cs = C // count
    taps = taps_i * taps_j
    m = taps_i // 2
    hid = win_scr.shape[0]
    hs = hid // count
    me = device_index(ms)

    fill(ms, src_ref, feat, got_ra, got_rb, got_ca, got_cb)
    columns = small_columns(slots_ref, hs, cs, count, me, order, cols_scr)
    cols_scr[...] = columns
    rows_form = columns.T
    small_ref[...] = rows_form
    for t in range(taps):
        kb_scr[t] = jnp.broadcast_to(rows_form[t : t + 1, :], (8, C))
    conv_bias = jnp.broadcast_to(rows_form[taps : taps + 1, :], (8, C))

    for s in range(count):
        win_scr[s * hs : (s + 1) * hs, :] = slots_ref[s, 0:hs, :]
        wout_scr[s * hs : (s + 1) * hs, :] = slots_ref[s, hs : 2 * hs, :]
    for s in range(count):
        cols_bias = jnp.broadcast_to(slots_ref[s, 2 * hs + cs : 2 * hs + cs + 1, :], (LANES, LANES)).T
        bias_scr[s * hs : (s + 1) * hs, :] = cols_bias[0:hs, :]

    scale_row = rows_form[taps + 4 : taps + 5, :]
    wh, wl = split(win_scr[...])
    w1_scr[:, 0:C] = wh
    w1_scr[:, C : 2 * C] = wl
    w1_scr[:, 2 * C : 3 * C] = wh
    oh, ol = split(wout_scr[...] * scale_row)
    w2_scr[:, 0:C] = oh
    w2_scr[:, C : 2 * C] = ol
    w2_scr[:, 2 * C : 3 * C] = oh
    th, tl = split(win_scr[...].T)
    w4_scr[0:C, :] = th
    w4_scr[C : 2 * C, :] = tl

    def conv_step(b, _):
        for q in range(0, cols, 8):
            acc = depthwise_block(
                lambda r, j: src_ref[b, r, LEFT - m + q + j : LEFT - m + q + j + 8, :],
                lambda i, j: kb_scr[i * taps_j + j],
                rows, taps_i, taps_j, [conv_bias] * rows,
            )
            for p in range(rows):
                conv_scr[b, p, q : q + 8, :] = acc[p]
        return 0

    lax.fori_loop(0, batch, conv_step, 0)

    for ref in (gw1_scr, gw2_scr, gb_scr, gg_scr, gs_scr, gc_scr, cot_sum):
        ref[...] = jnp.zeros_like(ref)
    tile_rows = tile // cols
    per_image = rows // tile_rows
    gain = cols_scr[:, taps + 1 : taps + 2]
    shift = cols_scr[:, taps + 2 : taps + 3]

    def lanes_sum(x):
        total = x[:, 0:LANES]
        for k in range(LANES, x.shape[1], LANES):
            total = total + x[:, k : k + LANES]
        return total

    def step(t, _):
        b = t // per_image
        p0 = (t % per_image) * tile_rows
        x = conv_scr[b, pl.ds(p0, tile_rows)].reshape(tile, C).T
        mean = jnp.mean(x, axis=0, keepdims=True)
        centred = x - mean
        variance = jnp.mean(centred * centred, axis=0, keepdims=True)
        inverse = lax.rsqrt(variance + norm_eps)
        normed = centred * inverse
        lin = normed * gain + shift
        lh, ll = split(lin)
        cot = cot_ref[b, pl.ds(p0, tile_rows)].reshape(tile, C)
        ch, cl = split(cot)
        act = dot(w1_scr[...], jnp.concatenate([lh, lh, ll], axis=0), NN)
        d_hid = dot(w2_scr[...], jnp.concatenate([ch, ch, cl], axis=1), NT)
        bias = bias_scr[...]
        act = act + jnp.concatenate([bias] * (tile // LANES), axis=1)
        e = jnp.exp2((act * act) * (-half_log2e))
        d = 1.0 + tail_p * jnp.abs(act)
        r = pltpu.reciprocal(d, approx=True)
        r = r * (2.0 - d * r)
        q = tail_c[5] * r + tail_c[4]
        for k in (3, 2, 1, 0):
            q = q * r + tail_c[k]
        q = q * r * e
        phi = jnp.where(act > 0, 1.0 - q, q)
        hidden = act * phi
        d_act = d_hid * (phi + act * e * inverse_root_twopi)
        hh, hl = split(hidden)
        dh, dl = split(d_act)
        gb_scr[...] += lanes_sum(d_act)
        both = dot(w4_scr[...], dh, NN)
        d_lin = both[0:C] + both[C : 2 * C] + dot(w4_scr[0:C, :], dl, NN)
        gw1_scr[...] += dot(dh, jnp.concatenate([lh, ll], axis=0), NT)
        gw1_scr[:, 0:C] += dot(dl, lh, NT)
        gw2_scr[...] += dot(hh, jnp.concatenate([ch, cl], axis=1), NN)
        gw2_scr[:, 0:C] += dot(hl, ch, NN)
        gg_scr[...] += lanes_sum(d_lin * normed)
        gs_scr[...] += lanes_sum(d_lin)
        d_norm = d_lin * gain
        d_conv = inverse * (
            d_norm
            - jnp.mean(d_norm, axis=0, keepdims=True)
            - normed * jnp.mean(d_norm * normed, axis=0, keepdims=True)
        )
        gc_scr[...] += lanes_sum(d_conv)
        dconv_ref[b, pl.ds(p0, tile_rows)] = d_conv.T.reshape(tile_rows, cols, C)
        cot_sum[...] += jnp.sum(cot.reshape(tile // 8, 8, C), axis=0)
        return 0

    lax.fori_loop(0, batch * per_image, step, 0)

    even_r, _ = side(ms, "row")
    even_c, _ = side(ms, "col")
    row_a[...] = dconv_ref[:, pl.ds(jnp.where(even_r, rows - m, 0), m)]
    row_b[...] = dconv_ref[:, pl.ds(jnp.where(even_r, 0, rows - m), m)]
    first, last = dconv_ref[:, :, 0:m], dconv_ref[:, :, cols - m : cols]
    col_a[...] = jnp.where(even_c, last, first)
    col_b[...] = jnp.where(even_c, first, last)

    h = gw2_scr[:, 0:C] + gw2_scr[:, C : 2 * C]
    gw1 = (gw1_scr[:, 0:C] + gw1_scr[:, C : 2 * C]) * factor
    gw2 = h * (scale_row * factor)
    gb = (jnp.sum(gb_scr[...].T, axis=0, keepdims=True)) * factor
    for s in range(count):
        grads_ref[s, 0:hs, :] = gw1[s * hs : (s + 1) * hs, :]
        grads_ref[s, hs : 2 * hs, :] = gw2[s * hs : (s + 1) * hs, :]
    total = jnp.sum(cot_sum[...], axis=0, keepdims=True)
    outb = rows_form[taps + 3 : taps + 4, :]
    scale_grad = jnp.sum(h * wout_scr[...], axis=0, keepdims=True) + outb * total
    chan_ref[...] = jnp.zeros_like(chan_ref)
    chan_ref[0:1, 0:C] = jnp.sum(gc_scr[...].T, axis=0, keepdims=True) * factor
    chan_ref[1:2, 0:C] = jnp.sum(gg_scr[...].T, axis=0, keepdims=True) * factor
    chan_ref[2:3, 0:C] = jnp.sum(gs_scr[...].T, axis=0, keepdims=True) * factor
    chan_ref[3:4, 0:C] = total * scale_row * factor
    chan_ref[4:5, 0:C] = scale_grad * factor
    chan_ref[5:6, :] = gb


def kernel_grad_body(ms, order, factor, taps_i, taps_j, count, src_ref, dconv_ref, chan_ref, out_ref, acc_scr, rows_scr):
    batch, rows, cols, C = dconv_ref.shape
    m = taps_i // 2
    taps = taps_i * taps_j
    cs = C // count
    me = device_index(ms)
    acc_scr[...] = jnp.zeros_like(acc_scr)

    def step(b, _):
        for j in range(taps_j):
            acc = [acc_scr[i * taps_j + j] for i in range(taps_i)]
            for q in range(0, cols, 8):
                d = [dconv_ref[b, p, q : q + 8, :] for p in range(rows)]
                for r in range(rows + taps_i - 1):
                    s = src_ref[b, r, LEFT - m + q + j : LEFT - m + q + j + 8, :]
                    for i in range(taps_i):
                        p = r - i
                        if 0 <= p < rows:
                            acc[i] = acc[i] + d[p] * s
            for i in range(taps_i):
                acc_scr[i * taps_j + j] = acc[i]
        return 0

    lax.fori_loop(0, batch, step, 0)
    rows_scr[...] = jnp.zeros_like(rows_scr)
    for t in range(taps):
        rows_scr[t : t + 1, :] = jnp.sum(acc_scr[t], axis=0, keepdims=True) * factor
    rows_scr[taps : taps + 5, :] = chan_ref[0:5, 0:C]
    columns = exchange_order(rows_scr[...].T, cs, count, me)
    out_ref[...] = jnp.zeros_like(out_ref)
    hs = chan_ref.shape[1] // count
    for s in range(count):
        out_ref[s, 0:cs, :] = columns[order[s] * cs : (order[s] + 1) * cs, :]
        out_ref[s, cs : cs + 1, 0:hs] = chan_ref[5:6, s * hs : (s + 1) * hs]


def features_grad_body(ms, taps_i, taps_j, inner, got_ra, got_rb, got_ca, got_cb, small_ref, cot_ref, out_ref, ext_scr, kb_scr):
    batch, rows, cols, C = inner.shape
    m = taps_i // 2
    taps = taps_i * taps_j
    fill(ms, ext_scr, inner, got_ra, got_rb, got_ca, got_cb)
    for t in range(taps):
        kb_scr[t] = jnp.broadcast_to(small_ref[t : t + 1, :], (8, C))

    def step(b, _):
        for q in range(0, cols, 8):
            acc = depthwise_block(
                lambda r, j: ext_scr[b, r, LEFT - m + q + j : LEFT - m + q + j + 8, :],
                lambda i, j: kb_scr[taps - 1 - (i * taps_j + j)],
                rows, taps_i, taps_j, [cot_ref[b, p, q : q + 8, :] for p in range(rows)],
            )
            for p in range(rows):
                out_ref[b, p, q : q + 8, :] = acc[p]
        return 0

    lax.fori_loop(0, batch, step, 0)


def finish_body(taps_i, taps_j, cs, hs, *refs):
    parts, outs = refs[:-9], refs[-9:]
    total = parts[0][...]
    for part in parts[1:]:
        total = total + part[...]
    kernel_out, cb, ng, ns, win_out, ib, wout_out, ob, ls = outs
    taps = taps_i * taps_j
    win_out[...] = total[0:hs, :]
    wout_out[...] = total[hs : 2 * hs, :]
    small = total[2 * hs : 2 * hs + 8, :]
    for i in range(taps_i):
        kernel_out[i] = small[0:cs, i * taps_j : (i + 1) * taps_j]
    flipped = small.T
    for n, ref in enumerate((cb, ng, ns, ob, ls)):
        ref[...] = flipped[taps + n : taps + n + 1, 0:cs]
    ib[...] = small[cs : cs + 1, 0:hs]


def flip(x, mask, count):
    return lax.ppermute(x, AXES, [(i, i ^ mask) for i in range(count)])


def groups_of(ms):
    bits_col = ms["col"].bit_length() - 1
    bits_row = ms["row"].bit_length() - 1
    col = [1 << k for k in range(bits_col)]
    row = [1 << (k + bits_col) for k in range(bits_row)]
    rest = col[1:]
    out = [rest[k : k + 2] for k in range(0, len(rest), 2)]
    out += [row[k : k + 2] for k in range(0, len(row), 2)]
    return out + [col[:1]]


def masks(group):
    out = [0]
    for bit in group:
        out += [bit ^ x for x in out]
    return out


def per_device(ms, features, cotangent, conv_kernel, conv_bias, norm_gain, norm_shift, w_in, in_bias, w_out, out_bias, layer_scale):
    batch, rows, cols, C = features.shape
    taps_i, taps_j, cs = conv_kernel.shape
    hs = w_out.shape[0]
    count = ms["row"] * ms["col"]
    hid = hs * count
    m = taps_i // 2
    taps = taps_i * taps_j
    cells = batch * rows * cols * count
    factor = 1.0 / math.sqrt(cells)
    slot = 2 * hs + 8
    wide = ceil8(LEFT + cols + m)

    vm = pltpu.VMEM
    vectors = [v.reshape(1, cs) for v in (conv_bias, norm_gain, norm_shift, out_bias, layer_scale)]
    block, row_a, row_b = call(
        functools.partial(start_body, ms),
        (
            shape(slot, LANES),
            *(shape(batch, m, cols, C) for _ in range(2)),
        ),
        scratch=(
            vm((taps_i, cs, taps_j), f32),
            *(vm((1, cs), f32) for _ in range(5)),
            vm((1, hs), f32),
            vm((hs, C), f32),
            vm((hs, C), f32),
            pltpu.SemaphoreType.DMA((11,)),
        ),
        size=10**6,
        limit=None,
        in_specs=[pl.BlockSpec(memory_space=pl.ANY)] * 10,
    )(features, conv_kernel.transpose(0, 2, 1), *vectors, w_in.T, in_bias.reshape(1, hs), w_out)

    edges = tuple(shape(batch, rows + 2 * m, m, C) for _ in range(2))
    anywhere, in_vmem = pl.BlockSpec(memory_space=pl.ANY), pl.BlockSpec(memory_space=pltpu.VMEM)
    groups = groups_of(ms)
    order = [0]
    got_ra, got_rb = both_pairs(row_a, row_b, "row")
    slots = block[None]
    for n, group in enumerate(groups):
        parts = [slots] + [flip(slots, mask, count) for mask in masks(group)[1:]]
        order = [mask ^ x for mask in masks(group) for x in order]
        slots = shape(len(order), slot, LANES)
        if n == 0:
            slots, edge_a, edge_b = call(
                functools.partial(first_join_body, ms),
                (slots, *edges),
                scratch=(*(vm((batch, rows, m, C), f32) for _ in range(2)), pltpu.SemaphoreType.DMA),
                in_specs=[anywhere] + [in_vmem] * (len(parts) + 2),
            )(parts[0], features, got_ra, got_rb, *parts[1:])
            got_ca, got_cb = both_pairs(edge_a, edge_b, "col")
        else:
            waits = (got_ca, got_cb) if n == 1 else ()
            slots = call(
                functools.partial(join_body, len(waits)), slots,
                in_specs=[anywhere] * len(waits) + [in_vmem] * len(parts),
            )(*waits, *parts)
    tile = 8 * cols
    src, dconv, d_row_a, d_row_b, d_col_a, d_col_b, grads, chan, small = call(
        functools.partial(mix_body, ms, order, factor, taps_i, taps_j, tile),
        (
            shape(batch, rows + 2 * m, wide, C),
            shape(batch, rows, cols, C),
            *(shape(batch, m, cols, C) for _ in range(2)),
            *(shape(batch, rows, m, C) for _ in range(2)),
            shape(count, 2 * hs, C),
            shape(8, hid),
            shape(LANES, C),
        ),
        scratch=(
            vm((batch, rows, cols, C), f32),
            vm((C, LANES), f32),
            vm((taps, 8, C), f32),
            vm((hid, C), f32),
            vm((hid, C), f32),
            vm((hid, 3 * C), bf16),
            vm((hid, 3 * C), bf16),
            vm((2 * C, hid), bf16),
            vm((hid, LANES), f32),
            vm((hid, 2 * C), f32),
            vm((hid, 2 * C), f32),
            vm((hid, LANES), f32),
            vm((C, LANES), f32),
            vm((C, LANES), f32),
            vm((C, LANES), f32),
            vm((8, C), f32),
        ),
        flops=12 * 10**9,
        size=8 * 10**6,
        limit=24,
    )(features, got_ra, got_rb, got_ca, got_cb, slots, cotangent)

    d_got_ra, d_got_rb = both_pairs(d_row_a, d_row_b, "row")
    last = groups[-1][0]
    half = count // 2
    large_got = flip(grads[half:], last, count)
    smalls = call(
        functools.partial(kernel_grad_body, ms, order, factor, taps_i, taps_j, count),
        shape(count, 8, LANES),
        scratch=(vm((taps, 8, C), f32), vm((LANES, C), f32)),
        flops=4 * 10**9,
        size=4 * 10**6,
    )(src, dconv, chan)
    small_got = flip(smalls[half:], last, count)
    ways = len(masks(groups[-2]))
    *parts, edge_a, edge_b = call(
        functools.partial(back_join_body, ms),
        (*(shape(half // ways, slot, LANES) for _ in range(ways)), *edges),
    )(d_col_a, d_col_b, d_got_ra, d_got_rb, grads, large_got, smalls, small_got)
    d_got_ca, d_got_cb = both_pairs(edge_a, edge_b, "col")
    for n, group in reversed(list(enumerate(groups[:-1]))):
        parts = [parts[0]] + [flip(part, mask, count) for part, mask in zip(parts[1:], masks(group)[1:])]
        if n:
            whole = parts[0]
            for part in parts[1:]:
                whole = whole + part
            ways = len(masks(groups[n - 1]))
            step = whole.shape[0] // ways
            parts = [whole[k * step : (k + 1) * step] for k in range(ways)]

    features_grad = call(
        functools.partial(features_grad_body, ms, taps_i, taps_j),
        shape(batch, rows, cols, C),
        scratch=(vm((batch, rows + 2 * m, wide, C), f32), vm((taps, 8, C), f32)),
        flops=4 * 10**9,
        size=4 * 10**6,
    )(dconv, d_got_ra, d_got_rb, d_got_ca, d_got_cb, small, cotangent)

    outs = call(
        functools.partial(finish_body, taps_i, taps_j, cs, hs),
        (
            shape(taps_i, cs, taps_j),
            *(shape(1, cs) for _ in range(3)),
            shape(hs, C),
            shape(1, hs),
            shape(hs, C),
            *(shape(1, cs) for _ in range(2)),
        ),
        size=100000,
    )(*(p.reshape(slot, LANES) for p in parts))
    kernel_grad, cb, ng, ns, win, ib, wout, ob, ls = outs
    return (
        features_grad,
        kernel_grad.transpose(0, 2, 1),
        cb.reshape(cs),
        ng.reshape(cs),
        ns.reshape(cs),
        win.T,
        ib.reshape(hs),
        wout,
        ob.reshape(cs),
        ls.reshape(cs),
    )


def solution(mesh):
    both = P(AXES)
    tiles = P(None, "row", "col", None)
    in_specs = (
        tiles, tiles, P(None, None, AXES), both, both, both, P(None, AXES), both, P(AXES, None), both, both,
    )
    out_specs = (
        tiles, P(None, None, AXES), both, both, both, P(None, AXES), both, P(AXES, None), both, both,
    )
    return jax.shard_map(
        functools.partial(per_device, dict(mesh.shape)),
        mesh=mesh, in_specs=in_specs, out_specs=out_specs, check_vma=False,
    )
```

```python
import functools
import math

import jax
import jax.numpy as jnp
from jax import lax
from jax.experimental import pallas as pl
from jax.experimental.pallas import tpu as pltpu
from jax.sharding import PartitionSpec as P

norm_eps = 1e-06
inverse_root_twopi = 0.3989422804014327
half_log2e = 0.7213475204444817
tail_p = 0.275
tail_c = (
    0.1178092510180382,
    0.04211149421929024,
    0.3339322641039753,
    -0.33099338058058636,
    0.45199870802757525,
    -0.11485833206946416,
)
AXES = ("row", "col")
LANES = 128
LEFT = 8
NN = (((1,), (0,)), ((), ()))
NT = (((1,), (1,)), ((), ()))
f32, bf16 = jnp.float32, jnp.bfloat16


def ceil8(n):
    return (n + 7) // 8 * 8


def call(body, outs, scratch=(), flops=0, size=0, limit=8, **more):
    return pl.pallas_call(
        body,
        out_shape=outs,
        scratch_shapes=list(scratch),
        compiler_params=pltpu.CompilerParams(vmem_limit_bytes=limit and limit * 1024 * 1024),
        **more,
        cost_estimate=pl.CostEstimate(flops=flops, bytes_accessed=size, transcendentals=0),
    )


def shape(*dims):
    return jax.ShapeDtypeStruct(dims, f32)


def device_index(mesh_shape):
    return lax.axis_index("row") * mesh_shape["col"] + lax.axis_index("col")


def split(x):
    high = x.astype(bf16)
    return high, (x - high.astype(f32)).astype(bf16)


def dot(a, b, dims):
    return lax.dot_general(a, b, dims, preferred_element_type=f32)


def exchange_order(x, unit, count, me):
    rows = x.shape[0]
    index = lax.broadcasted_iota(jnp.int32, x.shape, 0)
    step = unit
    bit = 1
    while bit < count:
        up = pltpu.roll(x, step, 0)
        down = pltpu.roll(x, rows - step, 0)
        swapped = jnp.where((index & step) != 0, up, down)
        x = jnp.where((me & bit) != 0, swapped, x)
        step *= 2
        bit *= 2
    return x


def pairs(count, second):
    if not second:
        return [(i, i ^ 1) for i in range(count)]
    return [(i, i + 1 if i % 2 else i - 1) for i in range(1, count - 1)]


def both_pairs(a, b, axis):
    count = lax.axis_size(axis)
    return lax.ppermute(a, axis, pairs(count, False)), lax.ppermute(b, axis, pairs(count, True))


def even(axis):
    return lax.axis_index(axis) % 2 == 0


def start_body(feat, kernel_hbm, cb, ng, ns, ob, ls, win_hbm, ib, wout_hbm, out_ref, row_a, row_b,
               kernel_scr, v0, v1, v2, v3, v4, ib_scr, win_scr, wout_scr, sems):
    batch, rows, cols, C = feat.shape
    taps_i, cs, taps_j = kernel_hbm.shape
    hs = win_hbm.shape[0]
    taps = taps_i * taps_j
    m = taps_i // 2
    even_r = even("row")
    far = jnp.where(even_r, rows - m, 0)
    near = jnp.where(even_r, 0, rows - m)
    vectors = (v0, v1, v2, v3, v4)
    moves = [(kernel_hbm, kernel_scr), (win_hbm, win_scr), (wout_hbm, wout_scr), (ib, ib_scr)]
    moves += list(zip((cb, ng, ns, ob, ls), vectors))
    moves += [(feat.at[:, pl.ds(far, m)], row_a), (feat.at[:, pl.ds(near, m)], row_b)]
    copies = [pltpu.make_async_copy(src, dst, sems.at[n]) for n, (src, dst) in enumerate(moves)]
    for copy in copies:
        copy.start()
    out_ref[...] = jnp.zeros_like(out_ref)
    for copy in copies:
        copy.wait()
    out_ref[0:hs, :] = win_scr[...]
    out_ref[hs : 2 * hs, :] = wout_scr[...]
    base = 2 * hs
    for i in range(taps_i):
        out_ref[base : base + cs, i * taps_j : (i + 1) * taps_j] = kernel_scr[i]
    for n, ref in enumerate(vectors):
        column = jnp.broadcast_to(ref[...], (8, cs)).T
        out_ref[base : base + cs, taps + n : taps + n + 1] = column[:, 0:1]
    out_ref[base + cs : base + cs + 1, 0:hs] = ib_scr[...]


def halo_rows(rows, m, batch):
    return (m + 3) // 4 * 4, batch * (rows + 2 * m)


def with_corners(edge_a, edge_b, got_a, got_b, out_a, out_b):
    batch, rows, m, C = edge_a.shape
    cols = got_a.shape[2]
    even_r, even_c = even("row"), even("col")
    out_a[:, m : m + rows] = edge_a[...]
    out_b[:, m : m + rows] = edge_b[...]
    for got, end in ((got_a, even_r), (got_b, jnp.logical_not(even_r))):
        at = jnp.where(end, rows + m, 0)
        last, first = got[:, :, cols - m :], got[:, :, 0:m]
        out_a[:, pl.ds(at, m)] = jnp.where(even_c, last, first)
        out_b[:, pl.ds(at, m)] = jnp.where(even_c, first, last)


def join_body(inner, got_a, got_b, *refs):
    parts, (message, out_b, out_a, edge_a, edge_b) = refs[:-5], refs[-5:]
    cols, m = inner.shape[2], got_a.shape[1]
    even_c = even("col")
    first, last = inner[:, :, 0:m], inner[:, :, cols - m :]
    edge_a[...] = jnp.where(even_c, last, first)
    edge_b[...] = jnp.where(even_c, first, last)
    with_corners(edge_a, edge_b, got_a, got_b, out_a, out_b)
    n = 0
    for part in parts:
        for k in range(part.shape[0]):
            message[n : n + part.shape[1], :] = part[k]
            n += part.shape[1]
    batch, rows, _, _ = out_a.shape
    step = (message.shape[0] - n) // (batch * rows)
    for b in range(batch):
        for r in range(rows):
            message[n : n + m, :] = out_a[b, r]
            n += step


def corners_body(edge_a, edge_b, got_a, got_b, out_a, out_b):
    with_corners(edge_a, edge_b, got_a, got_b, out_a, out_b)


def depthwise_block(read, weight, rows, taps_i, taps_j, start):
    acc = start
    for j in range(taps_j):
        w = [weight(i, j) for i in range(taps_i)]
        for r in range(rows + taps_i - 1):
            s = read(r, j)
            for i in range(taps_i):
                p = r - i
                if 0 <= p < rows:
                    term = w[i] * s
                    acc[p] = term if acc[p] is None else acc[p] + term
    return acc


def fill(dst, inner, row_a, row_b, col_a, col_b):
    batch, rows, cols, _ = inner.shape
    m = row_a.shape[1]
    even_r, even_c = even("row"), even("col")
    at_a = jnp.where(even_r, rows + m, 0)
    at_b = jnp.where(even_r, 0, rows + m)
    for b in range(batch):
        dst[b, m : m + rows, LEFT : LEFT + cols, :] = inner[b]
        dst[b, pl.ds(at_a, m), LEFT : LEFT + cols, :] = row_a[b]
        dst[b, pl.ds(at_b, m), LEFT : LEFT + cols, :] = row_b[b]
        for r in range(rows + 2 * m):
            x, y = col_a(b, r), col_b[b, r]
            dst[b, r, LEFT - m : LEFT, :] = jnp.where(even_c, y, x)
            dst[b, r, LEFT + cols : LEFT + cols + m, :] = jnp.where(even_c, x, y)


def small_columns(read, hs, cs, count, me, order, scratch):
    for s in range(count):
        scratch[order[s] * cs : (order[s] + 1) * cs, :] = read(s, 2 * hs, cs)
    return exchange_order(scratch[...], cs, count, me)


def mix_body(
    ms, order, factor, taps_i, taps_j, tile,
    feat, got_ra, got_rb, got_cb, kept, got, cot_ref,
    src_ref, dconv_ref, row_a, row_b, edge_a, edge_b, grads_ref, chan_ref, small_ref,
    conv_scr, cols_scr, kb_scr, win_scr, wout_scr, w1_scr, w2_scr, w4_scr, bias_scr,
    gw1_scr, gw2_scr, gb_scr, gg_scr, gs_scr, gc_scr, cot_sum,
):
    batch, rows, cols, C = feat.shape
    count = len(order)
    cs = C // count
    taps = taps_i * taps_j
    m = taps_i // 2
    hid = win_scr.shape[0]
    hs = hid // count
    me = device_index(ms)
    half = count // 2
    slot = 2 * hs + 8
    step_rows = (got.shape[0] - half * slot) // (batch * (rows + 2 * m))

    def read(s, first, size):
        at = (s % half) * slot + first
        return (kept if s < half else got)[at : at + size, :]

    def col_a(b, r):
        at = half * slot + (b * (rows + 2 * m) + r) * step_rows
        return got[at : at + m, :]

    fill(src_ref, feat, got_ra, got_rb, col_a, got_cb)
    columns = small_columns(read, hs, cs, count, me, order, cols_scr)
    cols_scr[...] = columns
    rows_form = columns.T
    small_ref[...] = rows_form
    for t in range(taps):
        kb_scr[t] = jnp.broadcast_to(rows_form[t : t + 1, :], (8, C))
    conv_bias = jnp.broadcast_to(rows_form[taps : taps + 1, :], (8, C))

    for s in range(count):
        win_scr[s * hs : (s + 1) * hs, :] = read(s, 0, hs)
        wout_scr[s * hs : (s + 1) * hs, :] = read(s, hs, hs)
    for s in range(count):
        cols_bias = jnp.broadcast_to(read(s, 2 * hs + cs, 1), (LANES, LANES)).T
        bias_scr[s * hs : (s + 1) * hs, :] = cols_bias[0:hs, :]

    scale_row = rows_form[taps + 4 : taps + 5, :]
    wh, wl = split(win_scr[...])
    w1_scr[:, 0:C] = wh
    w1_scr[:, C : 2 * C] = wl
    w1_scr[:, 2 * C : 3 * C] = wh
    oh, ol = split(wout_scr[...] * scale_row)
    w2_scr[:, 0:C] = oh
    w2_scr[:, C : 2 * C] = ol
    w2_scr[:, 2 * C : 3 * C] = oh
    th, tl = split(win_scr[...].T)
    w4_scr[0:C, :] = th
    w4_scr[C : 2 * C, :] = tl

    def conv_step(b, _):
        for q in range(0, cols, 8):
            acc = depthwise_block(
                lambda r, j: src_ref[b, r, LEFT - m + q + j : LEFT - m + q + j + 8, :],
                lambda i, j: kb_scr[i * taps_j + j],
                rows, taps_i, taps_j, [conv_bias] * rows,
            )
            for p in range(rows):
                conv_scr[b, p, q : q + 8, :] = acc[p]
        return 0

    lax.fori_loop(0, batch, conv_step, 0)

    for ref in (gw1_scr, gw2_scr, gb_scr, gg_scr, gs_scr, gc_scr, cot_sum):
        ref[...] = jnp.zeros_like(ref)
    tile_rows = tile // cols
    per_image = rows // tile_rows
    gain = cols_scr[:, taps + 1 : taps + 2]
    shift = cols_scr[:, taps + 2 : taps + 3]

    def lanes_sum(x):
        total = x[:, 0:LANES]
        for k in range(LANES, x.shape[1], LANES):
            total = total + x[:, k : k + LANES]
        return total

    def step(t, _):
        b = t // per_image
        p0 = (t % per_image) * tile_rows
        x = conv_scr[b, pl.ds(p0, tile_rows)].reshape(tile, C).T
        mean = jnp.mean(x, axis=0, keepdims=True)
        centred = x - mean
        variance = jnp.mean(centred * centred, axis=0, keepdims=True)
        inverse = lax.rsqrt(variance + norm_eps)
        normed = centred * inverse
        lin = normed * gain + shift
        lh, ll = split(lin)
        cot = cot_ref[b, pl.ds(p0, tile_rows)].reshape(tile, C)
        ch, cl = split(cot)
        act = dot(w1_scr[...], jnp.concatenate([lh, lh, ll], axis=0), NN)
        d_hid = dot(w2_scr[...], jnp.concatenate([ch, ch, cl], axis=1), NT)
        bias = bias_scr[...]
        act = act + jnp.concatenate([bias] * (tile // LANES), axis=1)
        e = jnp.exp2((act * act) * (-half_log2e))
        d = 1.0 + tail_p * jnp.abs(act)
        r = pltpu.reciprocal(d, approx=True)
        r = r * (2.0 - d * r)
        q = tail_c[5] * r + tail_c[4]
        for k in (3, 2, 1, 0):
            q = q * r + tail_c[k]
        q = q * r * e
        phi = jnp.where(act > 0, 1.0 - q, q)
        hidden = act * phi
        d_act = d_hid * (phi + act * e * inverse_root_twopi)
        hh, hl = split(hidden)
        dh, dl = split(d_act)
        gb_scr[...] += lanes_sum(d_act)
        both = dot(w4_scr[...], dh, NN)
        d_lin = both[0:C] + both[C : 2 * C] + dot(w4_scr[0:C, :], dl, NN)
        gw1_scr[...] += dot(dh, jnp.concatenate([lh, ll], axis=0), NT)
        gw1_scr[:, 0:C] += dot(dl, lh, NT)
        gw2_scr[...] += dot(hh, jnp.concatenate([ch, cl], axis=1), NN)
        gw2_scr[:, 0:C] += dot(hl, ch, NN)
        gg_scr[...] += lanes_sum(d_lin * normed)
        gs_scr[...] += lanes_sum(d_lin)
        d_norm = d_lin * gain
        d_conv = inverse * (
            d_norm
            - jnp.mean(d_norm, axis=0, keepdims=True)
            - normed * jnp.mean(d_norm * normed, axis=0, keepdims=True)
        )
        gc_scr[...] += lanes_sum(d_conv)
        dconv_ref[b, pl.ds(p0, tile_rows)] = d_conv.T.reshape(tile_rows, cols, C)
        cot_sum[...] += jnp.sum(cot.reshape(tile // 8, 8, C), axis=0)
        return 0

    lax.fori_loop(0, batch * per_image, step, 0)

    even_r, even_c = even("row"), even("col")
    row_a[...] = dconv_ref[:, pl.ds(jnp.where(even_r, rows - m, 0), m)]
    row_b[...] = dconv_ref[:, pl.ds(jnp.where(even_r, 0, rows - m), m)]
    first, last = dconv_ref[:, :, 0:m], dconv_ref[:, :, cols - m : cols]
    edge_a[...] = jnp.where(even_c, last, first)
    edge_b[...] = jnp.where(even_c, first, last)

    h = gw2_scr[:, 0:C] + gw2_scr[:, C : 2 * C]
    gw1 = (gw1_scr[:, 0:C] + gw1_scr[:, C : 2 * C]) * factor
    gw2 = h * (scale_row * factor)
    gb = (jnp.sum(gb_scr[...].T, axis=0, keepdims=True)) * factor
    for s in range(count):
        grads_ref[s, 0:hs, :] = gw1[s * hs : (s + 1) * hs, :]
        grads_ref[s, hs : 2 * hs, :] = gw2[s * hs : (s + 1) * hs, :]
    total = jnp.sum(cot_sum[...], axis=0, keepdims=True)
    outb = rows_form[taps + 3 : taps + 4, :]
    scale_grad = jnp.sum(h * wout_scr[...], axis=0, keepdims=True) + outb * total
    chan_ref[...] = jnp.zeros_like(chan_ref)
    chan_ref[0:1, 0:C] = jnp.sum(gc_scr[...].T, axis=0, keepdims=True) * factor
    chan_ref[1:2, 0:C] = jnp.sum(gg_scr[...].T, axis=0, keepdims=True) * factor
    chan_ref[2:3, 0:C] = jnp.sum(gs_scr[...].T, axis=0, keepdims=True) * factor
    chan_ref[3:4, 0:C] = total * scale_row * factor
    chan_ref[4:5, 0:C] = scale_grad * factor
    chan_ref[5:6, :] = gb


def kernel_grad_body(ms, order, factor, taps_i, taps_j, count, src_ref, dconv_ref, chan_ref, out_ref, acc_scr, rows_scr):
    batch, rows, cols, C = dconv_ref.shape
    m = taps_i // 2
    taps = taps_i * taps_j
    cs = C // count
    me = device_index(ms)
    acc_scr[...] = jnp.zeros_like(acc_scr)

    def step(b, _):
        for j in range(taps_j):
            acc = [acc_scr[i * taps_j + j] for i in range(taps_i)]
            for q in range(0, cols, 8):
                d = [dconv_ref[b, p, q : q + 8, :] for p in range(rows)]
                for r in range(rows + taps_i - 1):
                    s = src_ref[b, r, LEFT - m + q + j : LEFT - m + q + j + 8, :]
                    for i in range(taps_i):
                        p = r - i
                        if 0 <= p < rows:
                            acc[i] = acc[i] + d[p] * s
            for i in range(taps_i):
                acc_scr[i * taps_j + j] = acc[i]
        return 0

    lax.fori_loop(0, batch, step, 0)
    rows_scr[...] = jnp.zeros_like(rows_scr)
    for t in range(taps):
        rows_scr[t : t + 1, :] = jnp.sum(acc_scr[t], axis=0, keepdims=True) * factor
    rows_scr[taps : taps + 5, :] = chan_ref[0:5, 0:C]
    columns = exchange_order(rows_scr[...].T, cs, count, me)
    out_ref[...] = jnp.zeros_like(out_ref)
    hs = chan_ref.shape[1] // count
    for s in range(count):
        out_ref[s, 0:cs, :] = columns[order[s] * cs : (order[s] + 1) * cs, :]
        out_ref[s, cs : cs + 1, 0:hs] = chan_ref[5:6, s * hs : (s + 1) * hs]


def features_grad_body(taps_i, taps_j, inner, got_ra, got_rb, got_ca, got_cb, small_ref, cot_ref, out_ref, ext_scr, kb_scr):
    batch, rows, cols, C = inner.shape
    m = taps_i // 2
    taps = taps_i * taps_j
    fill(ext_scr, inner, got_ra, got_rb, lambda b, r: got_ca[b, r], got_cb)
    for t in range(taps):
        kb_scr[t] = jnp.broadcast_to(small_ref[t : t + 1, :], (8, C))

    def step(b, _):
        for q in range(0, cols, 8):
            acc = depthwise_block(
                lambda r, j: ext_scr[b, r, LEFT - m + q + j : LEFT - m + q + j + 8, :],
                lambda i, j: kb_scr[taps - 1 - (i * taps_j + j)],
                rows, taps_i, taps_j, [cot_ref[b, p, q : q + 8, :] for p in range(rows)],
            )
            for p in range(rows):
                out_ref[b, p, q : q + 8, :] = acc[p]
        return 0

    lax.fori_loop(0, batch, step, 0)


def finish_body(taps_i, taps_j, cs, hs, *refs):
    parts, outs = refs[:-9], refs[-9:]
    total = parts[0][...]
    for part in parts[1:]:
        total = total + part[...]
    kernel_out, cb, ng, ns, win_out, ib, wout_out, ob, ls = outs
    taps = taps_i * taps_j
    win_out[...] = total[0:hs, :]
    wout_out[...] = total[hs : 2 * hs, :]
    small = total[2 * hs : 2 * hs + 8, :]
    for i in range(taps_i):
        kernel_out[i] = small[0:cs, i * taps_j : (i + 1) * taps_j]
    flipped = small.T
    for n, ref in enumerate((cb, ng, ns, ob, ls)):
        ref[...] = flipped[taps + n : taps + n + 1, 0:cs]
    ib[...] = small[cs : cs + 1, 0:hs]


def flip(x, mask, count):
    return lax.ppermute(x, AXES, [(i, i ^ mask) for i in range(count)])


def groups_of(ms):
    bits_col = ms["col"].bit_length() - 1
    bits_row = ms["row"].bit_length() - 1
    col = [1 << k for k in range(bits_col)]
    row = [1 << (k + bits_col) for k in range(bits_row)]
    rest = col[1:]
    out = [rest[k : k + 2] for k in range(0, len(rest), 2)]
    out += [row[k : k + 2] for k in range(0, len(row), 2)]
    return out + [col[:1]]


def masks(group):
    out = [0]
    for bit in group:
        out += [bit ^ x for x in out]
    return out


def per_device(ms, features, cotangent, conv_kernel, conv_bias, norm_gain, norm_shift, w_in, in_bias, w_out, out_bias, layer_scale):
    batch, rows, cols, C = features.shape
    taps_i, taps_j, cs = conv_kernel.shape
    hs = w_out.shape[0]
    count = ms["row"] * ms["col"]
    hid = hs * count
    m = taps_i // 2
    taps = taps_i * taps_j
    cells = batch * rows * cols * count
    factor = 1.0 / math.sqrt(cells)
    slot = 2 * hs + 8
    wide = ceil8(LEFT + cols + m)

    vm = pltpu.VMEM
    vectors = [v.reshape(1, cs) for v in (conv_bias, norm_gain, norm_shift, out_bias, layer_scale)]
    block, row_a, row_b = call(
        start_body,
        (
            shape(slot, LANES),
            *(shape(batch, m, cols, C) for _ in range(2)),
        ),
        scratch=(
            vm((taps_i, cs, taps_j), f32),
            *(vm((1, cs), f32) for _ in range(5)),
            vm((1, hs), f32),
            vm((hs, C), f32),
            vm((hs, C), f32),
            pltpu.SemaphoreType.DMA((11,)),
        ),
        size=10**6,
        limit=None,
        in_specs=[pl.BlockSpec(memory_space=pl.ANY)] * 10,
    )(features, conv_kernel.transpose(0, 2, 1), *vectors, w_in.T, in_bias.reshape(1, hs), w_out)

    edges = tuple(shape(batch, rows + 2 * m, m, C) for _ in range(2))
    groups = groups_of(ms)
    order = [0]
    got_ra, got_rb = both_pairs(row_a, row_b, "row")
    parts = [block[None]]
    for group in groups[:-1]:
        slots = jnp.concatenate(parts)
        parts = [slots] + [flip(slots, mask, count) for mask in masks(group)[1:]]
        order = [mask ^ x for mask in masks(group) for x in order]
    per_row, halo = halo_rows(rows, m, batch)
    half = count // 2
    message, edge_b = call(
        join_body,
        (shape(half * slot + halo * per_row, LANES), edges[0]),
        scratch=[vm(edges[0].shape, f32)] + [vm((batch, rows, m, C), f32) for _ in range(2)],
    )(features, got_ra, got_rb, *parts)
    last = groups[-1][0]
    order += [last ^ x for x in order]
    got_cb = lax.ppermute(edge_b, "col", pairs(ms["col"], True))
    got = flip(message, last, count)
    tile = 8 * cols
    src, dconv, d_row_a, d_row_b, d_edge_a, d_edge_b, grads, chan, small = call(
        functools.partial(mix_body, ms, order, factor, taps_i, taps_j, tile),
        (
            shape(batch, rows + 2 * m, wide, C),
            shape(batch, rows, cols, C),
            *(shape(batch, m, cols, C) for _ in range(2)),
            *(shape(batch, rows, m, C) for _ in range(2)),
            shape(count, 2 * hs, C),
            shape(8, hid),
            shape(LANES, C),
        ),
        scratch=(
            vm((batch, rows, cols, C), f32),
            vm((C, LANES), f32),
            vm((taps, 8, C), f32),
            vm((hid, C), f32),
            vm((hid, C), f32),
            vm((hid, 3 * C), bf16),
            vm((hid, 3 * C), bf16),
            vm((2 * C, hid), bf16),
            vm((hid, LANES), f32),
            vm((hid, 2 * C), f32),
            vm((hid, 2 * C), f32),
            vm((hid, LANES), f32),
            vm((C, LANES), f32),
            vm((C, LANES), f32),
            vm((C, LANES), f32),
            vm((8, C), f32),
        ),
        flops=12 * 10**9,
        size=8 * 10**6,
        limit=24,
    )(features, got_ra, got_rb, got_cb, message, got, cotangent)

    d_got_ra, d_got_rb = both_pairs(d_row_a, d_row_b, "row")
    large_got = flip(grads[half:], last, count)
    smalls = call(
        functools.partial(kernel_grad_body, ms, order, factor, taps_i, taps_j, count),
        shape(count, 8, LANES),
        scratch=(vm((taps, 8, C), f32), vm((LANES, C), f32)),
        flops=4 * 10**9,
        size=4 * 10**6,
    )(src, dconv, chan)
    small_got = flip(smalls[half:], last, count)
    whole = jnp.concatenate([grads[:half] + large_got, smalls[:half] + small_got], axis=1)
    for group in reversed(groups[:-1]):
        ways = masks(group)
        step = whole.shape[0] // len(ways)
        parts = [whole[:step]]
        parts += [flip(whole[k * step : (k + 1) * step], mask, count) for k, mask in enumerate(ways) if k]
        whole = parts[0]
        for part in parts[1:]:
            whole = whole + part
    edge_a, edge_b = call(corners_body, edges)(d_edge_a, d_edge_b, d_got_ra, d_got_rb)
    d_got_ca, d_got_cb = both_pairs(edge_a, edge_b, "col")

    features_grad = call(
        functools.partial(features_grad_body, taps_i, taps_j),
        shape(batch, rows, cols, C),
        scratch=(vm((batch, rows + 2 * m, wide, C), f32), vm((taps, 8, C), f32)),
        flops=4 * 10**9,
        size=4 * 10**6,
    )(dconv, d_got_ra, d_got_rb, d_got_ca, d_got_cb, small, cotangent)

    outs = call(
        functools.partial(finish_body, taps_i, taps_j, cs, hs),
        (
            shape(taps_i, cs, taps_j),
            *(shape(1, cs) for _ in range(3)),
            shape(hs, C),
            shape(1, hs),
            shape(hs, C),
            *(shape(1, cs) for _ in range(2)),
        ),
        size=100000,
    )(*(p.reshape(slot, LANES) for p in parts))
    kernel_grad, cb, ng, ns, win, ib, wout, ob, ls = outs
    return (
        features_grad,
        kernel_grad.transpose(0, 2, 1),
        cb.reshape(cs),
        ng.reshape(cs),
        ns.reshape(cs),
        win.T,
        ib.reshape(hs),
        wout,
        ob.reshape(cs),
        ls.reshape(cs),
    )


def solution(mesh):
    both = P(AXES)
    tiles = P(None, "row", "col", None)
    in_specs = (
        tiles, tiles, P(None, None, AXES), both, both, both, P(None, AXES), both, P(AXES, None), both, both,
    )
    out_specs = (
        tiles, P(None, None, AXES), both, both, both, P(None, AXES), both, P(AXES, None), both, both,
    )
    return jax.shard_map(
        functools.partial(per_device, dict(mesh.shape)),
        mesh=mesh, in_specs=in_specs, out_specs=out_specs, check_vma=False,
    )
```

```python
import functools
import math

import jax
import jax.numpy as jnp
from jax import lax
from jax.experimental import pallas as pl
from jax.experimental.pallas import tpu as pltpu
from jax.sharding import PartitionSpec as P

norm_eps = 1e-06
inverse_root_twopi = 0.3989422804014327
half_log2e = 0.7213475204444817
tail_p = 0.275
tail_c = (
    0.1178092510180382,
    0.04211149421929024,
    0.3339322641039753,
    -0.33099338058058636,
    0.45199870802757525,
    -0.11485833206946416,
)
AXES = ("row", "col")
LANES = 128
LEFT = 8
NN = (((1,), (0,)), ((), ()))
NT = (((1,), (1,)), ((), ()))
f32, bf16 = jnp.float32, jnp.bfloat16


def ceil8(n):
    return (n + 7) // 8 * 8


def call(body, outs, scratch=(), flops=0, size=0, limit=8, **more):
    return pl.pallas_call(
        body,
        out_shape=outs,
        scratch_shapes=list(scratch),
        compiler_params=pltpu.CompilerParams(vmem_limit_bytes=limit and limit * 1024 * 1024),
        **more,
        cost_estimate=pl.CostEstimate(flops=flops, bytes_accessed=size, transcendentals=0),
    )


def shape(*dims):
    return jax.ShapeDtypeStruct(dims, f32)


def device_index(mesh_shape):
    return lax.axis_index("row") * mesh_shape["col"] + lax.axis_index("col")


def split(x):
    high = x.astype(bf16)
    return high, (x - high.astype(f32)).astype(bf16)


def dot(a, b, dims):
    return lax.dot_general(a, b, dims, preferred_element_type=f32)


def exchange_order(x, unit, count, me):
    rows = x.shape[0]
    index = lax.broadcasted_iota(jnp.int32, x.shape, 0)
    step = unit
    bit = 1
    while bit < count:
        up = pltpu.roll(x, step, 0)
        down = pltpu.roll(x, rows - step, 0)
        swapped = jnp.where((index & step) != 0, up, down)
        x = jnp.where((me & bit) != 0, swapped, x)
        step *= 2
        bit *= 2
    return x


def pairs(count, second):
    if not second:
        return [(i, i ^ 1) for i in range(count)]
    return [(i, (i + 1 if i % 2 else i - 1) % count) for i in range(count)]


def both_pairs(a, b, axis):
    count = lax.axis_size(axis)
    return lax.ppermute(a, axis, pairs(count, False)), lax.ppermute(b, axis, pairs(count, True))


def even(axis):
    return lax.axis_index(axis) % 2 == 0


def true_neighbour(ms, axis):
    i = lax.axis_index(axis)
    return jnp.where(i % 2 == 0, i > 0, i < ms[axis] - 1)


def start_body(feat, kernel_hbm, cb, ng, ns, ob, ls, win_hbm, ib, wout_hbm, out_ref, row_a, row_b,
               kernel_scr, v0, v1, v2, v3, v4, ib_scr, win_scr, wout_scr, sems):
    batch, rows, cols, C = feat.shape
    taps_i, cs, taps_j = kernel_hbm.shape
    hs = win_hbm.shape[0]
    taps = taps_i * taps_j
    m = taps_i // 2
    even_r = even("row")
    far = jnp.where(even_r, rows - m, 0)
    near = jnp.where(even_r, 0, rows - m)
    vectors = (v0, v1, v2, v3, v4)
    moves = [(kernel_hbm, kernel_scr), (win_hbm, win_scr), (wout_hbm, wout_scr), (ib, ib_scr)]
    moves += list(zip((cb, ng, ns, ob, ls), vectors))
    moves += [(feat.at[:, pl.ds(far, m)], row_a), (feat.at[:, pl.ds(near, m)], row_b)]
    copies = [pltpu.make_async_copy(src, dst, sems.at[n]) for n, (src, dst) in enumerate(moves)]
    for copy in copies:
        copy.start()
    out_ref[...] = jnp.zeros_like(out_ref)
    for copy in copies:
        copy.wait()
    out_ref[0:hs, :] = win_scr[...]
    out_ref[hs : 2 * hs, :] = wout_scr[...]
    base = 2 * hs
    for i in range(taps_i):
        out_ref[base : base + cs, i * taps_j : (i + 1) * taps_j] = kernel_scr[i]
    for n, ref in enumerate(vectors):
        column = jnp.broadcast_to(ref[...], (8, cs)).T
        out_ref[base : base + cs, taps + n : taps + n + 1] = column[:, 0:1]
    out_ref[base + cs : base + cs + 1, 0:hs] = ib_scr[...]


def with_corners(ms, edge_a, edge_b, got_a, got_b, out_a, out_b):
    batch, rows, m, C = edge_a.shape
    cols = got_a.shape[2]
    even_r, even_c = even("row"), even("col")
    out_a[:, m : m + rows, 0:m] = edge_a[...]
    out_b[:, m : m + rows, 0:m] = edge_b[...]
    true_r = true_neighbour(ms, "row")
    for got, end, keep in ((got_a, even_r, None), (got_b, jnp.logical_not(even_r), true_r)):
        at = jnp.where(end, rows + m, 0)
        last, first = got[:, :, cols - m :], got[:, :, 0:m]
        x, y = jnp.where(even_c, last, first), jnp.where(even_c, first, last)
        if keep is not None:
            x, y = jnp.where(keep, x, 0.0), jnp.where(keep, y, 0.0)
        out_a[:, pl.ds(at, m), 0:m] = x
        out_b[:, pl.ds(at, m), 0:m] = y


def first_join_body(ms, inner, got_a, got_b, *refs):
    parts, (slots, out_a, out_b, edge_a, edge_b) = refs[:-5], refs[-5:]
    cols, m = inner.shape[2], got_a.shape[1]
    even_c = even("col")
    first, last = inner[:, :, 0:m], inner[:, :, cols - m :]
    edge_a[...] = jnp.where(even_c, last, first)
    edge_b[...] = jnp.where(even_c, first, last)
    with_corners(ms, edge_a, edge_b, got_a, got_b, out_a, out_b)
    n = 0
    for part in parts:
        slots[n : n + part.shape[0]] = part[...]
        n += part.shape[0]


def message_body(waited, halo, *refs):
    parts, message = refs[:-1], refs[-1]
    n = 0
    for part in parts:
        for k in range(part.shape[0]):
            message[n : n + part.shape[1], :] = part[k]
            n += part.shape[1]
    batch, rows, m, _ = halo.shape
    step = (message.shape[0] - n) // (batch * rows)
    for b in range(batch):
        for r in range(rows):
            message[n : n + m, :] = halo[b, r]
            n += step


def back_join_body(ms, edge_a, edge_b, got_a, got_b, large, large_got, small, small_got, *refs):
    out_a, out_b = refs[-2:]
    rows = large.shape[1]
    n = 0
    for out in refs[:-2]:
        count = out.shape[0]
        out[:, 0:rows] = large[n : n + count] + large_got[n : n + count]
        out[:, rows:] = small[n : n + count] + small_got[n : n + count]
        n += count
    with_corners(ms, edge_a, edge_b, got_a, got_b, out_a, out_b)


def differences(src, out):
    for b in range(src.shape[0]):
        out[b] = src[b, 0 : src.shape[1] - 1] - src[b, 1:]


def pair_sums(weight, taps_i, taps_j, out):
    for a in range((taps_i + 1) // 2):
        for j in range(taps_j):
            w = weight(2 * a, j)
            if 2 * a + 1 < taps_i:
                w = w + weight(2 * a + 1, j)
            out[a * taps_j + j] = w


def depthwise_block(read, diff, weight, sums, rows, taps_i, taps_j, start):
    def add(total, k, term):
        total[k] = term if total[k] is None else total[k] + term

    n, n0, n1 = rows // 2, (taps_i + 1) // 2, taps_i // 2
    both, even_rows, odd_rows = [None] * n, list(start[0::2]), list(start[1::2])
    for j in range(taps_j):
        w0 = [weight(2 * a, j) for a in range(n0)]
        w1 = [weight(2 * a + 1, j) for a in range(n1)]
        ws = [sums(a, j) for a in range(n0)]
        for r in range(n + n0 - 1):
            x, d = read(2 * r + 1, j), diff(2 * r, j)
            for a in range(n0):
                if 0 <= r - a < n:
                    add(both, r - a, ws[a] * x)
                    add(even_rows, r - a, w0[a] * d)
        for r in range(n + n1 - 1):
            d = diff(2 * r + 1, j)
            for a in range(n1):
                if 0 <= r - a < n:
                    odd_rows[r - a] = odd_rows[r - a] - w1[a] * d
    out = []
    for k in range(n):
        out += [both[k] + even_rows[k], both[k] + odd_rows[k]]
    return out


def fill(ms, dst, inner, row_a, row_b, col_a, col_b):
    batch, rows, cols, _ = inner.shape
    m = row_a.shape[1]
    even_r, even_c = even("row"), even("col")
    true_r, true_c = true_neighbour(ms, "row"), true_neighbour(ms, "col")
    at_a = jnp.where(even_r, rows + m, 0)
    at_b = jnp.where(even_r, 0, rows + m)
    for b in range(batch):
        dst[b, m : m + rows, LEFT : LEFT + cols, :] = inner[b]
        dst[b, pl.ds(at_a, m), LEFT : LEFT + cols, :] = row_a[b]
        dst[b, pl.ds(at_b, m), LEFT : LEFT + cols, :] = jnp.where(true_r, row_b[b], 0.0)
        for r in range(rows + 2 * m):
            x, y = col_a(b, r), jnp.where(true_c, col_b[b, r, 0:m], 0.0)
            dst[b, r, LEFT - m : LEFT, :] = jnp.where(even_c, y, x)
            dst[b, r, LEFT + cols : LEFT + cols + m, :] = jnp.where(even_c, x, y)


def small_columns(read, hs, cs, count, me, order, scratch):
    for s in range(count):
        scratch[order[s] * cs : (order[s] + 1) * cs, :] = read(s, 2 * hs, cs)
    return exchange_order(scratch[...], cs, count, me)


def mix_body(
    ms, order, factor, taps_i, taps_j, tile,
    feat, got_ra, got_rb, got_cb, kept, got, cot_ref,
    src_ref, dconv_ref, row_a, row_b, edge_a, edge_b, grads_ref, chan_ref, small_ref,
    conv_scr, diff_scr, cols_scr, kb_scr, ks_scr, win_scr, wout_scr, w1_scr, w2_scr, w4_scr, bias_scr,
    gw1_scr, gw2_scr, gb_scr, gg_scr, gs_scr, gc_scr, cot_sum,
):
    batch, rows, cols, C = feat.shape
    count = len(order)
    cs = C // count
    taps = taps_i * taps_j
    m = taps_i // 2
    hid = win_scr.shape[0]
    hs = hid // count
    me = device_index(ms)
    half = count // 2
    slot = 2 * hs + 8
    step_rows = (got.shape[0] - half * slot) // (batch * (rows + 2 * m))

    def read(s, first, size):
        at = (s % half) * slot + first
        return (kept if s < half else got)[at : at + size, :]

    def col_a(b, r):
        at = half * slot + (b * (rows + 2 * m) + r) * step_rows
        return got[at : at + m, :]

    fill(ms, src_ref, feat, got_ra, got_rb, col_a, got_cb)
    columns = small_columns(read, hs, cs, count, me, order, cols_scr)
    cols_scr[...] = columns
    rows_form = columns.T
    small_ref[...] = rows_form
    for t in range(taps):
        kb_scr[t] = jnp.broadcast_to(rows_form[t : t + 1, :], (8, C))
    conv_bias = jnp.broadcast_to(rows_form[taps : taps + 1, :], (8, C))

    for s in range(count):
        win_scr[s * hs : (s + 1) * hs, :] = read(s, 0, hs)
        wout_scr[s * hs : (s + 1) * hs, :] = read(s, hs, hs)
    for s in range(count):
        cols_bias = jnp.broadcast_to(read(s, 2 * hs + cs, 1), (LANES, LANES)).T
        bias_scr[s * hs : (s + 1) * hs, :] = cols_bias[0:hs, :]

    scale_row = rows_form[taps + 4 : taps + 5, :]
    wh, wl = split(win_scr[...])
    w1_scr[:, 0:C] = wh
    w1_scr[:, C : 2 * C] = wl
    w1_scr[:, 2 * C : 3 * C] = wh
    oh, ol = split(wout_scr[...] * scale_row)
    w2_scr[:, 0:C] = oh
    w2_scr[:, C : 2 * C] = ol
    w2_scr[:, 2 * C : 3 * C] = oh
    th, tl = split(win_scr[...].T)
    w4_scr[0:C, :] = th
    w4_scr[C : 2 * C, :] = tl

    differences(src_ref, diff_scr)
    weight = lambda i, j: kb_scr[i * taps_j + j]
    pair_sums(weight, taps_i, taps_j, ks_scr)

    def conv_step(b, _):
        for q in range(0, cols, 8):
            acc = depthwise_block(
                lambda r, j: src_ref[b, r, LEFT - m + q + j : LEFT - m + q + j + 8, :],
                lambda r, j: diff_scr[b, r, LEFT - m + q + j : LEFT - m + q + j + 8, :],
                weight, lambda a, j: ks_scr[a * taps_j + j],
                rows, taps_i, taps_j, [conv_bias] * rows,
            )
            for p in range(rows):
                conv_scr[b, p, q : q + 8, :] = acc[p]
        return 0

    lax.fori_loop(0, batch, conv_step, 0)

    for ref in (gw1_scr, gw2_scr, gb_scr, gg_scr, gs_scr, gc_scr, cot_sum):
        ref[...] = jnp.zeros_like(ref)
    tile_rows = tile // cols
    per_image = rows // tile_rows
    gain = cols_scr[:, taps + 1 : taps + 2]
    shift = cols_scr[:, taps + 2 : taps + 3]

    def lanes_sum(x):
        total = x[:, 0:LANES]
        for k in range(LANES, x.shape[1], LANES):
            total = total + x[:, k : k + LANES]
        return total

    def step(t, _):
        b = t // per_image
        p0 = (t % per_image) * tile_rows
        x = conv_scr[b, pl.ds(p0, tile_rows)].reshape(tile, C).T
        mean = jnp.mean(x, axis=0, keepdims=True)
        centred = x - mean
        variance = jnp.mean(centred * centred, axis=0, keepdims=True)
        inverse = lax.rsqrt(variance + norm_eps)
        normed = centred * inverse
        lin = normed * gain + shift
        lh, ll = split(lin)
        cot = cot_ref[b, pl.ds(p0, tile_rows)].reshape(tile, C)
        ch, cl = split(cot)
        act = dot(w1_scr[...], jnp.concatenate([lh, lh, ll], axis=0), NN)
        d_hid = dot(w2_scr[...], jnp.concatenate([ch, ch, cl], axis=1), NT)
        bias = bias_scr[...]
        act = act + jnp.concatenate([bias] * (tile // LANES), axis=1)
        e = jnp.exp2((act * act) * (-half_log2e))
        d = 1.0 + tail_p * jnp.abs(act)
        r = pltpu.reciprocal(d, approx=True)
        r = r * (2.0 - d * r)
        q = tail_c[5] * r + tail_c[4]
        for k in (3, 2, 1, 0):
            q = q * r + tail_c[k]
        q = q * r * e
        phi = jnp.where(act > 0, 1.0 - q, q)
        hidden = act * phi
        d_act = d_hid * (phi + act * e * inverse_root_twopi)
        hh, hl = split(hidden)
        dh, dl = split(d_act)
        gb_scr[...] += lanes_sum(d_act)
        both = dot(w4_scr[...], dh, NN)
        d_lin = both[0:C] + both[C : 2 * C] + dot(w4_scr[0:C, :], dl, NN)
        gw1_scr[...] += dot(dh, jnp.concatenate([lh, ll], axis=0), NT)
        gw1_scr[:, 0:C] += dot(dl, lh, NT)
        gw2_scr[...] += dot(hh, jnp.concatenate([ch, cl], axis=1), NN)
        gw2_scr[:, 0:C] += dot(hl, ch, NN)
        gg_scr[...] += lanes_sum(d_lin * normed)
        gs_scr[...] += lanes_sum(d_lin)
        d_norm = d_lin * gain
        d_conv = inverse * (
            d_norm
            - jnp.mean(d_norm, axis=0, keepdims=True)
            - normed * jnp.mean(d_norm * normed, axis=0, keepdims=True)
        )
        gc_scr[...] += lanes_sum(d_conv)
        dconv_ref[b, pl.ds(p0, tile_rows)] = d_conv.T.reshape(tile_rows, cols, C)
        cot_sum[...] += jnp.sum(cot.reshape(tile // 8, 8, C), axis=0)
        return 0

    lax.fori_loop(0, batch * per_image, step, 0)

    even_r, even_c = even("row"), even("col")
    row_a[...] = dconv_ref[:, pl.ds(jnp.where(even_r, rows - m, 0), m)]
    row_b[...] = dconv_ref[:, pl.ds(jnp.where(even_r, 0, rows - m), m)]
    first, last = dconv_ref[:, :, 0:m], dconv_ref[:, :, cols - m : cols]
    edge_a[...] = jnp.where(even_c, last, first)
    edge_b[...] = jnp.where(even_c, first, last)

    h = gw2_scr[:, 0:C] + gw2_scr[:, C : 2 * C]
    gw1 = (gw1_scr[:, 0:C] + gw1_scr[:, C : 2 * C]) * factor
    gw2 = h * (scale_row * factor)
    gb = (jnp.sum(gb_scr[...].T, axis=0, keepdims=True)) * factor
    for s in range(count):
        grads_ref[s, 0:hs, :] = gw1[s * hs : (s + 1) * hs, :]
        grads_ref[s, hs : 2 * hs, :] = gw2[s * hs : (s + 1) * hs, :]
    total = jnp.sum(cot_sum[...], axis=0, keepdims=True)
    outb = rows_form[taps + 3 : taps + 4, :]
    scale_grad = jnp.sum(h * wout_scr[...], axis=0, keepdims=True) + outb * total
    chan_ref[...] = jnp.zeros_like(chan_ref)
    chan_ref[0:1, 0:C] = jnp.sum(gc_scr[...].T, axis=0, keepdims=True) * factor
    chan_ref[1:2, 0:C] = jnp.sum(gg_scr[...].T, axis=0, keepdims=True) * factor
    chan_ref[2:3, 0:C] = jnp.sum(gs_scr[...].T, axis=0, keepdims=True) * factor
    chan_ref[3:4, 0:C] = total * scale_row * factor
    chan_ref[4:5, 0:C] = scale_grad * factor
    chan_ref[5:6, :] = gb


def kernel_grad_body(ms, order, factor, taps_i, taps_j, count, src_ref, dconv_ref, chan_ref, out_ref, acc_scr, rows_scr, diff_scr, sum_scr):
    batch, rows, cols, C = dconv_ref.shape
    m = taps_i // 2
    taps = taps_i * taps_j
    cs = C // count
    me = device_index(ms)
    n, n0, n1 = rows // 2, (taps_i + 1) // 2, taps_i // 2
    acc_scr[...] = jnp.zeros_like(acc_scr)
    differences(src_ref, diff_scr)
    for b in range(batch):
        for k in range(n):
            sum_scr[b, k] = dconv_ref[b, 2 * k] + dconv_ref[b, 2 * k + 1]

    def step(b, _):
        for j in range(taps_j):
            both = [jnp.zeros((8, C), f32)] * n0
            first = [acc_scr[2 * a * taps_j + j] for a in range(n0)]
            second = [acc_scr[(2 * a + 1) * taps_j + j] for a in range(n1)]
            for q in range(0, cols, 8):
                own, at = pl.ds(q, 8), pl.ds(LEFT - m + q + j, 8)
                ds = [sum_scr[b, k, own, :] for k in range(n)]
                d0 = [dconv_ref[b, 2 * k, own, :] for k in range(n)]
                d1 = [dconv_ref[b, 2 * k + 1, own, :] for k in range(n)]
                for r in range(n + n0 - 1):
                    x, d = src_ref[b, 2 * r + 1, at, :], diff_scr[b, 2 * r, at, :]
                    for a in range(n0):
                        if 0 <= r - a < n:
                            both[a] = both[a] + ds[r - a] * x
                            first[a] = first[a] + d0[r - a] * d
                for r in range(n + n1 - 1):
                    d = diff_scr[b, 2 * r + 1, at, :]
                    for a in range(n1):
                        if 0 <= r - a < n:
                            second[a] = second[a] - d1[r - a] * d
            for a in range(n0):
                acc_scr[2 * a * taps_j + j] = first[a] + both[a]
            for a in range(n1):
                acc_scr[(2 * a + 1) * taps_j + j] = second[a] + both[a]
        return 0

    lax.fori_loop(0, batch, step, 0)
    rows_scr[...] = jnp.zeros_like(rows_scr)
    for t in range(taps):
        rows_scr[t : t + 1, :] = jnp.sum(acc_scr[t], axis=0, keepdims=True) * factor
    rows_scr[taps : taps + 5, :] = chan_ref[0:5, 0:C]
    columns = exchange_order(rows_scr[...].T, cs, count, me)
    out_ref[...] = jnp.zeros_like(out_ref)
    hs = chan_ref.shape[1] // count
    for s in range(count):
        out_ref[s, 0:cs, :] = columns[order[s] * cs : (order[s] + 1) * cs, :]
        out_ref[s, cs : cs + 1, 0:hs] = chan_ref[5:6, s * hs : (s + 1) * hs]


def features_grad_body(ms, taps_i, taps_j, inner, got_ra, got_rb, got_ca, got_cb, small_ref, cot_ref, out_ref, ext_scr, diff_scr, kb_scr, ks_scr):
    batch, rows, cols, C = inner.shape
    m = taps_i // 2
    taps = taps_i * taps_j
    fill(ms, ext_scr, inner, got_ra, got_rb, lambda b, r: got_ca[b, r, 0 : taps_i // 2], got_cb)
    for t in range(taps):
        kb_scr[t] = jnp.broadcast_to(small_ref[t : t + 1, :], (8, C))

    differences(ext_scr, diff_scr)
    weight = lambda i, j: kb_scr[taps - 1 - (i * taps_j + j)]
    pair_sums(weight, taps_i, taps_j, ks_scr)

    def step(b, _):
        for q in range(0, cols, 8):
            acc = depthwise_block(
                lambda r, j: ext_scr[b, r, LEFT - m + q + j : LEFT - m + q + j + 8, :],
                lambda r, j: diff_scr[b, r, LEFT - m + q + j : LEFT - m + q + j + 8, :],
                weight, lambda a, j: ks_scr[a * taps_j + j],
                rows, taps_i, taps_j, [cot_ref[b, p, q : q + 8, :] for p in range(rows)],
            )
            for p in range(rows):
                out_ref[b, p, q : q + 8, :] = acc[p]
        return 0

    lax.fori_loop(0, batch, step, 0)


def finish_body(taps_i, taps_j, cs, hs, *refs):
    parts, outs = refs[:-9], refs[-9:]
    total = parts[0][...]
    for part in parts[1:]:
        total = total + part[...]
    kernel_out, cb, ng, ns, win_out, ib, wout_out, ob, ls = outs
    taps = taps_i * taps_j
    win_out[...] = total[0:hs, :]
    wout_out[...] = total[hs : 2 * hs, :]
    small = total[2 * hs : 2 * hs + 8, :]
    for i in range(taps_i):
        kernel_out[i] = small[0:cs, i * taps_j : (i + 1) * taps_j]
    flipped = small.T
    for n, ref in enumerate((cb, ng, ns, ob, ls)):
        ref[...] = flipped[taps + n : taps + n + 1, 0:cs]
    ib[...] = small[cs : cs + 1, 0:hs]


def flip(x, mask, count):
    return lax.ppermute(x, AXES, [(i, i ^ mask) for i in range(count)])


def groups_of(ms):
    bits_col = ms["col"].bit_length() - 1
    bits_row = ms["row"].bit_length() - 1
    col = [1 << k for k in range(bits_col)]
    row = [1 << (k + bits_col) for k in range(bits_row)]
    rest = col[1:]
    out = [rest[k : k + 2] for k in range(0, len(rest), 2)]
    out += [row[k : k + 2] for k in range(0, len(row), 2)]
    return out + [col[:1]]


def masks(group):
    out = [0]
    for bit in group:
        out += [bit ^ x for x in out]
    return out


def per_device(ms, features, cotangent, conv_kernel, conv_bias, norm_gain, norm_shift, w_in, in_bias, w_out, out_bias, layer_scale):
    batch, rows, cols, C = features.shape
    taps_i, taps_j, cs = conv_kernel.shape
    hs = w_out.shape[0]
    count = ms["row"] * ms["col"]
    hid = hs * count
    m = taps_i // 2
    taps = taps_i * taps_j
    cells = batch * rows * cols * count
    factor = 1.0 / math.sqrt(cells)
    slot = 2 * hs + 8
    wide = ceil8(LEFT + cols + m)

    vm = pltpu.VMEM
    vectors = [v.reshape(1, cs) for v in (conv_bias, norm_gain, norm_shift, out_bias, layer_scale)]
    block, row_a, row_b = call(
        start_body,
        (
            shape(slot, LANES),
            *(shape(batch, m, cols, C) for _ in range(2)),
        ),
        scratch=(
            vm((taps_i, cs, taps_j), f32),
            *(vm((1, cs), f32) for _ in range(5)),
            vm((1, hs), f32),
            vm((hs, C), f32),
            vm((hs, C), f32),
            pltpu.SemaphoreType.DMA((11,)),
        ),
        size=10**6,
        limit=None,
        in_specs=[pl.BlockSpec(memory_space=pl.ANY)] * 10,
    )(features, conv_kernel.transpose(0, 2, 1), *vectors, w_in.T, in_bias.reshape(1, hs), w_out)

    wide_m = (m + 3) // 4 * 4
    edges = (shape(batch, rows + 2 * m, m, C), shape(batch, rows + 2 * m, wide_m, C))
    anywhere, in_vmem = pl.BlockSpec(memory_space=pl.ANY), pl.BlockSpec(memory_space=pltpu.VMEM)
    groups = groups_of(ms)
    order = [0]
    got_ra, got_rb = both_pairs(row_a, row_b, "row")
    parts = [block[None]]
    for n, group in enumerate(groups[:-1]):
        if n == 1:
            slots, edge_a, edge_b = call(
                functools.partial(first_join_body, ms),
                (shape(len(order), slot, LANES), *edges),
                scratch=[vm((batch, rows, m, C), f32) for _ in range(2)],
            )(features, got_ra, got_rb, *parts)
            got_cb = lax.ppermute(edge_b, "col", pairs(ms["col"], True))
        else:
            slots = jnp.concatenate(parts)
        parts = [slots] + [flip(slots, mask, count) for mask in masks(group)[1:]]
        order = [mask ^ x for mask in masks(group) for x in order]
    half = count // 2
    message = call(
        message_body,
        shape(half * slot + edges[0].shape[0] * edges[0].shape[1] * wide_m, LANES),
        in_specs=[anywhere] + [in_vmem] * (1 + len(parts)),
    )(got_cb, edge_a, *parts)
    last = groups[-1][0]
    order += [last ^ x for x in order]
    got = flip(message, last, count)
    tile = 8 * cols
    src, dconv, d_row_a, d_row_b, d_edge_a, d_edge_b, grads, chan, small = call(
        functools.partial(mix_body, ms, order, factor, taps_i, taps_j, tile),
        (
            shape(batch, rows + 2 * m, wide, C),
            shape(batch, rows, cols, C),
            *(shape(batch, m, cols, C) for _ in range(2)),
            *(shape(batch, rows, m, C) for _ in range(2)),
            shape(count, 2 * hs, C),
            shape(8, hid),
            shape(LANES, C),
        ),
        scratch=(
            vm((batch, rows, cols, C), f32),
            vm((batch, rows + 2 * m - 1, wide, C), f32),
            vm((C, LANES), f32),
            vm((taps, 8, C), f32),
            vm(((taps_i + 1) // 2 * taps_j, 8, C), f32),
            vm((hid, C), f32),
            vm((hid, C), f32),
            vm((hid, 3 * C), bf16),
            vm((hid, 3 * C), bf16),
            vm((2 * C, hid), bf16),
            vm((hid, LANES), f32),
            vm((hid, 2 * C), f32),
            vm((hid, 2 * C), f32),
            vm((hid, LANES), f32),
            vm((C, LANES), f32),
            vm((C, LANES), f32),
            vm((C, LANES), f32),
            vm((8, C), f32),
        ),
        flops=12 * 10**9,
        size=8 * 10**6,
        limit=24,
    )(features, got_ra, got_rb, got_cb, message, got, cotangent)

    d_got_ra, d_got_rb = both_pairs(d_row_a, d_row_b, "row")
    large_got = flip(grads[half:], last, count)
    smalls = call(
        functools.partial(kernel_grad_body, ms, order, factor, taps_i, taps_j, count),
        shape(count, 8, LANES),
        scratch=(
            vm((taps, 8, C), f32),
            vm((LANES, C), f32),
            vm((batch, rows + 2 * m - 1, wide, C), f32),
            vm((batch, rows // 2, cols, C), f32),
        ),
        flops=4 * 10**9,
        size=4 * 10**6,
    )(src, dconv, chan)
    small_got = flip(smalls[half:], last, count)
    ways = len(masks(groups[-2]))
    *parts, edge_a, edge_b = call(
        functools.partial(back_join_body, ms),
        (*(shape(half // ways, slot, LANES) for _ in range(ways)), edges[1], edges[1]),
    )(d_edge_a, d_edge_b, d_got_ra, d_got_rb, grads, large_got, smalls, small_got)
    d_got_ca, d_got_cb = both_pairs(edge_a, edge_b, "col")
    for n, group in reversed(list(enumerate(groups[:-1]))):
        parts = [parts[0]] + [flip(part, mask, count) for part, mask in zip(parts[1:], masks(group)[1:])]
        if n:
            whole = parts[0]
            for part in parts[1:]:
                whole = whole + part
            ways = len(masks(groups[n - 1]))
            step = whole.shape[0] // ways
            parts = [whole[k * step : (k + 1) * step] for k in range(ways)]

    features_grad = call(
        functools.partial(features_grad_body, ms, taps_i, taps_j),
        shape(batch, rows, cols, C),
        scratch=(
            vm((batch, rows + 2 * m, wide, C), f32),
            vm((batch, rows + 2 * m - 1, wide, C), f32),
            vm((taps, 8, C), f32),
            vm(((taps_i + 1) // 2 * taps_j, 8, C), f32),
        ),
        flops=4 * 10**9,
        size=4 * 10**6,
    )(dconv, d_got_ra, d_got_rb, d_got_ca, d_got_cb, small, cotangent)

    outs = call(
        functools.partial(finish_body, taps_i, taps_j, cs, hs),
        (
            shape(taps_i, cs, taps_j),
            *(shape(1, cs) for _ in range(3)),
            shape(hs, C),
            shape(1, hs),
            shape(hs, C),
            *(shape(1, cs) for _ in range(2)),
        ),
        size=100000,
    )(*(p.reshape(slot, LANES) for p in parts))
    kernel_grad, cb, ng, ns, win, ib, wout, ob, ls = outs
    return (
        features_grad,
        kernel_grad.transpose(0, 2, 1),
        cb.reshape(cs),
        ng.reshape(cs),
        ns.reshape(cs),
        win.T,
        ib.reshape(hs),
        wout,
        ob.reshape(cs),
        ls.reshape(cs),
    )


def solution(mesh):
    both = P(AXES)
    tiles = P(None, "row", "col", None)
    in_specs = (
        tiles, tiles, P(None, None, AXES), both, both, both, P(None, AXES), both, P(AXES, None), both, both,
    )
    out_specs = (
        tiles, P(None, None, AXES), both, both, both, P(None, AXES), both, P(AXES, None), both, both,
    )
    return jax.shard_map(
        functools.partial(per_device, dict(mesh.shape)),
        mesh=mesh, in_specs=in_specs, out_specs=out_specs, check_vma=False,
    )
```

```python
import functools
import math

import jax
import jax.numpy as jnp
from jax import lax
from jax.experimental import pallas as pl
from jax.experimental.pallas import tpu as pltpu
from jax.sharding import PartitionSpec as P

norm_eps = 1e-06
inverse_root_twopi = 0.3989422804014327
half_log2e = 0.7213475204444817
tail_p = 0.275
tail_c = (
    0.1178092510180382,
    0.04211149421929024,
    0.3339322641039753,
    -0.33099338058058636,
    0.45199870802757525,
    -0.11485833206946416,
)
AXES = ("row", "col")
LANES = 128
LEFT = 8
NN = (((1,), (0,)), ((), ()))
NT = (((1,), (1,)), ((), ()))
f32, bf16 = jnp.float32, jnp.bfloat16


def ceil8(n):
    return (n + 7) // 8 * 8


def call(body, outs, scratch=(), flops=0, size=0, limit=8, **more):
    return pl.pallas_call(
        body,
        out_shape=outs,
        scratch_shapes=list(scratch),
        compiler_params=pltpu.CompilerParams(vmem_limit_bytes=limit and limit * 1024 * 1024),
        **more,
        cost_estimate=pl.CostEstimate(flops=flops, bytes_accessed=size, transcendentals=0),
    )


def shape(*dims):
    return jax.ShapeDtypeStruct(dims, f32)


def device_index(mesh_shape):
    return lax.axis_index("row") * mesh_shape["col"] + lax.axis_index("col")


def split(x):
    high = x.astype(bf16)
    return high, (x - high.astype(f32)).astype(bf16)


def dot(a, b, dims):
    return lax.dot_general(a, b, dims, preferred_element_type=f32)


def exchange_order(x, unit, count, me):
    rows = x.shape[0]
    index = lax.broadcasted_iota(jnp.int32, x.shape, 0)
    step = unit
    bit = 1
    while bit < count:
        up = pltpu.roll(x, step, 0)
        down = pltpu.roll(x, rows - step, 0)
        swapped = jnp.where((index & step) != 0, up, down)
        x = jnp.where((me & bit) != 0, swapped, x)
        step *= 2
        bit *= 2
    return x


def pairs(count, second):
    if not second:
        return [(i, i ^ 1) for i in range(count)]
    return [(i, (i + 1 if i % 2 else i - 1) % count) for i in range(count)]


def both_pairs(a, b, axis):
    count = lax.axis_size(axis)
    return lax.ppermute(a, axis, pairs(count, False)), lax.ppermute(b, axis, pairs(count, True))


def even(axis):
    return lax.axis_index(axis) % 2 == 0


def true_neighbour(ms, axis):
    i = lax.axis_index(axis)
    return jnp.where(i % 2 == 0, i > 0, i < ms[axis] - 1)


def start_body(feat, kernel_hbm, cb, ng, ns, ob, ls, win_hbm, ib, wout_hbm, out_ref, row_a, row_b,
               kernel_scr, v0, v1, v2, v3, v4, ib_scr, win_scr, wout_scr, sems):
    batch, rows, cols, C = feat.shape
    taps_i, cs, taps_j = kernel_hbm.shape
    hs = win_hbm.shape[0]
    taps = taps_i * taps_j
    m = taps_i // 2
    even_r = even("row")
    far = jnp.where(even_r, rows - m, 0)
    near = jnp.where(even_r, 0, rows - m)
    vectors = (v0, v1, v2, v3, v4)
    moves = [(kernel_hbm, kernel_scr), (win_hbm, win_scr), (wout_hbm, wout_scr), (ib, ib_scr)]
    moves += list(zip((cb, ng, ns, ob, ls), vectors))
    moves += [(feat.at[:, pl.ds(far, m)], row_a), (feat.at[:, pl.ds(near, m)], row_b)]
    copies = [pltpu.make_async_copy(src, dst, sems.at[n]) for n, (src, dst) in enumerate(moves)]
    for copy in copies:
        copy.start()
    out_ref[...] = jnp.zeros_like(out_ref)
    for copy in copies:
        copy.wait()
    out_ref[0:hs, :] = win_scr[...]
    out_ref[hs : 2 * hs, :] = wout_scr[...]
    base = 2 * hs
    for i in range(taps_i):
        out_ref[base : base + cs, i * taps_j : (i + 1) * taps_j] = kernel_scr[i]
    for n, ref in enumerate(vectors):
        column = jnp.broadcast_to(ref[...], (8, cs)).T
        out_ref[base : base + cs, taps + n : taps + n + 1] = column[:, 0:1]
    out_ref[base + cs : base + cs + 1, 0:hs] = ib_scr[...]


def with_corners(ms, edge_a, edge_b, got_a, got_b, out_a, out_b):
    batch, rows, m, C = edge_a.shape
    cols = got_a.shape[2]
    even_r, even_c = even("row"), even("col")
    out_a[:, m : m + rows, 0:m] = edge_a[...]
    out_b[:, m : m + rows, 0:m] = edge_b[...]
    true_r = true_neighbour(ms, "row")
    for got, end, keep in ((got_a, even_r, None), (got_b, jnp.logical_not(even_r), true_r)):
        at = jnp.where(end, rows + m, 0)
        last, first = got[:, :, cols - m :], got[:, :, 0:m]
        x, y = jnp.where(even_c, last, first), jnp.where(even_c, first, last)
        if keep is not None:
            x, y = jnp.where(keep, x, 0.0), jnp.where(keep, y, 0.0)
        out_a[:, pl.ds(at, m), 0:m] = x
        out_b[:, pl.ds(at, m), 0:m] = y


def first_join_body(ms, inner, got_a, got_b, *refs):
    parts, (slots, out_a, out_b, edge_a, edge_b) = refs[:-5], refs[-5:]
    cols, m = inner.shape[2], got_a.shape[1]
    even_c = even("col")
    first, last = inner[:, :, 0:m], inner[:, :, cols - m :]
    edge_a[...] = jnp.where(even_c, last, first)
    edge_b[...] = jnp.where(even_c, first, last)
    with_corners(ms, edge_a, edge_b, got_a, got_b, out_a, out_b)
    n = 0
    for part in parts:
        slots[n : n + part.shape[0]] = part[...]
        n += part.shape[0]


def message_body(waited, halo, *refs):
    parts, message = refs[:-1], refs[-1]
    n = 0
    for part in parts:
        for k in range(part.shape[0]):
            message[n : n + part.shape[1], :] = part[k]
            n += part.shape[1]
    batch, rows, m, _ = halo.shape
    step = (message.shape[0] - n) // (batch * rows)
    for b in range(batch):
        for r in range(rows):
            message[n : n + m, :] = halo[b, r]
            n += step


def back_join_body(ms, edge_a, edge_b, got_a, got_b, large, large_got, small, small_got, *refs):
    out_a, out_b = refs[-2:]
    rows = large.shape[1]
    n = 0
    for out in refs[:-2]:
        count = out.shape[0]
        out[:, 0:rows] = large[n : n + count] + large_got[n : n + count]
        out[:, rows:] = small[n : n + count] + small_got[n : n + count]
        n += count
    with_corners(ms, edge_a, edge_b, got_a, got_b, out_a, out_b)


def depthwise_block(read, weight, rows, taps_i, taps_j, start):
    acc = start
    for j in range(taps_j):
        w = [weight(i, j) for i in range(taps_i)]
        for r in range(rows + taps_i - 1):
            s = read(r, j)
            for i in range(taps_i):
                p = r - i
                if 0 <= p < rows:
                    term = w[i] * s
                    acc[p] = term if acc[p] is None else acc[p] + term
    return acc


def fill(ms, dst, inner, row_a, row_b, col_a, col_b):
    batch, rows, cols, _ = inner.shape
    m = row_a.shape[1]
    even_r, even_c = even("row"), even("col")
    true_r, true_c = true_neighbour(ms, "row"), true_neighbour(ms, "col")
    at_a = jnp.where(even_r, rows + m, 0)
    at_b = jnp.where(even_r, 0, rows + m)
    for b in range(batch):
        dst[b, m : m + rows, LEFT : LEFT + cols, :] = inner[b]
        dst[b, pl.ds(at_a, m), LEFT : LEFT + cols, :] = row_a[b]
        dst[b, pl.ds(at_b, m), LEFT : LEFT + cols, :] = jnp.where(true_r, row_b[b], 0.0)
        for r in range(rows + 2 * m):
            x, y = col_a(b, r), jnp.where(true_c, col_b[b, r, 0:m], 0.0)
            dst[b, r, LEFT - m : LEFT, :] = jnp.where(even_c, y, x)
            dst[b, r, LEFT + cols : LEFT + cols + m, :] = jnp.where(even_c, x, y)


def small_columns(read, hs, cs, count, me, order, scratch):
    for s in range(count):
        scratch[order[s] * cs : (order[s] + 1) * cs, :] = read(s, 2 * hs, cs)
    return exchange_order(scratch[...], cs, count, me)


def mix_body(
    ms, order, factor, taps_i, taps_j, tile,
    feat, got_ra, got_rb, got_cb, kept, got, cot_ref,
    src_ref, dconv_ref, row_a, row_b, edge_a, edge_b, grads_ref, chan_ref, small_ref,
    conv_scr, cols_scr, kb_scr, win_scr, wout_scr, w1_scr, w2_scr, w4_scr, bias_scr,
    gw1_scr, gw2_scr, gb_scr, gg_scr, gs_scr, gc_scr, cot_sum,
):
    batch, rows, cols, C = feat.shape
    count = len(order)
    cs = C // count
    taps = taps_i * taps_j
    m = taps_i // 2
    hid = win_scr.shape[0]
    hs = hid // count
    me = device_index(ms)
    half = count // 2
    slot = 2 * hs + 8
    step_rows = (got.shape[0] - half * slot) // (batch * (rows + 2 * m))

    def read(s, first, size):
        at = (s % half) * slot + first
        return (kept if s < half else got)[at : at + size, :]

    def col_a(b, r):
        at = half * slot + (b * (rows + 2 * m) + r) * step_rows
        return got[at : at + m, :]

    fill(ms, src_ref, feat, got_ra, got_rb, col_a, got_cb)
    columns = small_columns(read, hs, cs, count, me, order, cols_scr)
    cols_scr[...] = columns
    rows_form = columns.T
    small_ref[...] = rows_form
    for t in range(taps):
        kb_scr[t] = jnp.broadcast_to(rows_form[t : t + 1, :], (8, C))
    conv_bias = jnp.broadcast_to(rows_form[taps : taps + 1, :], (8, C))

    for s in range(count):
        win_scr[s * hs : (s + 1) * hs, :] = read(s, 0, hs)
        wout_scr[s * hs : (s + 1) * hs, :] = read(s, hs, hs)
    for s in range(count):
        cols_bias = jnp.broadcast_to(read(s, 2 * hs + cs, 1), (LANES, LANES)).T
        bias_scr[s * hs : (s + 1) * hs, :] = cols_bias[0:hs, :]

    scale_row = rows_form[taps + 4 : taps + 5, :]
    wh, wl = split(win_scr[...])
    w1_scr[:, 0:C] = wh
    w1_scr[:, C : 2 * C] = wl
    w1_scr[:, 2 * C : 3 * C] = wh
    oh, ol = split(wout_scr[...] * scale_row)
    w2_scr[:, 0:C] = oh
    w2_scr[:, C : 2 * C] = ol
    w2_scr[:, 2 * C : 3 * C] = oh
    th, tl = split(win_scr[...].T)
    w4_scr[0:C, :] = th
    w4_scr[C : 2 * C, :] = tl

    def conv_step(b, _):
        for q in range(0, cols, 8):
            acc = depthwise_block(
                lambda r, j: src_ref[b, r, LEFT - m + q + j : LEFT - m + q + j + 8, :],
                lambda i, j: kb_scr[i * taps_j + j],
                rows, taps_i, taps_j, [conv_bias] * rows,
            )
            for p in range(rows):
                conv_scr[b, p, q : q + 8, :] = acc[p]
        return 0

    lax.fori_loop(0, batch, conv_step, 0)

    for ref in (gw1_scr, gw2_scr, gb_scr, gg_scr, gs_scr, gc_scr, cot_sum):
        ref[...] = jnp.zeros_like(ref)
    tile_rows = tile // cols
    per_image = rows // tile_rows
    gain = cols_scr[:, taps + 1 : taps + 2]
    shift = cols_scr[:, taps + 2 : taps + 3]

    def lanes_sum(x):
        total = x[:, 0:LANES]
        for k in range(LANES, x.shape[1], LANES):
            total = total + x[:, k : k + LANES]
        return total

    def step(t, _):
        b = t // per_image
        p0 = (t % per_image) * tile_rows
        x = conv_scr[b, pl.ds(p0, tile_rows)].reshape(tile, C).T
        mean = jnp.mean(x, axis=0, keepdims=True)
        centred = x - mean
        variance = jnp.mean(centred * centred, axis=0, keepdims=True)
        inverse = lax.rsqrt(variance + norm_eps)
        normed = centred * inverse
        lin = normed * gain + shift
        lh, ll = split(lin)
        cot = cot_ref[b, pl.ds(p0, tile_rows)].reshape(tile, C)
        ch, cl = split(cot)
        act = dot(w1_scr[...], jnp.concatenate([lh, lh, ll], axis=0), NN)
        d_hid = dot(w2_scr[...], jnp.concatenate([ch, ch, cl], axis=1), NT)
        bias = bias_scr[...]
        act = act + jnp.concatenate([bias] * (tile // LANES), axis=1)
        e = jnp.exp2((act * act) * (-half_log2e))
        d = 1.0 + tail_p * jnp.abs(act)
        r = pltpu.reciprocal(d, approx=True)
        r = r * (2.0 - d * r)
        q = tail_c[5] * r + tail_c[4]
        for k in (3, 2, 1, 0):
            q = q * r + tail_c[k]
        q = q * r * e
        phi = jnp.where(act > 0, 1.0 - q, q)
        hidden = act * phi
        d_act = d_hid * (phi + act * e * inverse_root_twopi)
        hh, hl = split(hidden)
        dh, dl = split(d_act)
        gb_scr[...] += lanes_sum(d_act)
        both = dot(w4_scr[...], dh, NN)
        d_lin = both[0:C] + both[C : 2 * C] + dot(w4_scr[0:C, :], dl, NN)
        gw1_scr[...] += dot(dh, jnp.concatenate([lh, ll], axis=0), NT)
        gw1_scr[:, 0:C] += dot(dl, lh, NT)
        gw2_scr[...] += dot(hh, jnp.concatenate([ch, cl], axis=1), NN)
        gw2_scr[:, 0:C] += dot(hl, ch, NN)
        gg_scr[...] += lanes_sum(d_lin * normed)
        gs_scr[...] += lanes_sum(d_lin)
        d_norm = d_lin * gain
        d_conv = inverse * (
            d_norm
            - jnp.mean(d_norm, axis=0, keepdims=True)
            - normed * jnp.mean(d_norm * normed, axis=0, keepdims=True)
        )
        gc_scr[...] += lanes_sum(d_conv)
        dconv_ref[b, pl.ds(p0, tile_rows)] = d_conv.T.reshape(tile_rows, cols, C)
        cot_sum[...] += jnp.sum(cot.reshape(tile // 8, 8, C), axis=0)
        return 0

    lax.fori_loop(0, batch * per_image, step, 0)

    even_r, even_c = even("row"), even("col")
    row_a[...] = dconv_ref[:, pl.ds(jnp.where(even_r, rows - m, 0), m)]
    row_b[...] = dconv_ref[:, pl.ds(jnp.where(even_r, 0, rows - m), m)]
    first, last = dconv_ref[:, :, 0:m], dconv_ref[:, :, cols - m : cols]
    edge_a[...] = jnp.where(even_c, last, first)
    edge_b[...] = jnp.where(even_c, first, last)

    h = gw2_scr[:, 0:C] + gw2_scr[:, C : 2 * C]
    gw1 = (gw1_scr[:, 0:C] + gw1_scr[:, C : 2 * C]) * factor
    gw2 = h * (scale_row * factor)
    gb = (jnp.sum(gb_scr[...].T, axis=0, keepdims=True)) * factor
    for s in range(count):
        grads_ref[s, 0:hs, :] = gw1[s * hs : (s + 1) * hs, :]
        grads_ref[s, hs : 2 * hs, :] = gw2[s * hs : (s + 1) * hs, :]
    total = jnp.sum(cot_sum[...], axis=0, keepdims=True)
    outb = rows_form[taps + 3 : taps + 4, :]
    scale_grad = jnp.sum(h * wout_scr[...], axis=0, keepdims=True) + outb * total
    chan_ref[...] = jnp.zeros_like(chan_ref)
    chan_ref[0:1, 0:C] = jnp.sum(gc_scr[...].T, axis=0, keepdims=True) * factor
    chan_ref[1:2, 0:C] = jnp.sum(gg_scr[...].T, axis=0, keepdims=True) * factor
    chan_ref[2:3, 0:C] = jnp.sum(gs_scr[...].T, axis=0, keepdims=True) * factor
    chan_ref[3:4, 0:C] = total * scale_row * factor
    chan_ref[4:5, 0:C] = scale_grad * factor
    chan_ref[5:6, :] = gb


def kernel_grad_body(ms, order, factor, taps_i, taps_j, count, src_ref, dconv_ref, chan_ref, out_ref, acc_scr, rows_scr):
    batch, rows, cols, C = dconv_ref.shape
    m = taps_i // 2
    taps = taps_i * taps_j
    cs = C // count
    me = device_index(ms)
    acc_scr[...] = jnp.zeros_like(acc_scr)

    def step(b, _):
        for j in range(taps_j):
            acc = [acc_scr[i * taps_j + j] for i in range(taps_i)]
            for q in range(0, cols, 8):
                d = [dconv_ref[b, p, q : q + 8, :] for p in range(rows)]
                for r in range(rows + taps_i - 1):
                    s = src_ref[b, r, LEFT - m + q + j : LEFT - m + q + j + 8, :]
                    for i in range(taps_i):
                        p = r - i
                        if 0 <= p < rows:
                            acc[i] = acc[i] + d[p] * s
            for i in range(taps_i):
                acc_scr[i * taps_j + j] = acc[i]
        return 0

    lax.fori_loop(0, batch, step, 0)
    rows_scr[...] = jnp.zeros_like(rows_scr)
    for t in range(taps):
        rows_scr[t : t + 1, :] = jnp.sum(acc_scr[t], axis=0, keepdims=True) * factor
    rows_scr[taps : taps + 5, :] = chan_ref[0:5, 0:C]
    columns = exchange_order(rows_scr[...].T, cs, count, me)
    out_ref[...] = jnp.zeros_like(out_ref)
    hs = chan_ref.shape[1] // count
    for s in range(count):
        out_ref[s, 0:cs, :] = columns[order[s] * cs : (order[s] + 1) * cs, :]
        out_ref[s, cs : cs + 1, 0:hs] = chan_ref[5:6, s * hs : (s + 1) * hs]


def features_grad_body(ms, taps_i, taps_j, inner, got_ra, got_rb, got_ca, got_cb, small_ref, cot_ref, out_ref, ext_scr, kb_scr):
    batch, rows, cols, C = inner.shape
    m = taps_i // 2
    taps = taps_i * taps_j
    fill(ms, ext_scr, inner, got_ra, got_rb, lambda b, r: got_ca[b, r, 0 : taps_i // 2], got_cb)
    for t in range(taps):
        kb_scr[t] = jnp.broadcast_to(small_ref[t : t + 1, :], (8, C))

    def step(b, _):
        for q in range(0, cols, 8):
            acc = depthwise_block(
                lambda r, j: ext_scr[b, r, LEFT - m + q + j : LEFT - m + q + j + 8, :],
                lambda i, j: kb_scr[taps - 1 - (i * taps_j + j)],
                rows, taps_i, taps_j, [cot_ref[b, p, q : q + 8, :] for p in range(rows)],
            )
            for p in range(rows):
                out_ref[b, p, q : q + 8, :] = acc[p]
        return 0

    lax.fori_loop(0, batch, step, 0)


def finish_body(taps_i, taps_j, cs, hs, *refs):
    parts, outs = refs[:-9], refs[-9:]
    total = parts[0][...]
    for part in parts[1:]:
        total = total + part[...]
    kernel_out, cb, ng, ns, win_out, ib, wout_out, ob, ls = outs
    taps = taps_i * taps_j
    win_out[...] = total[0:hs, :]
    wout_out[...] = total[hs : 2 * hs, :]
    small = total[2 * hs : 2 * hs + 8, :]
    for i in range(taps_i):
        kernel_out[i] = small[0:cs, i * taps_j : (i + 1) * taps_j]
    flipped = small.T
    for n, ref in enumerate((cb, ng, ns, ob, ls)):
        ref[...] = flipped[taps + n : taps + n + 1, 0:cs]
    ib[...] = small[cs : cs + 1, 0:hs]


def flip(x, mask, count):
    return lax.ppermute(x, AXES, [(i, i ^ mask) for i in range(count)])


def groups_of(ms):
    bits_col = ms["col"].bit_length() - 1
    bits_row = ms["row"].bit_length() - 1
    col = [1 << k for k in range(bits_col)]
    row = [1 << (k + bits_col) for k in range(bits_row)]
    rest = col[1:]
    out = [rest[k : k + 2] for k in range(0, len(rest), 2)]
    out += [row[k : k + 2] for k in range(0, len(row), 2)]
    return out + [col[:1]]


def masks(group):
    out = [0]
    for bit in group:
        out += [bit ^ x for x in out]
    return out


def per_device(ms, features, cotangent, conv_kernel, conv_bias, norm_gain, norm_shift, w_in, in_bias, w_out, out_bias, layer_scale):
    batch, rows, cols, C = features.shape
    taps_i, taps_j, cs = conv_kernel.shape
    hs = w_out.shape[0]
    count = ms["row"] * ms["col"]
    hid = hs * count
    m = taps_i // 2
    taps = taps_i * taps_j
    cells = batch * rows * cols * count
    factor = 1.0 / math.sqrt(cells)
    slot = 2 * hs + 8
    wide = ceil8(LEFT + cols + m)

    vm = pltpu.VMEM
    vectors = [v.reshape(1, cs) for v in (conv_bias, norm_gain, norm_shift, out_bias, layer_scale)]
    block, row_a, row_b = call(
        start_body,
        (
            shape(slot, LANES),
            *(shape(batch, m, cols, C) for _ in range(2)),
        ),
        scratch=(
            vm((taps_i, cs, taps_j), f32),
            *(vm((1, cs), f32) for _ in range(5)),
            vm((1, hs), f32),
            vm((hs, C), f32),
            vm((hs, C), f32),
            pltpu.SemaphoreType.DMA((11,)),
        ),
        size=10**6,
        limit=None,
        in_specs=[pl.BlockSpec(memory_space=pl.ANY)] * 10,
    )(features, conv_kernel.transpose(0, 2, 1), *vectors, w_in.T, in_bias.reshape(1, hs), w_out)

    wide_m = (m + 3) // 4 * 4
    edges = (shape(batch, rows + 2 * m, m, C), shape(batch, rows + 2 * m, wide_m, C))
    anywhere, in_vmem = pl.BlockSpec(memory_space=pl.ANY), pl.BlockSpec(memory_space=pltpu.VMEM)
    groups = groups_of(ms)
    order = [0]
    got_ra, got_rb = both_pairs(row_a, row_b, "row")
    parts = [block[None]]
    for n, group in enumerate(groups[:-1]):
        if n == 1:
            slots, edge_a, edge_b = call(
                functools.partial(first_join_body, ms),
                (shape(len(order), slot, LANES), *edges),
                scratch=[vm((batch, rows, m, C), f32) for _ in range(2)],
            )(features, got_ra, got_rb, *parts)
            got_cb = lax.ppermute(edge_b, "col", pairs(ms["col"], True))
        else:
            slots = jnp.concatenate(parts)
        parts = [slots] + [flip(slots, mask, count) for mask in masks(group)[1:]]
        order = [mask ^ x for mask in masks(group) for x in order]
    half = count // 2
    message = call(
        message_body,
        shape(half * slot + edges[0].shape[0] * edges[0].shape[1] * wide_m, LANES),
        in_specs=[anywhere] + [in_vmem] * (1 + len(parts)),
    )(got_cb, edge_a, *parts)
    last = groups[-1][0]
    order += [last ^ x for x in order]
    got = flip(message, last, count)
    tile = 8 * cols
    src, dconv, d_row_a, d_row_b, d_edge_a, d_edge_b, grads, chan, small = call(
        functools.partial(mix_body, ms, order, factor, taps_i, taps_j, tile),
        (
            shape(batch, rows + 2 * m, wide, C),
            shape(batch, rows, cols, C),
            *(shape(batch, m, cols, C) for _ in range(2)),
            *(shape(batch, rows, m, C) for _ in range(2)),
            shape(count, 2 * hs, C),
            shape(8, hid),
            shape(LANES, C),
        ),
        scratch=(
            vm((batch, rows, cols, C), f32),
            vm((C, LANES), f32),
            vm((taps, 8, C), f32),
            vm((hid, C), f32),
            vm((hid, C), f32),
            vm((hid, 3 * C), bf16),
            vm((hid, 3 * C), bf16),
            vm((2 * C, hid), bf16),
            vm((hid, LANES), f32),
            vm((hid, 2 * C), f32),
            vm((hid, 2 * C), f32),
            vm((hid, LANES), f32),
            vm((C, LANES), f32),
            vm((C, LANES), f32),
            vm((C, LANES), f32),
            vm((8, C), f32),
        ),
        flops=12 * 10**9,
        size=8 * 10**6,
        limit=24,
    )(features, got_ra, got_rb, got_cb, message, got, cotangent)

    d_got_ra, d_got_rb = both_pairs(d_row_a, d_row_b, "row")
    large_got = flip(grads[half:], last, count)
    smalls = call(
        functools.partial(kernel_grad_body, ms, order, factor, taps_i, taps_j, count),
        shape(count, 8, LANES),
        scratch=(
            vm((taps, 8, C), f32),
            vm((LANES, C), f32),
        ),
        flops=4 * 10**9,
        size=4 * 10**6,
    )(src, dconv, chan)
    small_got = flip(smalls[half:], last, count)
    ways = len(masks(groups[-2]))
    *parts, edge_a, edge_b = call(
        functools.partial(back_join_body, ms),
        (*(shape(half // ways, slot, LANES) for _ in range(ways)), edges[1], edges[1]),
    )(d_edge_a, d_edge_b, d_got_ra, d_got_rb, grads, large_got, smalls, small_got)
    d_got_ca, d_got_cb = both_pairs(edge_a, edge_b, "col")
    for n, group in reversed(list(enumerate(groups[:-1]))):
        parts = [parts[0]] + [flip(part, mask, count) for part, mask in zip(parts[1:], masks(group)[1:])]
        if n:
            whole = parts[0]
            for part in parts[1:]:
                whole = whole + part
            ways = len(masks(groups[n - 1]))
            step = whole.shape[0] // ways
            parts = [whole[k * step : (k + 1) * step] for k in range(ways)]

    features_grad = call(
        functools.partial(features_grad_body, ms, taps_i, taps_j),
        shape(batch, rows, cols, C),
        scratch=(
            vm((batch, rows + 2 * m, wide, C), f32),
            vm((taps, 8, C), f32),
        ),
        flops=4 * 10**9,
        size=4 * 10**6,
    )(dconv, d_got_ra, d_got_rb, d_got_ca, d_got_cb, small, cotangent)

    outs = call(
        functools.partial(finish_body, taps_i, taps_j, cs, hs),
        (
            shape(taps_i, cs, taps_j),
            *(shape(1, cs) for _ in range(3)),
            shape(hs, C),
            shape(1, hs),
            shape(hs, C),
            *(shape(1, cs) for _ in range(2)),
        ),
        size=100000,
    )(*(p.reshape(slot, LANES) for p in parts))
    kernel_grad, cb, ng, ns, win, ib, wout, ob, ls = outs
    return (
        features_grad,
        kernel_grad.transpose(0, 2, 1),
        cb.reshape(cs),
        ng.reshape(cs),
        ns.reshape(cs),
        win.T,
        ib.reshape(hs),
        wout,
        ob.reshape(cs),
        ls.reshape(cs),
    )


def solution(mesh):
    both = P(AXES)
    tiles = P(None, "row", "col", None)
    in_specs = (
        tiles, tiles, P(None, None, AXES), both, both, both, P(None, AXES), both, P(AXES, None), both, both,
    )
    out_specs = (
        tiles, P(None, None, AXES), both, both, both, P(None, AXES), both, P(AXES, None), both, both,
    )
    return jax.shard_map(
        functools.partial(per_device, dict(mesh.shape)),
        mesh=mesh, in_specs=in_specs, out_specs=out_specs, check_vma=False,
    )
```

```python
import functools
import math

import jax
import jax.numpy as jnp
from jax import lax
from jax.experimental import pallas as pl
from jax.experimental.pallas import tpu as pltpu
from jax.sharding import PartitionSpec as P

norm_eps = 1e-06
inverse_root_twopi = 0.3989422804014327
half_log2e = 0.7213475204444817
tail_p = 0.275
tail_c = (
    0.1178092510180382,
    0.04211149421929024,
    0.3339322641039753,
    -0.33099338058058636,
    0.45199870802757525,
    -0.11485833206946416,
)
AXES = ("row", "col")
LANES = 128
LEFT = 8
NN = (((1,), (0,)), ((), ()))
NT = (((1,), (1,)), ((), ()))
f32, bf16 = jnp.float32, jnp.bfloat16


def ceil8(n):
    return (n + 7) // 8 * 8


def odd_tiles(n):
    return (n + 7) // 8 // 2 * 16 + 8 if (n + 7) // 8 % 2 == 0 else ceil8(n)


def call(body, outs, scratch=(), flops=0, size=0, limit=8, **more):
    return pl.pallas_call(
        body,
        out_shape=outs,
        scratch_shapes=list(scratch),
        compiler_params=pltpu.CompilerParams(vmem_limit_bytes=limit and limit * 1024 * 1024),
        **more,
        cost_estimate=pl.CostEstimate(flops=flops, bytes_accessed=size, transcendentals=0),
    )


def shape(*dims):
    return jax.ShapeDtypeStruct(dims, f32)


def device_index(mesh_shape):
    return lax.axis_index("row") * mesh_shape["col"] + lax.axis_index("col")


def split(x):
    high = x.astype(bf16)
    return high, (x - high.astype(f32)).astype(bf16)


def dot(a, b, dims):
    return lax.dot_general(a, b, dims, preferred_element_type=f32)


def exchange_order(x, unit, count, me):
    rows = x.shape[0]
    index = lax.broadcasted_iota(jnp.int32, x.shape, 0)
    step = unit
    bit = 1
    while bit < count:
        up = pltpu.roll(x, step, 0)
        down = pltpu.roll(x, rows - step, 0)
        swapped = jnp.where((index & step) != 0, up, down)
        x = jnp.where((me & bit) != 0, swapped, x)
        step *= 2
        bit *= 2
    return x


def pairs(count, second):
    if not second:
        return [(i, i ^ 1) for i in range(count)]
    return [(i, (i + 1 if i % 2 else i - 1) % count) for i in range(count)]


def both_pairs(a, b, axis):
    count = lax.axis_size(axis)
    return lax.ppermute(a, axis, pairs(count, False)), lax.ppermute(b, axis, pairs(count, True))


def even(axis):
    return lax.axis_index(axis) % 2 == 0


def true_neighbour(ms, axis):
    i = lax.axis_index(axis)
    return jnp.where(i % 2 == 0, i > 0, i < ms[axis] - 1)


def start_body(feat, kernel_hbm, cb, ng, ns, ob, ls, win_hbm, ib, wout_hbm, out_ref, row_a, row_b,
               kernel_scr, v0, v1, v2, v3, v4, ib_scr, win_scr, wout_scr, sems):
    batch, rows, cols, C = feat.shape
    taps_i, cs, taps_j = kernel_hbm.shape
    hs = win_hbm.shape[0]
    taps = taps_i * taps_j
    m = taps_i // 2
    even_r = even("row")
    far = jnp.where(even_r, rows - m, 0)
    near = jnp.where(even_r, 0, rows - m)
    vectors = (v0, v1, v2, v3, v4)
    moves = [(kernel_hbm, kernel_scr), (win_hbm, win_scr), (wout_hbm, wout_scr), (ib, ib_scr)]
    moves += list(zip((cb, ng, ns, ob, ls), vectors))
    moves += [(feat.at[:, pl.ds(far, m)], row_a), (feat.at[:, pl.ds(near, m)], row_b)]
    copies = [pltpu.make_async_copy(src, dst, sems.at[n]) for n, (src, dst) in enumerate(moves)]
    for copy in copies:
        copy.start()
    out_ref[...] = jnp.zeros_like(out_ref)
    for copy in copies:
        copy.wait()
    out_ref[0:hs, :] = win_scr[...]
    out_ref[hs : 2 * hs, :] = wout_scr[...]
    base = 2 * hs
    for i in range(taps_i):
        out_ref[base : base + cs, i * taps_j : (i + 1) * taps_j] = kernel_scr[i]
    for n, ref in enumerate(vectors):
        column = jnp.broadcast_to(ref[...], (8, cs)).T
        out_ref[base : base + cs, taps + n : taps + n + 1] = column[:, 0:1]
    out_ref[base + cs : base + cs + 1, 0:hs] = ib_scr[...]


def with_corners(ms, edge_a, edge_b, got_a, got_b, out_a, out_b):
    batch, rows, m, C = edge_a.shape
    cols = got_a.shape[2]
    even_r, even_c = even("row"), even("col")
    out_a[:, m : m + rows, 0:m] = edge_a[...]
    out_b[:, m : m + rows, 0:m] = edge_b[...]
    true_r = true_neighbour(ms, "row")
    for got, end, keep in ((got_a, even_r, None), (got_b, jnp.logical_not(even_r), true_r)):
        at = jnp.where(end, rows + m, 0)
        last, first = got[:, :, cols - m :], got[:, :, 0:m]
        x, y = jnp.where(even_c, last, first), jnp.where(even_c, first, last)
        if keep is not None:
            x, y = jnp.where(keep, x, 0.0), jnp.where(keep, y, 0.0)
        out_a[:, pl.ds(at, m), 0:m] = x
        out_b[:, pl.ds(at, m), 0:m] = y


def first_join_body(ms, inner, got_a, got_b, *refs):
    parts, (slots, out_a, out_b, edge_a, edge_b) = refs[:-5], refs[-5:]
    cols, m = inner.shape[2], got_a.shape[1]
    even_c = even("col")
    first, last = inner[:, :, 0:m], inner[:, :, cols - m :]
    edge_a[...] = jnp.where(even_c, last, first)
    edge_b[...] = jnp.where(even_c, first, last)
    with_corners(ms, edge_a, edge_b, got_a, got_b, out_a, out_b)
    n = 0
    for part in parts:
        slots[n : n + part.shape[0]] = part[...]
        n += part.shape[0]


def message_body(waited, halo, *refs):
    parts, message = refs[:-1], refs[-1]
    n = 0
    for part in parts:
        for k in range(part.shape[0]):
            message[n : n + part.shape[1], :] = part[k]
            n += part.shape[1]
    batch, rows, m, _ = halo.shape
    step = (message.shape[0] - n) // (batch * rows)
    for b in range(batch):
        for r in range(rows):
            message[n : n + m, :] = halo[b, r]
            n += step


def back_join_body(ms, edge_a, edge_b, got_a, got_b, large, large_got, small, small_got, *refs):
    out_a, out_b = refs[-2:]
    rows = large.shape[1]
    n = 0
    for out in refs[:-2]:
        count = out.shape[0]
        out[:, 0:rows] = large[n : n + count] + large_got[n : n + count]
        out[:, rows:] = small[n : n + count] + small_got[n : n + count]
        n += count
    with_corners(ms, edge_a, edge_b, got_a, got_b, out_a, out_b)


def depthwise_block(read, weight, rows, taps_i, taps_j, start):
    acc = start
    for j in range(taps_j):
        w = [weight(i, j) for i in range(taps_i)]
        for r in range(rows + taps_i - 1):
            s = read(r, j)
            for i in range(taps_i):
                p = r - i
                if 0 <= p < rows:
                    term = w[i] * s
                    acc[p] = term if acc[p] is None else acc[p] + term
    return acc


def fill(ms, dst, inner, row_a, row_b, col_a, col_b):
    batch, rows, cols, _ = inner.shape
    m = row_a.shape[1]
    even_r, even_c = even("row"), even("col")
    true_r, true_c = true_neighbour(ms, "row"), true_neighbour(ms, "col")
    at_a = jnp.where(even_r, rows + m, 0)
    at_b = jnp.where(even_r, 0, rows + m)
    for b in range(batch):
        dst[b, m : m + rows, LEFT : LEFT + cols, :] = inner[b]
        dst[b, pl.ds(at_a, m), LEFT : LEFT + cols, :] = row_a[b]
        dst[b, pl.ds(at_b, m), LEFT : LEFT + cols, :] = jnp.where(true_r, row_b[b], 0.0)
        for r in range(rows + 2 * m):
            x, y = col_a(b, r), jnp.where(true_c, col_b[b, r, 0:m], 0.0)
            dst[b, r, LEFT - m : LEFT, :] = jnp.where(even_c, y, x)
            dst[b, r, LEFT + cols : LEFT + cols + m, :] = jnp.where(even_c, x, y)


def small_columns(read, hs, cs, count, me, order, scratch):
    for s in range(count):
        scratch[order[s] * cs : (order[s] + 1) * cs, :] = read(s, 2 * hs, cs)
    return exchange_order(scratch[...], cs, count, me)


def mix_body(
    ms, order, factor, taps_i, taps_j, tile,
    feat, got_ra, got_rb, got_cb, kept, got, cot_ref,
    src_out, dconv_ref, row_a, row_b, edge_a, edge_b, grads_ref, chan_ref, small_ref,
    src_ref, conv_scr, cols_scr, kb_scr, win_scr, wout_scr, w1_scr, w2_scr, w4_scr, bias_scr,
    gw1_scr, gw2_scr, gb_scr, gg_scr, gs_scr, gc_scr, cot_sum,
):
    batch, rows, cols, C = feat.shape
    count = len(order)
    cs = C // count
    taps = taps_i * taps_j
    m = taps_i // 2
    hid = win_scr.shape[0]
    hs = hid // count
    me = device_index(ms)
    half = count // 2
    slot = 2 * hs + 8
    step_rows = (got.shape[0] - half * slot) // (batch * (rows + 2 * m))

    def read(s, first, size):
        at = (s % half) * slot + first
        return (kept if s < half else got)[at : at + size, :]

    def col_a(b, r):
        at = half * slot + (b * (rows + 2 * m) + r) * step_rows
        return got[at : at + m, :]

    fill(ms, src_ref, feat, got_ra, got_rb, col_a, got_cb)
    src_out[...] = src_ref[...]
    columns = small_columns(read, hs, cs, count, me, order, cols_scr)
    cols_scr[...] = columns
    rows_form = columns.T
    small_ref[...] = rows_form
    for t in range(taps):
        kb_scr[t] = jnp.broadcast_to(rows_form[t : t + 1, :], (8, C))
    conv_bias = jnp.broadcast_to(rows_form[taps : taps + 1, :], (8, C))

    for s in range(count):
        win_scr[s * hs : (s + 1) * hs, :] = read(s, 0, hs)
        wout_scr[s * hs : (s + 1) * hs, :] = read(s, hs, hs)
    for s in range(count):
        cols_bias = jnp.broadcast_to(read(s, 2 * hs + cs, 1), (LANES, LANES)).T
        bias_scr[s * hs : (s + 1) * hs, :] = cols_bias[0:hs, :]

    scale_row = rows_form[taps + 4 : taps + 5, :]
    wh, wl = split(win_scr[...])
    w1_scr[:, 0:C] = wh
    w1_scr[:, C : 2 * C] = wl
    w1_scr[:, 2 * C : 3 * C] = wh
    oh, ol = split(wout_scr[...] * scale_row)
    w2_scr[:, 0:C] = oh
    w2_scr[:, C : 2 * C] = ol
    w2_scr[:, 2 * C : 3 * C] = oh
    th, tl = split(win_scr[...].T)
    w4_scr[0:C, :] = th
    w4_scr[C : 2 * C, :] = tl

    def conv_step(b, _):
        for q in range(0, cols, 8):
            acc = depthwise_block(
                lambda r, j: src_ref[b, r, LEFT - m + q + j : LEFT - m + q + j + 8, :],
                lambda i, j: kb_scr[i * taps_j + j],
                rows, taps_i, taps_j, [conv_bias] * rows,
            )
            for p in range(rows):
                conv_scr[b, p, q : q + 8, :] = acc[p]
        return 0

    lax.fori_loop(0, batch, conv_step, 0)

    for ref in (gw1_scr, gw2_scr, gb_scr, gg_scr, gs_scr, gc_scr, cot_sum):
        ref[...] = jnp.zeros_like(ref)
    tile_rows = tile // cols
    per_image = rows // tile_rows
    gain = cols_scr[:, taps + 1 : taps + 2]
    shift = cols_scr[:, taps + 2 : taps + 3]

    def lanes_sum(x):
        total = x[:, 0:LANES]
        for k in range(LANES, x.shape[1], LANES):
            total = total + x[:, k : k + LANES]
        return total

    def step(t, _):
        b = t // per_image
        p0 = (t % per_image) * tile_rows
        x = conv_scr[b, pl.ds(p0, tile_rows)].reshape(tile, C).T
        mean = jnp.mean(x, axis=0, keepdims=True)
        centred = x - mean
        variance = jnp.mean(centred * centred, axis=0, keepdims=True)
        inverse = lax.rsqrt(variance + norm_eps)
        normed = centred * inverse
        lin = normed * gain + shift
        lh, ll = split(lin)
        cot = cot_ref[b, pl.ds(p0, tile_rows)].reshape(tile, C)
        ch, cl = split(cot)
        act = dot(w1_scr[...], jnp.concatenate([lh, lh, ll], axis=0), NN)
        d_hid = dot(w2_scr[...], jnp.concatenate([ch, ch, cl], axis=1), NT)
        bias = bias_scr[...]
        act = act + jnp.concatenate([bias] * (tile // LANES), axis=1)
        e = jnp.exp2((act * act) * (-half_log2e))
        d = 1.0 + tail_p * jnp.abs(act)
        r = pltpu.reciprocal(d, approx=True)
        r = r * (2.0 - d * r)
        q = tail_c[5] * r + tail_c[4]
        for k in (3, 2, 1, 0):
            q = q * r + tail_c[k]
        q = q * r * e
        phi = jnp.where(act > 0, 1.0 - q, q)
        hidden = act * phi
        d_act = d_hid * (phi + act * e * inverse_root_twopi)
        hh, hl = split(hidden)
        dh, dl = split(d_act)
        gb_scr[...] += lanes_sum(d_act)
        both = dot(w4_scr[...], dh, NN)
        d_lin = both[0:C] + both[C : 2 * C] + dot(w4_scr[0:C, :], dl, NN)
        gw1_scr[...] += dot(dh, jnp.concatenate([lh, ll], axis=0), NT)
        gw1_scr[:, 0:C] += dot(dl, lh, NT)
        gw2_scr[...] += dot(hh, jnp.concatenate([ch, cl], axis=1), NN)
        gw2_scr[:, 0:C] += dot(hl, ch, NN)
        gg_scr[...] += lanes_sum(d_lin * normed)
        gs_scr[...] += lanes_sum(d_lin)
        d_norm = d_lin * gain
        d_conv = inverse * (
            d_norm
            - jnp.mean(d_norm, axis=0, keepdims=True)
            - normed * jnp.mean(d_norm * normed, axis=0, keepdims=True)
        )
        gc_scr[...] += lanes_sum(d_conv)
        dconv_ref[b, pl.ds(p0, tile_rows)] = d_conv.T.reshape(tile_rows, cols, C)
        cot_sum[...] += jnp.sum(cot.reshape(tile // 8, 8, C), axis=0)
        return 0

    lax.fori_loop(0, batch * per_image, step, 0)

    even_r, even_c = even("row"), even("col")
    row_a[...] = dconv_ref[:, pl.ds(jnp.where(even_r, rows - m, 0), m)]
    row_b[...] = dconv_ref[:, pl.ds(jnp.where(even_r, 0, rows - m), m)]
    first, last = dconv_ref[:, :, 0:m], dconv_ref[:, :, cols - m : cols]
    edge_a[...] = jnp.where(even_c, last, first)
    edge_b[...] = jnp.where(even_c, first, last)

    h = gw2_scr[:, 0:C] + gw2_scr[:, C : 2 * C]
    gw1 = (gw1_scr[:, 0:C] + gw1_scr[:, C : 2 * C]) * factor
    gw2 = h * (scale_row * factor)
    gb = (jnp.sum(gb_scr[...].T, axis=0, keepdims=True)) * factor
    for s in range(count):
        grads_ref[s, 0:hs, :] = gw1[s * hs : (s + 1) * hs, :]
        grads_ref[s, hs : 2 * hs, :] = gw2[s * hs : (s + 1) * hs, :]
    total = jnp.sum(cot_sum[...], axis=0, keepdims=True)
    outb = rows_form[taps + 3 : taps + 4, :]
    scale_grad = jnp.sum(h * wout_scr[...], axis=0, keepdims=True) + outb * total
    chan_ref[...] = jnp.zeros_like(chan_ref)
    chan_ref[0:1, 0:C] = jnp.sum(gc_scr[...].T, axis=0, keepdims=True) * factor
    chan_ref[1:2, 0:C] = jnp.sum(gg_scr[...].T, axis=0, keepdims=True) * factor
    chan_ref[2:3, 0:C] = jnp.sum(gs_scr[...].T, axis=0, keepdims=True) * factor
    chan_ref[3:4, 0:C] = total * scale_row * factor
    chan_ref[4:5, 0:C] = scale_grad * factor
    chan_ref[5:6, :] = gb


def kernel_grad_body(ms, order, factor, taps_i, taps_j, count, src_in, dconv_in, chan_ref, out_ref, src_ref, dconv_ref, acc_scr, rows_scr):
    batch, rows, cols, C = dconv_in.shape
    m = taps_i // 2
    taps = taps_i * taps_j
    cs = C // count
    me = device_index(ms)
    src_ref[...] = src_in[...]
    dconv_ref[:, :, 0:cols, :] = dconv_in[...]
    acc_scr[...] = jnp.zeros_like(acc_scr)

    def step(b, _):
        for j in range(taps_j):
            acc = [acc_scr[i * taps_j + j] for i in range(taps_i)]
            for q in range(0, cols, 8):
                d = [dconv_ref[b, p, q : q + 8, :] for p in range(rows)]
                for r in range(rows + taps_i - 1):
                    s = src_ref[b, r, LEFT - m + q + j : LEFT - m + q + j + 8, :]
                    for i in range(taps_i):
                        p = r - i
                        if 0 <= p < rows:
                            acc[i] = acc[i] + d[p] * s
            for i in range(taps_i):
                acc_scr[i * taps_j + j] = acc[i]
        return 0

    lax.fori_loop(0, batch, step, 0)
    rows_scr[...] = jnp.zeros_like(rows_scr)
    for t in range(taps):
        rows_scr[t : t + 1, :] = jnp.sum(acc_scr[t], axis=0, keepdims=True) * factor
    rows_scr[taps : taps + 5, :] = chan_ref[0:5, 0:C]
    columns = exchange_order(rows_scr[...].T, cs, count, me)
    out_ref[...] = jnp.zeros_like(out_ref)
    hs = chan_ref.shape[1] // count
    for s in range(count):
        out_ref[s, 0:cs, :] = columns[order[s] * cs : (order[s] + 1) * cs, :]
        out_ref[s, cs : cs + 1, 0:hs] = chan_ref[5:6, s * hs : (s + 1) * hs]


def features_grad_body(ms, taps_i, taps_j, inner, got_ra, got_rb, got_ca, got_cb, small_ref, cot_ref, out_ref, ext_scr, kb_scr):
    batch, rows, cols, C = inner.shape
    m = taps_i // 2
    taps = taps_i * taps_j
    fill(ms, ext_scr, inner, got_ra, got_rb, lambda b, r: got_ca[b, r, 0 : taps_i // 2], got_cb)
    for t in range(taps):
        kb_scr[t] = jnp.broadcast_to(small_ref[t : t + 1, :], (8, C))

    def step(b, _):
        for q in range(0, cols, 8):
            acc = depthwise_block(
                lambda r, j: ext_scr[b, r, LEFT - m + q + j : LEFT - m + q + j + 8, :],
                lambda i, j: kb_scr[taps - 1 - (i * taps_j + j)],
                rows, taps_i, taps_j, [cot_ref[b, p, q : q + 8, :] for p in range(rows)],
            )
            for p in range(rows):
                out_ref[b, p, q : q + 8, :] = acc[p]
        return 0

    lax.fori_loop(0, batch, step, 0)


def finish_body(taps_i, taps_j, cs, hs, *refs):
    parts, outs = refs[:-9], refs[-9:]
    total = parts[0][...]
    for part in parts[1:]:
        total = total + part[...]
    kernel_out, cb, ng, ns, win_out, ib, wout_out, ob, ls = outs
    taps = taps_i * taps_j
    win_out[...] = total[0:hs, :]
    wout_out[...] = total[hs : 2 * hs, :]
    small = total[2 * hs : 2 * hs + 8, :]
    for i in range(taps_i):
        kernel_out[i] = small[0:cs, i * taps_j : (i + 1) * taps_j]
    flipped = small.T
    for n, ref in enumerate((cb, ng, ns, ob, ls)):
        ref[...] = flipped[taps + n : taps + n + 1, 0:cs]
    ib[...] = small[cs : cs + 1, 0:hs]


def flip(x, mask, count):
    return lax.ppermute(x, AXES, [(i, i ^ mask) for i in range(count)])


def groups_of(ms):
    bits_col = ms["col"].bit_length() - 1
    bits_row = ms["row"].bit_length() - 1
    col = [1 << k for k in range(bits_col)]
    row = [1 << (k + bits_col) for k in range(bits_row)]
    rest = col[1:]
    out = [rest[k : k + 2] for k in range(0, len(rest), 2)]
    out += [row[k : k + 2] for k in range(0, len(row), 2)]
    return out + [col[:1]]


def masks(group):
    out = [0]
    for bit in group:
        out += [bit ^ x for x in out]
    return out


def per_device(ms, features, cotangent, conv_kernel, conv_bias, norm_gain, norm_shift, w_in, in_bias, w_out, out_bias, layer_scale):
    batch, rows, cols, C = features.shape
    taps_i, taps_j, cs = conv_kernel.shape
    hs = w_out.shape[0]
    count = ms["row"] * ms["col"]
    hid = hs * count
    m = taps_i // 2
    taps = taps_i * taps_j
    cells = batch * rows * cols * count
    factor = 1.0 / math.sqrt(cells)
    slot = 2 * hs + 8
    wide = odd_tiles(LEFT + cols + m)

    vm = pltpu.VMEM
    vectors = [v.reshape(1, cs) for v in (conv_bias, norm_gain, norm_shift, out_bias, layer_scale)]
    block, row_a, row_b = call(
        start_body,
        (
            shape(slot, LANES),
            *(shape(batch, m, cols, C) for _ in range(2)),
        ),
        scratch=(
            vm((taps_i, cs, taps_j), f32),
            *(vm((1, cs), f32) for _ in range(5)),
            vm((1, hs), f32),
            vm((hs, C), f32),
            vm((hs, C), f32),
            pltpu.SemaphoreType.DMA((11,)),
        ),
        size=10**6,
        limit=None,
        in_specs=[pl.BlockSpec(memory_space=pl.ANY)] * 10,
    )(features, conv_kernel.transpose(0, 2, 1), *vectors, w_in.T, in_bias.reshape(1, hs), w_out)

    wide_m = (m + 3) // 4 * 4
    edges = (shape(batch, rows + 2 * m, m, C), shape(batch, rows + 2 * m, wide_m, C))
    anywhere, in_vmem = pl.BlockSpec(memory_space=pl.ANY), pl.BlockSpec(memory_space=pltpu.VMEM)
    groups = groups_of(ms)
    order = [0]
    got_ra, got_rb = both_pairs(row_a, row_b, "row")
    parts = [block[None]]
    for n, group in enumerate(groups[:-1]):
        if n == 1:
            slots, edge_a, edge_b = call(
                functools.partial(first_join_body, ms),
                (shape(len(order), slot, LANES), *edges),
                scratch=[vm((batch, rows, m, C), f32) for _ in range(2)],
            )(features, got_ra, got_rb, *parts)
            got_cb = lax.ppermute(edge_b, "col", pairs(ms["col"], True))
        else:
            slots = jnp.concatenate(parts)
        parts = [slots] + [flip(slots, mask, count) for mask in masks(group)[1:]]
        order = [mask ^ x for mask in masks(group) for x in order]
    half = count // 2
    message = call(
        message_body,
        shape(half * slot + edges[0].shape[0] * edges[0].shape[1] * wide_m, LANES),
        in_specs=[anywhere] + [in_vmem] * (1 + len(parts)),
    )(got_cb, edge_a, *parts)
    last = groups[-1][0]
    order += [last ^ x for x in order]
    got = flip(message, last, count)
    tile = 8 * cols
    src, dconv, d_row_a, d_row_b, d_edge_a, d_edge_b, grads, chan, small = call(
        functools.partial(mix_body, ms, order, factor, taps_i, taps_j, tile),
        (
            shape(batch, rows + 2 * m, wide, C),
            shape(batch, rows, cols, C),
            *(shape(batch, m, cols, C) for _ in range(2)),
            *(shape(batch, rows, m, C) for _ in range(2)),
            shape(count, 2 * hs, C),
            shape(8, hid),
            shape(LANES, C),
        ),
        scratch=(
            vm((batch, rows + 2 * m, wide, C), f32),
            vm((batch, rows, cols, C), f32),
            vm((C, LANES), f32),
            vm((taps, 8, C), f32),
            vm((hid, C), f32),
            vm((hid, C), f32),
            vm((hid, 3 * C), bf16),
            vm((hid, 3 * C), bf16),
            vm((2 * C, hid), bf16),
            vm((hid, LANES), f32),
            vm((hid, 2 * C), f32),
            vm((hid, 2 * C), f32),
            vm((hid, LANES), f32),
            vm((C, LANES), f32),
            vm((C, LANES), f32),
            vm((C, LANES), f32),
            vm((8, C), f32),
        ),
        flops=12 * 10**9,
        size=8 * 10**6,
        limit=24,
    )(features, got_ra, got_rb, got_cb, message, got, cotangent)

    d_got_ra, d_got_rb = both_pairs(d_row_a, d_row_b, "row")
    large_got = flip(grads[half:], last, count)
    smalls = call(
        functools.partial(kernel_grad_body, ms, order, factor, taps_i, taps_j, count),
        shape(count, 8, LANES),
        scratch=(
            vm((batch, rows + 2 * m, wide, C), f32),
            vm((batch, rows, odd_tiles(cols), C), f32),
            vm((taps, 8, C), f32),
            vm((LANES, C), f32),
        ),
        flops=4 * 10**9,
        size=4 * 10**6,
    )(src, dconv, chan)
    small_got = flip(smalls[half:], last, count)
    ways = len(masks(groups[-2]))
    *parts, edge_a, edge_b = call(
        functools.partial(back_join_body, ms),
        (*(shape(half // ways, slot, LANES) for _ in range(ways)), edges[1], edges[1]),
    )(d_edge_a, d_edge_b, d_got_ra, d_got_rb, grads, large_got, smalls, small_got)
    d_got_ca, d_got_cb = both_pairs(edge_a, edge_b, "col")
    for n, group in reversed(list(enumerate(groups[:-1]))):
        parts = [parts[0]] + [flip(part, mask, count) for part, mask in zip(parts[1:], masks(group)[1:])]
        if n:
            whole = parts[0]
            for part in parts[1:]:
                whole = whole + part
            ways = len(masks(groups[n - 1]))
            step = whole.shape[0] // ways
            parts = [whole[k * step : (k + 1) * step] for k in range(ways)]

    features_grad = call(
        functools.partial(features_grad_body, ms, taps_i, taps_j),
        shape(batch, rows, cols, C),
        scratch=(
            vm((batch, rows + 2 * m, wide, C), f32),
            vm((taps, 8, C), f32),
        ),
        flops=4 * 10**9,
        size=4 * 10**6,
    )(dconv, d_got_ra, d_got_rb, d_got_ca, d_got_cb, small, cotangent)

    outs = call(
        functools.partial(finish_body, taps_i, taps_j, cs, hs),
        (
            shape(taps_i, cs, taps_j),
            *(shape(1, cs) for _ in range(3)),
            shape(hs, C),
            shape(1, hs),
            shape(hs, C),
            *(shape(1, cs) for _ in range(2)),
        ),
        size=100000,
    )(*(p.reshape(slot, LANES) for p in parts))
    kernel_grad, cb, ng, ns, win, ib, wout, ob, ls = outs
    return (
        features_grad,
        kernel_grad.transpose(0, 2, 1),
        cb.reshape(cs),
        ng.reshape(cs),
        ns.reshape(cs),
        win.T,
        ib.reshape(hs),
        wout,
        ob.reshape(cs),
        ls.reshape(cs),
    )


def solution(mesh):
    both = P(AXES)
    tiles = P(None, "row", "col", None)
    in_specs = (
        tiles, tiles, P(None, None, AXES), both, both, both, P(None, AXES), both, P(AXES, None), both, both,
    )
    out_specs = (
        tiles, P(None, None, AXES), both, both, both, P(None, AXES), both, P(AXES, None), both, both,
    )
    return jax.shard_map(
        functools.partial(per_device, dict(mesh.shape)),
        mesh=mesh, in_specs=in_specs, out_specs=out_specs, check_vma=False,
    )
```

```python
import functools
import math

import jax
import jax.numpy as jnp
from jax import lax
from jax.experimental import pallas as pl
from jax.experimental.pallas import tpu as pltpu
from jax.sharding import PartitionSpec as P

norm_eps = 1e-06
inverse_root_twopi = 0.3989422804014327
half_log2e = 0.7213475204444817
tail_p = 0.275
tail_c = (
    0.1178092510180382,
    0.04211149421929024,
    0.3339322641039753,
    -0.33099338058058636,
    0.45199870802757525,
    -0.11485833206946416,
)
AXES = ("row", "col")
LANES = 128
LEFT = 8
NN = (((1,), (0,)), ((), ()))
NT = (((1,), (1,)), ((), ()))
f32, bf16 = jnp.float32, jnp.bfloat16


def ceil8(n):
    return (n + 7) // 8 * 8


def call(body, outs, scratch=(), flops=0, size=0, limit=8, **more):
    return pl.pallas_call(
        body,
        out_shape=outs,
        scratch_shapes=list(scratch),
        compiler_params=pltpu.CompilerParams(vmem_limit_bytes=limit and limit * 1024 * 1024),
        **more,
        cost_estimate=pl.CostEstimate(flops=flops, bytes_accessed=size, transcendentals=0),
    )


def shape(*dims):
    return jax.ShapeDtypeStruct(dims, f32)


def device_index(mesh_shape):
    return lax.axis_index("row") * mesh_shape["col"] + lax.axis_index("col")


def split(x):
    high = x.astype(bf16)
    return high, (x - high.astype(f32)).astype(bf16)


def dot(a, b, dims):
    return lax.dot_general(a, b, dims, preferred_element_type=f32)


def exchange_order(x, unit, count, me):
    rows = x.shape[0]
    index = lax.broadcasted_iota(jnp.int32, x.shape, 0)
    step = unit
    bit = 1
    while bit < count:
        up = pltpu.roll(x, step, 0)
        down = pltpu.roll(x, rows - step, 0)
        swapped = jnp.where((index & step) != 0, up, down)
        x = jnp.where((me & bit) != 0, swapped, x)
        step *= 2
        bit *= 2
    return x


def pairs(count, second):
    if not second:
        return [(i, i ^ 1) for i in range(count)]
    return [(i, (i + 1 if i % 2 else i - 1) % count) for i in range(count)]


def both_pairs(a, b, axis):
    count = lax.axis_size(axis)
    return lax.ppermute(a, axis, pairs(count, False)), lax.ppermute(b, axis, pairs(count, True))


def even(axis):
    return lax.axis_index(axis) % 2 == 0


def true_neighbour(ms, axis):
    i = lax.axis_index(axis)
    return jnp.where(i % 2 == 0, i > 0, i < ms[axis] - 1)


def start_body(feat, kernel_hbm, cb, ng, ns, ob, ls, win_hbm, ib, wout_hbm, out_ref, row_a, row_b,
               kernel_scr, v0, v1, v2, v3, v4, ib_scr, win_scr, wout_scr, sems):
    batch, rows, cols, C = feat.shape
    taps_i, cs, taps_j = kernel_hbm.shape
    hs = win_hbm.shape[0]
    taps = taps_i * taps_j
    m = taps_i // 2
    even_r = even("row")
    far = jnp.where(even_r, rows - m, 0)
    near = jnp.where(even_r, 0, rows - m)
    vectors = (v0, v1, v2, v3, v4)
    moves = [(kernel_hbm, kernel_scr), (win_hbm, win_scr), (wout_hbm, wout_scr), (ib, ib_scr)]
    moves += list(zip((cb, ng, ns, ob, ls), vectors))
    moves += [(feat.at[:, pl.ds(far, m)], row_a), (feat.at[:, pl.ds(near, m)], row_b)]
    copies = [pltpu.make_async_copy(src, dst, sems.at[n]) for n, (src, dst) in enumerate(moves)]
    for copy in copies:
        copy.start()
    out_ref[...] = jnp.zeros_like(out_ref)
    for copy in copies:
        copy.wait()
    out_ref[0:hs, :] = win_scr[...]
    out_ref[hs : 2 * hs, :] = wout_scr[...]
    base = 2 * hs
    for i in range(taps_i):
        out_ref[base : base + cs, i * taps_j : (i + 1) * taps_j] = kernel_scr[i]
    for n, ref in enumerate(vectors):
        column = jnp.broadcast_to(ref[...], (8, cs)).T
        out_ref[base : base + cs, taps + n : taps + n + 1] = column[:, 0:1]
    out_ref[base + cs : base + cs + 1, 0:hs] = ib_scr[...]


def with_corners(ms, edge_a, edge_b, got_a, got_b, out_a, out_b):
    batch, rows, m, C = edge_a.shape
    cols = got_a.shape[2]
    even_r, even_c = even("row"), even("col")
    out_a[:, m : m + rows, 0:m] = edge_a[...]
    out_b[:, m : m + rows, 0:m] = edge_b[...]
    true_r = true_neighbour(ms, "row")
    for got, end, keep in ((got_a, even_r, None), (got_b, jnp.logical_not(even_r), true_r)):
        at = jnp.where(end, rows + m, 0)
        last, first = got[:, :, cols - m :], got[:, :, 0:m]
        x, y = jnp.where(even_c, last, first), jnp.where(even_c, first, last)
        if keep is not None:
            x, y = jnp.where(keep, x, 0.0), jnp.where(keep, y, 0.0)
        out_a[:, pl.ds(at, m), 0:m] = x
        out_b[:, pl.ds(at, m), 0:m] = y


def first_join_body(ms, inner, got_a, got_b, *refs):
    parts, (slots, out_a, out_b, edge_a, edge_b) = refs[:-5], refs[-5:]
    cols, m = inner.shape[2], got_a.shape[1]
    even_c = even("col")
    first, last = inner[:, :, 0:m], inner[:, :, cols - m :]
    edge_a[...] = jnp.where(even_c, last, first)
    edge_b[...] = jnp.where(even_c, first, last)
    with_corners(ms, edge_a, edge_b, got_a, got_b, out_a, out_b)
    n = 0
    for part in parts:
        slots[n : n + part.shape[0]] = part[...]
        n += part.shape[0]


def message_body(waited, halo, *refs):
    parts, message = refs[:-1], refs[-1]
    n = 0
    for part in parts:
        for k in range(part.shape[0]):
            message[n : n + part.shape[1], :] = part[k]
            n += part.shape[1]
    batch, rows, m, _ = halo.shape
    step = (message.shape[0] - n) // (batch * rows)
    for b in range(batch):
        for r in range(rows):
            message[n : n + m, :] = halo[b, r]
            n += step


def back_join_body(ms, edge_a, edge_b, got_a, got_b, large, large_got, small, small_got, *refs):
    out_a, out_b = refs[-2:]
    rows = large.shape[1]
    n = 0
    for out in refs[:-2]:
        count = out.shape[0]
        out[:, 0:rows] = large[n : n + count] + large_got[n : n + count]
        out[:, rows:] = small[n : n + count] + small_got[n : n + count]
        n += count
    with_corners(ms, edge_a, edge_b, got_a, got_b, out_a, out_b)


def depthwise_block(read, weight, rows, taps_i, taps_j, start):
    acc = start
    for j in range(taps_j):
        w = [weight(i, j) for i in range(taps_i)]
        for r in range(rows + taps_i - 1):
            s = read(r, j)
            for i in range(taps_i):
                p = r - i
                if 0 <= p < rows:
                    term = w[i] * s
                    acc[p] = term if acc[p] is None else acc[p] + term
    return acc


def fill(ms, dst, inner, row_a, row_b, col_a, col_b):
    batch, rows, cols, _ = inner.shape
    m = row_a.shape[1]
    even_r, even_c = even("row"), even("col")
    true_r, true_c = true_neighbour(ms, "row"), true_neighbour(ms, "col")
    at_a = jnp.where(even_r, rows + m, 0)
    at_b = jnp.where(even_r, 0, rows + m)
    for b in range(batch):
        dst[b, m : m + rows, LEFT : LEFT + cols, :] = inner[b]
        dst[b, pl.ds(at_a, m), LEFT : LEFT + cols, :] = row_a[b]
        dst[b, pl.ds(at_b, m), LEFT : LEFT + cols, :] = jnp.where(true_r, row_b[b], 0.0)
        for r in range(rows + 2 * m):
            x, y = col_a(b, r), jnp.where(true_c, col_b[b, r, 0:m], 0.0)
            dst[b, r, LEFT - m : LEFT, :] = jnp.where(even_c, y, x)
            dst[b, r, LEFT + cols : LEFT + cols + m, :] = jnp.where(even_c, x, y)


def small_columns(read, hs, cs, count, me, order, scratch):
    for s in range(count):
        scratch[order[s] * cs : (order[s] + 1) * cs, :] = read(s, 2 * hs, cs)
    return exchange_order(scratch[...], cs, count, me)


def mix_body(
    ms, order, factor, taps_i, taps_j, tile,
    feat, got_ra, got_rb, got_cb, kept, got, cot_ref,
    src_out, dconv_ref, row_a, row_b, edge_a, edge_b, grads_ref, chan_ref, small_ref,
    src_ref, conv_scr, cols_scr, kb_scr, win_scr, wout_scr, w1_scr, w2_scr, w4_scr, bias_scr,
    gw1_scr, gw2_scr, gb_scr, gg_scr, gs_scr, gc_scr, cot_sum,
):
    batch, rows, cols, C = feat.shape
    count = len(order)
    cs = C // count
    taps = taps_i * taps_j
    m = taps_i // 2
    hid = win_scr.shape[0]
    hs = hid // count
    me = device_index(ms)
    half = count // 2
    slot = 2 * hs + 8
    step_rows = (got.shape[0] - half * slot) // (batch * (rows + 2 * m))

    def read(s, first, size):
        at = (s % half) * slot + first
        return (kept if s < half else got)[at : at + size, :]

    def col_a(b, r):
        at = half * slot + (b * (rows + 2 * m) + r) * step_rows
        return got[at : at + m, :]

    fill(ms, src_ref, feat, got_ra, got_rb, col_a, got_cb)
    src_out[...] = src_ref[...]
    columns = small_columns(read, hs, cs, count, me, order, cols_scr)
    cols_scr[...] = columns
    rows_form = columns.T
    small_ref[...] = rows_form
    for t in range(taps):
        kb_scr[t] = jnp.broadcast_to(rows_form[t : t + 1, :], (8, C))
    conv_bias = jnp.broadcast_to(rows_form[taps : taps + 1, :], (8, C))

    for s in range(count):
        win_scr[s * hs : (s + 1) * hs, :] = read(s, 0, hs)
        wout_scr[s * hs : (s + 1) * hs, :] = read(s, hs, hs)
    for s in range(count):
        cols_bias = jnp.broadcast_to(read(s, 2 * hs + cs, 1), (LANES, LANES)).T
        bias_scr[s * hs : (s + 1) * hs, :] = cols_bias[0:hs, :]

    scale_row = rows_form[taps + 4 : taps + 5, :]
    wh, wl = split(win_scr[...])
    w1_scr[:, 0:C] = wh
    w1_scr[:, C : 2 * C] = wl
    w1_scr[:, 2 * C : 3 * C] = wh
    oh, ol = split(wout_scr[...] * scale_row)
    w2_scr[:, 0:C] = oh
    w2_scr[:, C : 2 * C] = ol
    w2_scr[:, 2 * C : 3 * C] = oh
    th, tl = split(win_scr[...].T)
    w4_scr[0:C, :] = th
    w4_scr[C : 2 * C, :] = tl

    def conv_step(b, _):
        for q in range(0, cols, 8):
            acc = depthwise_block(
                lambda r, j: src_ref[b, r, LEFT - m + q + j : LEFT - m + q + j + 8, :],
                lambda i, j: kb_scr[i * taps_j + j],
                rows, taps_i, taps_j, [conv_bias] * rows,
            )
            for p in range(rows):
                conv_scr[b, p, q : q + 8, :] = acc[p]
        return 0

    lax.fori_loop(0, batch, conv_step, 0)

    for ref in (gw1_scr, gw2_scr, gb_scr, gg_scr, gs_scr, gc_scr, cot_sum):
        ref[...] = jnp.zeros_like(ref)
    tile_rows = tile // cols
    per_image = rows // tile_rows
    gain = cols_scr[:, taps + 1 : taps + 2]
    shift = cols_scr[:, taps + 2 : taps + 3]

    def lanes_sum(x):
        total = x[:, 0:LANES]
        for k in range(LANES, x.shape[1], LANES):
            total = total + x[:, k : k + LANES]
        return total

    def step(t, _):
        b = t // per_image
        p0 = (t % per_image) * tile_rows
        x = conv_scr[b, pl.ds(p0, tile_rows)].reshape(tile, C).T
        mean = jnp.mean(x, axis=0, keepdims=True)
        centred = x - mean
        variance = jnp.mean(centred * centred, axis=0, keepdims=True)
        inverse = lax.rsqrt(variance + norm_eps)
        normed = centred * inverse
        lin = normed * gain + shift
        lh, ll = split(lin)
        cot = cot_ref[b, pl.ds(p0, tile_rows)].reshape(tile, C)
        ch, cl = split(cot)
        act = dot(w1_scr[...], jnp.concatenate([lh, lh, ll], axis=0), NN)
        d_hid = dot(w2_scr[...], jnp.concatenate([ch, ch, cl], axis=1), NT)
        bias = bias_scr[...]
        act = act + jnp.concatenate([bias] * (tile // LANES), axis=1)
        e = jnp.exp2((act * act) * (-half_log2e))
        d = 1.0 + tail_p * jnp.abs(act)
        r = pltpu.reciprocal(d, approx=True)
        r = r * (2.0 - d * r)
        q = tail_c[5] * r + tail_c[4]
        for k in (3, 2, 1, 0):
            q = q * r + tail_c[k]
        q = q * r * e
        phi = jnp.where(act > 0, 1.0 - q, q)
        hidden = act * phi
        d_act = d_hid * (phi + act * e * inverse_root_twopi)
        hh, hl = split(hidden)
        dh, dl = split(d_act)
        gb_scr[...] += lanes_sum(d_act)
        both = dot(w4_scr[...], dh, NN)
        d_lin = both[0:C] + both[C : 2 * C] + dot(w4_scr[0:C, :], dl, NN)
        gw1_scr[...] += dot(dh, jnp.concatenate([lh, ll], axis=0), NT)
        gw1_scr[:, 0:C] += dot(dl, lh, NT)
        gw2_scr[...] += dot(hh, jnp.concatenate([ch, cl], axis=1), NN)
        gw2_scr[:, 0:C] += dot(hl, ch, NN)
        gg_scr[...] += lanes_sum(d_lin * normed)
        gs_scr[...] += lanes_sum(d_lin)
        d_norm = d_lin * gain
        d_conv = inverse * (
            d_norm
            - jnp.mean(d_norm, axis=0, keepdims=True)
            - normed * jnp.mean(d_norm * normed, axis=0, keepdims=True)
        )
        gc_scr[...] += lanes_sum(d_conv)
        dconv_ref[b, pl.ds(p0, tile_rows)] = d_conv.T.reshape(tile_rows, cols, C)
        cot_sum[...] += jnp.sum(cot.reshape(tile // 8, 8, C), axis=0)
        return 0

    lax.fori_loop(0, batch * per_image, step, 0)

    even_r, even_c = even("row"), even("col")
    row_a[...] = dconv_ref[:, pl.ds(jnp.where(even_r, rows - m, 0), m)]
    row_b[...] = dconv_ref[:, pl.ds(jnp.where(even_r, 0, rows - m), m)]
    first, last = dconv_ref[:, :, 0:m], dconv_ref[:, :, cols - m : cols]
    edge_a[...] = jnp.where(even_c, last, first)
    edge_b[...] = jnp.where(even_c, first, last)

    h = gw2_scr[:, 0:C] + gw2_scr[:, C : 2 * C]
    gw1 = (gw1_scr[:, 0:C] + gw1_scr[:, C : 2 * C]) * factor
    gw2 = h * (scale_row * factor)
    gb = (jnp.sum(gb_scr[...].T, axis=0, keepdims=True)) * factor
    for s in range(count):
        grads_ref[s, 0:hs, :] = gw1[s * hs : (s + 1) * hs, :]
        grads_ref[s, hs : 2 * hs, :] = gw2[s * hs : (s + 1) * hs, :]
    total = jnp.sum(cot_sum[...], axis=0, keepdims=True)
    outb = rows_form[taps + 3 : taps + 4, :]
    scale_grad = jnp.sum(h * wout_scr[...], axis=0, keepdims=True) + outb * total
    chan_ref[...] = jnp.zeros_like(chan_ref)
    chan_ref[0:1, 0:C] = jnp.sum(gc_scr[...].T, axis=0, keepdims=True) * factor
    chan_ref[1:2, 0:C] = jnp.sum(gg_scr[...].T, axis=0, keepdims=True) * factor
    chan_ref[2:3, 0:C] = jnp.sum(gs_scr[...].T, axis=0, keepdims=True) * factor
    chan_ref[3:4, 0:C] = total * scale_row * factor
    chan_ref[4:5, 0:C] = scale_grad * factor
    chan_ref[5:6, :] = gb


def kernel_grad_body(ms, order, factor, taps_i, taps_j, count, src_in, dconv_in, chan_ref, out_ref, src_ref, dconv_ref, acc_scr, rows_scr):
    batch, rows, cols, C = dconv_in.shape
    m = taps_i // 2
    taps = taps_i * taps_j
    cs = C // count
    me = device_index(ms)
    src_ref[...] = src_in[...]
    dconv_ref[:, :, 0:cols, :] = dconv_in[...]
    acc_scr[...] = jnp.zeros_like(acc_scr)

    def step(b, _):
        for j in range(taps_j):
            acc = [acc_scr[i * taps_j + j] for i in range(taps_i)]
            for q in range(0, cols, 8):
                d = [dconv_ref[b, p, q : q + 8, :] for p in range(rows)]
                for r in range(rows + taps_i - 1):
                    s = src_ref[b, r, LEFT - m + q + j : LEFT - m + q + j + 8, :]
                    for i in range(taps_i):
                        p = r - i
                        if 0 <= p < rows:
                            acc[i] = acc[i] + d[p] * s
            for i in range(taps_i):
                acc_scr[i * taps_j + j] = acc[i]
        return 0

    lax.fori_loop(0, batch, step, 0)
    rows_scr[...] = jnp.zeros_like(rows_scr)
    for t in range(taps):
        rows_scr[t : t + 1, :] = jnp.sum(acc_scr[t], axis=0, keepdims=True) * factor
    rows_scr[taps : taps + 5, :] = chan_ref[0:5, 0:C]
    columns = exchange_order(rows_scr[...].T, cs, count, me)
    out_ref[...] = jnp.zeros_like(out_ref)
    hs = chan_ref.shape[1] // count
    for s in range(count):
        out_ref[s, 0:cs, :] = columns[order[s] * cs : (order[s] + 1) * cs, :]
        out_ref[s, cs : cs + 1, 0:hs] = chan_ref[5:6, s * hs : (s + 1) * hs]


def features_grad_body(ms, taps_i, taps_j, inner, got_ra, got_rb, got_ca, got_cb, small_ref, cot_ref, out_ref, ext_scr, kb_scr):
    batch, rows, cols, C = inner.shape
    m = taps_i // 2
    taps = taps_i * taps_j
    fill(ms, ext_scr, inner, got_ra, got_rb, lambda b, r: got_ca[b, r, 0 : taps_i // 2], got_cb)
    for t in range(taps):
        kb_scr[t] = jnp.broadcast_to(small_ref[t : t + 1, :], (8, C))

    def step(b, _):
        for q in range(0, cols, 8):
            acc = depthwise_block(
                lambda r, j: ext_scr[b, r, LEFT - m + q + j : LEFT - m + q + j + 8, :],
                lambda i, j: kb_scr[taps - 1 - (i * taps_j + j)],
                rows, taps_i, taps_j, [cot_ref[b, p, q : q + 8, :] for p in range(rows)],
            )
            for p in range(rows):
                out_ref[b, p, q : q + 8, :] = acc[p]
        return 0

    lax.fori_loop(0, batch, step, 0)


def finish_body(taps_i, taps_j, cs, hs, *refs):
    parts, outs = refs[:-9], refs[-9:]
    total = parts[0][...]
    for part in parts[1:]:
        total = total + part[...]
    kernel_out, cb, ng, ns, win_out, ib, wout_out, ob, ls = outs
    taps = taps_i * taps_j
    win_out[...] = total[0:hs, :]
    wout_out[...] = total[hs : 2 * hs, :]
    small = total[2 * hs : 2 * hs + 8, :]
    for i in range(taps_i):
        kernel_out[i] = small[0:cs, i * taps_j : (i + 1) * taps_j]
    flipped = small.T
    for n, ref in enumerate((cb, ng, ns, ob, ls)):
        ref[...] = flipped[taps + n : taps + n + 1, 0:cs]
    ib[...] = small[cs : cs + 1, 0:hs]


def flip(x, mask, count):
    return lax.ppermute(x, AXES, [(i, i ^ mask) for i in range(count)])


def groups_of(ms):
    bits_col = ms["col"].bit_length() - 1
    bits_row = ms["row"].bit_length() - 1
    col = [1 << k for k in range(bits_col)]
    row = [1 << (k + bits_col) for k in range(bits_row)]
    rest = col[1:]
    out = [rest[k : k + 2] for k in range(0, len(rest), 2)]
    out += [row[k : k + 2] for k in range(0, len(row), 2)]
    return out + [col[:1]]


def masks(group):
    out = [0]
    for bit in group:
        out += [bit ^ x for x in out]
    return out


def per_device(ms, features, cotangent, conv_kernel, conv_bias, norm_gain, norm_shift, w_in, in_bias, w_out, out_bias, layer_scale):
    batch, rows, cols, C = features.shape
    taps_i, taps_j, cs = conv_kernel.shape
    hs = w_out.shape[0]
    count = ms["row"] * ms["col"]
    hid = hs * count
    m = taps_i // 2
    taps = taps_i * taps_j
    cells = batch * rows * cols * count
    factor = 1.0 / math.sqrt(cells)
    slot = 2 * hs + 8
    wide = ceil8(LEFT + cols + m)

    vm = pltpu.VMEM
    vectors = [v.reshape(1, cs) for v in (conv_bias, norm_gain, norm_shift, out_bias, layer_scale)]
    block, row_a, row_b = call(
        start_body,
        (
            shape(slot, LANES),
            *(shape(batch, m, cols, C) for _ in range(2)),
        ),
        scratch=(
            vm((taps_i, cs, taps_j), f32),
            *(vm((1, cs), f32) for _ in range(5)),
            vm((1, hs), f32),
            vm((hs, C), f32),
            vm((hs, C), f32),
            pltpu.SemaphoreType.DMA((11,)),
        ),
        size=10**6,
        limit=None,
        in_specs=[pl.BlockSpec(memory_space=pl.ANY)] * 10,
    )(features, conv_kernel.transpose(0, 2, 1), *vectors, w_in.T, in_bias.reshape(1, hs), w_out)

    wide_m = (m + 3) // 4 * 4
    edges = (shape(batch, rows + 2 * m, m, C), shape(batch, rows + 2 * m, wide_m, C))
    anywhere, in_vmem = pl.BlockSpec(memory_space=pl.ANY), pl.BlockSpec(memory_space=pltpu.VMEM)
    groups = groups_of(ms)
    order = [0]
    got_ra, got_rb = both_pairs(row_a, row_b, "row")
    parts = [block[None]]
    for n, group in enumerate(groups[:-1]):
        if n == 1:
            slots, edge_a, edge_b = call(
                functools.partial(first_join_body, ms),
                (shape(len(order), slot, LANES), *edges),
                scratch=[vm((batch, rows, m, C), f32) for _ in range(2)],
            )(features, got_ra, got_rb, *parts)
            got_cb = lax.ppermute(edge_b, "col", pairs(ms["col"], True))
        else:
            slots = jnp.concatenate(parts)
        parts = [slots] + [flip(slots, mask, count) for mask in masks(group)[1:]]
        order = [mask ^ x for mask in masks(group) for x in order]
    half = count // 2
    message = call(
        message_body,
        shape(half * slot + edges[0].shape[0] * edges[0].shape[1] * wide_m, LANES),
        in_specs=[anywhere] + [in_vmem] * (1 + len(parts)),
    )(got_cb, edge_a, *parts)
    last = groups[-1][0]
    order += [last ^ x for x in order]
    got = flip(message, last, count)
    tile = rows * cols
    src, dconv, d_row_a, d_row_b, d_edge_a, d_edge_b, grads, chan, small = call(
        functools.partial(mix_body, ms, order, factor, taps_i, taps_j, tile),
        (
            shape(batch, rows + 2 * m, wide, C),
            shape(batch, rows, cols, C),
            *(shape(batch, m, cols, C) for _ in range(2)),
            *(shape(batch, rows, m, C) for _ in range(2)),
            shape(count, 2 * hs, C),
            shape(8, hid),
            shape(LANES, C),
        ),
        scratch=(
            vm((batch, rows + 2 * m, wide, C), f32),
            vm((batch, rows, cols, C), f32),
            vm((C, LANES), f32),
            vm((taps, 8, C), f32),
            vm((hid, C), f32),
            vm((hid, C), f32),
            vm((hid, 3 * C), bf16),
            vm((hid, 3 * C), bf16),
            vm((2 * C, hid), bf16),
            vm((hid, LANES), f32),
            vm((hid, 2 * C), f32),
            vm((hid, 2 * C), f32),
            vm((hid, LANES), f32),
            vm((C, LANES), f32),
            vm((C, LANES), f32),
            vm((C, LANES), f32),
            vm((8, C), f32),
        ),
        flops=12 * 10**9,
        size=8 * 10**6,
        limit=24,
    )(features, got_ra, got_rb, got_cb, message, got, cotangent)

    d_got_ra, d_got_rb = both_pairs(d_row_a, d_row_b, "row")
    large_got = flip(grads[half:], last, count)
    smalls = call(
        functools.partial(kernel_grad_body, ms, order, factor, taps_i, taps_j, count),
        shape(count, 8, LANES),
        scratch=(
            vm((batch, rows + 2 * m, wide, C), f32),
            vm((batch, rows, cols + 8, C), f32),
            vm((taps, 8, C), f32),
            vm((LANES, C), f32),
        ),
        flops=4 * 10**9,
        size=4 * 10**6,
    )(src, dconv, chan)
    small_got = flip(smalls[half:], last, count)
    ways = len(masks(groups[-2]))
    *parts, edge_a, edge_b = call(
        functools.partial(back_join_body, ms),
        (*(shape(half // ways, slot, LANES) for _ in range(ways)), edges[1], edges[1]),
    )(d_edge_a, d_edge_b, d_got_ra, d_got_rb, grads, large_got, smalls, small_got)
    d_got_ca, d_got_cb = both_pairs(edge_a, edge_b, "col")
    for n, group in reversed(list(enumerate(groups[:-1]))):
        parts = [parts[0]] + [flip(part, mask, count) for part, mask in zip(parts[1:], masks(group)[1:])]
        if n:
            whole = parts[0]
            for part in parts[1:]:
                whole = whole + part
            ways = len(masks(groups[n - 1]))
            step = whole.shape[0] // ways
            parts = [whole[k * step : (k + 1) * step] for k in range(ways)]

    features_grad = call(
        functools.partial(features_grad_body, ms, taps_i, taps_j),
        shape(batch, rows, cols, C),
        scratch=(
            vm((batch, rows + 2 * m, wide, C), f32),
            vm((taps, 8, C), f32),
        ),
        flops=4 * 10**9,
        size=4 * 10**6,
    )(dconv, d_got_ra, d_got_rb, d_got_ca, d_got_cb, small, cotangent)

    outs = call(
        functools.partial(finish_body, taps_i, taps_j, cs, hs),
        (
            shape(taps_i, cs, taps_j),
            *(shape(1, cs) for _ in range(3)),
            shape(hs, C),
            shape(1, hs),
            shape(hs, C),
            *(shape(1, cs) for _ in range(2)),
        ),
        size=100000,
    )(*(p.reshape(slot, LANES) for p in parts))
    kernel_grad, cb, ng, ns, win, ib, wout, ob, ls = outs
    return (
        features_grad,
        kernel_grad.transpose(0, 2, 1),
        cb.reshape(cs),
        ng.reshape(cs),
        ns.reshape(cs),
        win.T,
        ib.reshape(hs),
        wout,
        ob.reshape(cs),
        ls.reshape(cs),
    )


def solution(mesh):
    both = P(AXES)
    tiles = P(None, "row", "col", None)
    in_specs = (
        tiles, tiles, P(None, None, AXES), both, both, both, P(None, AXES), both, P(AXES, None), both, both,
    )
    out_specs = (
        tiles, P(None, None, AXES), both, both, both, P(None, AXES), both, P(AXES, None), both, both,
    )
    return jax.shard_map(
        functools.partial(per_device, dict(mesh.shape)),
        mesh=mesh, in_specs=in_specs, out_specs=out_specs, check_vma=False,
    )
```

```python
import functools
import math

import jax
import jax.numpy as jnp
from jax import lax
from jax.experimental import pallas as pl
from jax.experimental.pallas import tpu as pltpu
from jax.sharding import PartitionSpec as P

norm_eps = 1e-06
inverse_root_twopi = 0.3989422804014327
half_log2e = 0.7213475204444817
tail_p = 0.275
tail_c = (
    0.1178092510180382,
    0.04211149421929024,
    0.3339322641039753,
    -0.33099338058058636,
    0.45199870802757525,
    -0.11485833206946416,
)
AXES = ("row", "col")
LANES = 128
LEFT = 8
NN = (((1,), (0,)), ((), ()))
NT = (((1,), (1,)), ((), ()))
f32, bf16 = jnp.float32, jnp.bfloat16


def ceil8(n):
    return (n + 7) // 8 * 8


def call(body, outs, scratch=(), flops=0, size=0, limit=8, **more):
    return pl.pallas_call(
        body,
        out_shape=outs,
        scratch_shapes=list(scratch),
        compiler_params=pltpu.CompilerParams(vmem_limit_bytes=limit and limit * 1024 * 1024),
        **more,
        cost_estimate=pl.CostEstimate(flops=flops, bytes_accessed=size, transcendentals=0),
    )


def shape(*dims):
    return jax.ShapeDtypeStruct(dims, f32)


def device_index(mesh_shape):
    return lax.axis_index("row") * mesh_shape["col"] + lax.axis_index("col")


def split(x):
    high = x.astype(bf16)
    return high, (x - high.astype(f32)).astype(bf16)


def dot(a, b, dims):
    return lax.dot_general(a, b, dims, preferred_element_type=f32)


def exchange_order(x, unit, count, me):
    rows = x.shape[0]
    index = lax.broadcasted_iota(jnp.int32, x.shape, 0)
    step = unit
    bit = 1
    while bit < count:
        up = pltpu.roll(x, step, 0)
        down = pltpu.roll(x, rows - step, 0)
        swapped = jnp.where((index & step) != 0, up, down)
        x = jnp.where((me & bit) != 0, swapped, x)
        step *= 2
        bit *= 2
    return x


def pairs(count, second):
    if not second:
        return [(i, i ^ 1) for i in range(count)]
    return [(i, (i + 1 if i % 2 else i - 1) % count) for i in range(count)]


def both_pairs(a, b, axis):
    count = lax.axis_size(axis)
    return lax.ppermute(a, axis, pairs(count, False)), lax.ppermute(b, axis, pairs(count, True))


def even(axis):
    return lax.axis_index(axis) % 2 == 0


def true_neighbour(ms, axis):
    i = lax.axis_index(axis)
    return jnp.where(i % 2 == 0, i > 0, i < ms[axis] - 1)


def start_body(feat, kernel_hbm, cb, ng, ns, ob, ls, win_hbm, ib, wout_hbm, out_ref, row_a, row_b,
               kernel_scr, v0, v1, v2, v3, v4, ib_scr, win_scr, wout_scr, sems):
    batch, rows, cols, C = feat.shape
    taps_i, cs, taps_j = kernel_hbm.shape
    hs = win_hbm.shape[0]
    taps = taps_i * taps_j
    m = taps_i // 2
    even_r = even("row")
    far = jnp.where(even_r, rows - m, 0)
    near = jnp.where(even_r, 0, rows - m)
    vectors = (v0, v1, v2, v3, v4)
    moves = [(kernel_hbm, kernel_scr), (win_hbm, win_scr), (wout_hbm, wout_scr), (ib, ib_scr)]
    moves += list(zip((cb, ng, ns, ob, ls), vectors))
    moves += [(feat.at[:, pl.ds(far, m)], row_a), (feat.at[:, pl.ds(near, m)], row_b)]
    copies = [pltpu.make_async_copy(src, dst, sems.at[n]) for n, (src, dst) in enumerate(moves)]
    for copy in copies:
        copy.start()
    out_ref[...] = jnp.zeros_like(out_ref)
    for copy in copies:
        copy.wait()
    out_ref[0:hs, :] = win_scr[...]
    out_ref[hs : 2 * hs, :] = wout_scr[...]
    base = 2 * hs
    for i in range(taps_i):
        out_ref[base : base + cs, i * taps_j : (i + 1) * taps_j] = kernel_scr[i]
    for n, ref in enumerate(vectors):
        column = jnp.broadcast_to(ref[...], (8, cs)).T
        out_ref[base : base + cs, taps + n : taps + n + 1] = column[:, 0:1]
    out_ref[base + cs : base + cs + 1, 0:hs] = ib_scr[...]


def with_corners(ms, edge_a, edge_b, got_a, got_b, out_a, out_b):
    batch, rows, m, C = edge_a.shape
    cols = got_a.shape[2]
    even_r, even_c = even("row"), even("col")
    out_a[:, m : m + rows, 0:m] = edge_a[...]
    out_b[:, m : m + rows, 0:m] = edge_b[...]
    true_r = true_neighbour(ms, "row")
    for got, end, keep in ((got_a, even_r, None), (got_b, jnp.logical_not(even_r), true_r)):
        at = jnp.where(end, rows + m, 0)
        last, first = got[:, :, cols - m :], got[:, :, 0:m]
        x, y = jnp.where(even_c, last, first), jnp.where(even_c, first, last)
        if keep is not None:
            x, y = jnp.where(keep, x, 0.0), jnp.where(keep, y, 0.0)
        out_a[:, pl.ds(at, m), 0:m] = x
        out_b[:, pl.ds(at, m), 0:m] = y


def first_join_body(ms, inner, got_a, got_b, *refs):
    parts, (slots, out_a, out_b, edge_a, edge_b) = refs[:-5], refs[-5:]
    cols, m = inner.shape[2], got_a.shape[1]
    even_c = even("col")
    first, last = inner[:, :, 0:m], inner[:, :, cols - m :]
    edge_a[...] = jnp.where(even_c, last, first)
    edge_b[...] = jnp.where(even_c, first, last)
    with_corners(ms, edge_a, edge_b, got_a, got_b, out_a, out_b)
    n = 0
    for part in parts:
        slots[n : n + part.shape[0]] = part[...]
        n += part.shape[0]


def message_body(waited, halo, *refs):
    parts, message = refs[:-1], refs[-1]
    n = 0
    for part in parts:
        for k in range(part.shape[0]):
            message[n : n + part.shape[1], :] = part[k]
            n += part.shape[1]
    batch, rows, m, _ = halo.shape
    step = (message.shape[0] - n) // (batch * rows)
    for b in range(batch):
        for r in range(rows):
            message[n : n + m, :] = halo[b, r]
            n += step


def back_join_body(ms, edge_a, edge_b, got_a, got_b, large, large_got, small, small_got, *refs):
    out_a, out_b = refs[-2:]
    rows = large.shape[1]
    n = 0
    for out in refs[:-2]:
        count = out.shape[0]
        out[:, 0:rows] = large[n : n + count] + large_got[n : n + count]
        out[:, rows:] = small[n : n + count] + small_got[n : n + count]
        n += count
    with_corners(ms, edge_a, edge_b, got_a, got_b, out_a, out_b)


def depthwise_block(read, weight, rows, taps_i, taps_j, start):
    acc = start
    for j in range(taps_j):
        w = [weight(i, j) for i in range(taps_i)]
        for r in range(rows + taps_i - 1):
            s = read(r, j)
            for i in range(taps_i):
                p = r - i
                if 0 <= p < rows:
                    term = w[i] * s
                    acc[p] = term if acc[p] is None else acc[p] + term
    return acc


def fill(ms, dst, inner, row_a, row_b, col_a, col_b):
    batch, rows, cols, _ = inner.shape
    m = row_a.shape[1]
    even_r, even_c = even("row"), even("col")
    true_r, true_c = true_neighbour(ms, "row"), true_neighbour(ms, "col")
    at_a = jnp.where(even_r, rows + m, 0)
    at_b = jnp.where(even_r, 0, rows + m)
    for b in range(batch):
        dst[b, m : m + rows, LEFT : LEFT + cols, :] = inner[b]
        dst[b, pl.ds(at_a, m), LEFT : LEFT + cols, :] = row_a[b]
        dst[b, pl.ds(at_b, m), LEFT : LEFT + cols, :] = jnp.where(true_r, row_b[b], 0.0)
        for r in range(rows + 2 * m):
            x, y = col_a(b, r), jnp.where(true_c, col_b[b, r, 0:m], 0.0)
            dst[b, r, LEFT - m : LEFT, :] = jnp.where(even_c, y, x)
            dst[b, r, LEFT + cols : LEFT + cols + m, :] = jnp.where(even_c, x, y)


def small_columns(read, hs, cs, count, me, order, scratch):
    for s in range(count):
        scratch[order[s] * cs : (order[s] + 1) * cs, :] = read(s, 2 * hs, cs)
    return exchange_order(scratch[...], cs, count, me)


def mix_body(
    ms, order, factor, taps_i, taps_j, tile,
    feat, got_ra, got_rb, got_cb, kept, got, cot_ref,
    src_out, dconv_ref, row_a, row_b, edge_a, edge_b, grads_ref, chan_ref, small_ref,
    src_ref, conv_scr, cols_scr, kb_scr, win_scr, wout_scr, w1_scr, w2_scr, w4_scr, bias_scr,
    gw1_scr, gw2_scr, gb_scr, gg_scr, gs_scr, gc_scr, cot_sum,
):
    batch, rows, cols, C = feat.shape
    count = len(order)
    cs = C // count
    taps = taps_i * taps_j
    m = taps_i // 2
    hid = win_scr.shape[0]
    hs = hid // count
    me = device_index(ms)
    half = count // 2
    slot = 2 * hs + 8
    step_rows = (got.shape[0] - half * slot) // (batch * (rows + 2 * m))

    def read(s, first, size):
        at = (s % half) * slot + first
        return (kept if s < half else got)[at : at + size, :]

    def col_a(b, r):
        at = half * slot + (b * (rows + 2 * m) + r) * step_rows
        return got[at : at + m, :]

    fill(ms, src_ref, feat, got_ra, got_rb, col_a, got_cb)
    src_out[...] = src_ref[...]
    columns = small_columns(read, hs, cs, count, me, order, cols_scr)
    cols_scr[...] = columns
    rows_form = columns.T
    small_ref[...] = rows_form
    for t in range(taps):
        kb_scr[t] = jnp.broadcast_to(rows_form[t : t + 1, :], (8, C))
    conv_bias = jnp.broadcast_to(rows_form[taps : taps + 1, :], (8, C))

    for s in range(count):
        win_scr[s * hs : (s + 1) * hs, :] = read(s, 0, hs)
        wout_scr[s * hs : (s + 1) * hs, :] = read(s, hs, hs)
    for s in range(count):
        cols_bias = jnp.broadcast_to(read(s, 2 * hs + cs, 1), (LANES, LANES)).T
        bias_scr[s * hs : (s + 1) * hs, :] = cols_bias[0:hs, :]

    scale_row = rows_form[taps + 4 : taps + 5, :]
    wh, wl = split(win_scr[...])
    w1_scr[:, 0:C] = wh
    w1_scr[:, C : 2 * C] = wl
    w1_scr[:, 2 * C : 3 * C] = wh
    oh, ol = split(wout_scr[...] * scale_row)
    w2_scr[:, 0:C] = oh
    w2_scr[:, C : 2 * C] = ol
    w2_scr[:, 2 * C : 3 * C] = oh
    th, tl = split(win_scr[...].T)
    w4_scr[0:C, :] = th
    w4_scr[C : 2 * C, :] = tl

    def conv_block(b, q):
        acc = depthwise_block(
            lambda r, j: src_ref[b, r, LEFT - m + q + j : LEFT - m + q + j + 8, :],
            lambda i, j: kb_scr[i * taps_j + j],
            rows, taps_i, taps_j, [conv_bias] * rows,
        )
        for p in range(rows):
            conv_scr[b, p, q : q + 8, :] = acc[p]

    for ref in (gw1_scr, gw2_scr, gb_scr, gg_scr, gs_scr, gc_scr, cot_sum):
        ref[...] = jnp.zeros_like(ref)
    gain = cols_scr[:, taps + 1 : taps + 2]
    shift = cols_scr[:, taps + 2 : taps + 3]

    def lanes_sum(x):
        total = x[:, 0:LANES]
        for k in range(LANES, x.shape[1], LANES):
            total = total + x[:, k : k + LANES]
        return total

    def image(b):
        x = conv_scr[b].reshape(tile, C).T
        mean = jnp.mean(x, axis=0, keepdims=True)
        centred = x - mean
        variance = jnp.mean(centred * centred, axis=0, keepdims=True)
        inverse = lax.rsqrt(variance + norm_eps)
        normed = centred * inverse
        lin = normed * gain + shift
        lh, ll = split(lin)
        cot = cot_ref[b].reshape(tile, C)
        ch, cl = split(cot)
        yield
        act = dot(w1_scr[...], jnp.concatenate([lh, lh, ll], axis=0), NN)
        d_hid = dot(w2_scr[...], jnp.concatenate([ch, ch, cl], axis=1), NT)
        yield
        bias = bias_scr[...]
        act = act + jnp.concatenate([bias] * (tile // LANES), axis=1)
        e = jnp.exp2((act * act) * (-half_log2e))
        d = 1.0 + tail_p * jnp.abs(act)
        r = pltpu.reciprocal(d, approx=True)
        r = r * (2.0 - d * r)
        q = tail_c[5] * r + tail_c[4]
        for k in (3, 2, 1, 0):
            q = q * r + tail_c[k]
        q = q * r * e
        phi = jnp.where(act > 0, 1.0 - q, q)
        hidden = act * phi
        d_act = d_hid * (phi + act * e * inverse_root_twopi)
        yield
        hh, hl = split(hidden)
        dh, dl = split(d_act)
        gb_scr[...] += lanes_sum(d_act)
        both = dot(w4_scr[...], dh, NN)
        d_lin = both[0:C] + both[C : 2 * C] + dot(w4_scr[0:C, :], dl, NN)
        yield
        gw1_scr[...] += dot(dh, jnp.concatenate([lh, ll], axis=0), NT)
        gw1_scr[:, 0:C] += dot(dl, lh, NT)
        gw2_scr[...] += dot(hh, jnp.concatenate([ch, cl], axis=1), NN)
        gw2_scr[:, 0:C] += dot(hl, ch, NN)
        yield
        gg_scr[...] += lanes_sum(d_lin * normed)
        gs_scr[...] += lanes_sum(d_lin)
        d_norm = d_lin * gain
        d_conv = inverse * (
            d_norm
            - jnp.mean(d_norm, axis=0, keepdims=True)
            - normed * jnp.mean(d_norm * normed, axis=0, keepdims=True)
        )
        gc_scr[...] += lanes_sum(d_conv)
        dconv_ref[b] = d_conv.T.reshape(rows, cols, C)
        cot_sum[...] += jnp.sum(cot.reshape(tile // 8, 8, C), axis=0)

    blocks = list(range(0, cols, 8))
    for q in blocks:
        conv_block(0, q)
    for b in range(batch):
        ahead = list(blocks) if b + 1 < batch else []
        stages = 5
        share = -(-len(ahead) // stages)
        for _ in image(b):
            for q in ahead[:share]:
                conv_block(b + 1, q)
            ahead = ahead[share:]
        for q in ahead:
            conv_block(b + 1, q)

    even_r, even_c = even("row"), even("col")
    row_a[...] = dconv_ref[:, pl.ds(jnp.where(even_r, rows - m, 0), m)]
    row_b[...] = dconv_ref[:, pl.ds(jnp.where(even_r, 0, rows - m), m)]
    first, last = dconv_ref[:, :, 0:m], dconv_ref[:, :, cols - m : cols]
    edge_a[...] = jnp.where(even_c, last, first)
    edge_b[...] = jnp.where(even_c, first, last)

    h = gw2_scr[:, 0:C] + gw2_scr[:, C : 2 * C]
    gw1 = (gw1_scr[:, 0:C] + gw1_scr[:, C : 2 * C]) * factor
    gw2 = h * (scale_row * factor)
    gb = (jnp.sum(gb_scr[...].T, axis=0, keepdims=True)) * factor
    for s in range(count):
        grads_ref[s, 0:hs, :] = gw1[s * hs : (s + 1) * hs, :]
        grads_ref[s, hs : 2 * hs, :] = gw2[s * hs : (s + 1) * hs, :]
    total = jnp.sum(cot_sum[...], axis=0, keepdims=True)
    outb = rows_form[taps + 3 : taps + 4, :]
    scale_grad = jnp.sum(h * wout_scr[...], axis=0, keepdims=True) + outb * total
    chan_ref[...] = jnp.zeros_like(chan_ref)
    chan_ref[0:1, 0:C] = jnp.sum(gc_scr[...].T, axis=0, keepdims=True) * factor
    chan_ref[1:2, 0:C] = jnp.sum(gg_scr[...].T, axis=0, keepdims=True) * factor
    chan_ref[2:3, 0:C] = jnp.sum(gs_scr[...].T, axis=0, keepdims=True) * factor
    chan_ref[3:4, 0:C] = total * scale_row * factor
    chan_ref[4:5, 0:C] = scale_grad * factor
    chan_ref[5:6, :] = gb


def kernel_grad_body(ms, order, factor, taps_i, taps_j, count, src_in, dconv_in, chan_ref, out_ref, src_ref, dconv_ref, acc_scr, rows_scr):
    batch, rows, cols, C = dconv_in.shape
    m = taps_i // 2
    taps = taps_i * taps_j
    cs = C // count
    me = device_index(ms)
    src_ref[...] = src_in[...]
    dconv_ref[:, :, 0:cols, :] = dconv_in[...]
    acc_scr[...] = jnp.zeros_like(acc_scr)

    def step(b, _):
        for j in range(taps_j):
            acc = [acc_scr[i * taps_j + j] for i in range(taps_i)]
            for q in range(0, cols, 8):
                d = [dconv_ref[b, p, q : q + 8, :] for p in range(rows)]
                for r in range(rows + taps_i - 1):
                    s = src_ref[b, r, LEFT - m + q + j : LEFT - m + q + j + 8, :]
                    for i in range(taps_i):
                        p = r - i
                        if 0 <= p < rows:
                            acc[i] = acc[i] + d[p] * s
            for i in range(taps_i):
                acc_scr[i * taps_j + j] = acc[i]
        return 0

    lax.fori_loop(0, batch, step, 0)
    rows_scr[...] = jnp.zeros_like(rows_scr)
    for t in range(taps):
        rows_scr[t : t + 1, :] = jnp.sum(acc_scr[t], axis=0, keepdims=True) * factor
    rows_scr[taps : taps + 5, :] = chan_ref[0:5, 0:C]
    columns = exchange_order(rows_scr[...].T, cs, count, me)
    out_ref[...] = jnp.zeros_like(out_ref)
    hs = chan_ref.shape[1] // count
    for s in range(count):
        out_ref[s, 0:cs, :] = columns[order[s] * cs : (order[s] + 1) * cs, :]
        out_ref[s, cs : cs + 1, 0:hs] = chan_ref[5:6, s * hs : (s + 1) * hs]


def features_grad_body(ms, taps_i, taps_j, inner, got_ra, got_rb, got_ca, got_cb, small_ref, cot_ref, out_ref, ext_scr, kb_scr):
    batch, rows, cols, C = inner.shape
    m = taps_i // 2
    taps = taps_i * taps_j
    fill(ms, ext_scr, inner, got_ra, got_rb, lambda b, r: got_ca[b, r, 0 : taps_i // 2], got_cb)
    for t in range(taps):
        kb_scr[t] = jnp.broadcast_to(small_ref[t : t + 1, :], (8, C))

    def step(b, _):
        for q in range(0, cols, 8):
            acc = depthwise_block(
                lambda r, j: ext_scr[b, r, LEFT - m + q + j : LEFT - m + q + j + 8, :],
                lambda i, j: kb_scr[taps - 1 - (i * taps_j + j)],
                rows, taps_i, taps_j, [cot_ref[b, p, q : q + 8, :] for p in range(rows)],
            )
            for p in range(rows):
                out_ref[b, p, q : q + 8, :] = acc[p]
        return 0

    lax.fori_loop(0, batch, step, 0)


def finish_body(taps_i, taps_j, cs, hs, *refs):
    parts, outs = refs[:-9], refs[-9:]
    total = parts[0][...]
    for part in parts[1:]:
        total = total + part[...]
    kernel_out, cb, ng, ns, win_out, ib, wout_out, ob, ls = outs
    taps = taps_i * taps_j
    win_out[...] = total[0:hs, :]
    wout_out[...] = total[hs : 2 * hs, :]
    small = total[2 * hs : 2 * hs + 8, :]
    for i in range(taps_i):
        kernel_out[i] = small[0:cs, i * taps_j : (i + 1) * taps_j]
    flipped = small.T
    for n, ref in enumerate((cb, ng, ns, ob, ls)):
        ref[...] = flipped[taps + n : taps + n + 1, 0:cs]
    ib[...] = small[cs : cs + 1, 0:hs]


def flip(x, mask, count):
    return lax.ppermute(x, AXES, [(i, i ^ mask) for i in range(count)])


def groups_of(ms):
    bits_col = ms["col"].bit_length() - 1
    bits_row = ms["row"].bit_length() - 1
    col = [1 << k for k in range(bits_col)]
    row = [1 << (k + bits_col) for k in range(bits_row)]
    rest = col[1:]
    out = [rest[k : k + 2] for k in range(0, len(rest), 2)]
    out += [row[k : k + 2] for k in range(0, len(row), 2)]
    return out + [col[:1]]


def masks(group):
    out = [0]
    for bit in group:
        out += [bit ^ x for x in out]
    return out


def per_device(ms, features, cotangent, conv_kernel, conv_bias, norm_gain, norm_shift, w_in, in_bias, w_out, out_bias, layer_scale):
    batch, rows, cols, C = features.shape
    taps_i, taps_j, cs = conv_kernel.shape
    hs = w_out.shape[0]
    count = ms["row"] * ms["col"]
    hid = hs * count
    m = taps_i // 2
    taps = taps_i * taps_j
    cells = batch * rows * cols * count
    factor = 1.0 / math.sqrt(cells)
    slot = 2 * hs + 8
    wide = ceil8(LEFT + cols + m)

    vm = pltpu.VMEM
    vectors = [v.reshape(1, cs) for v in (conv_bias, norm_gain, norm_shift, out_bias, layer_scale)]
    block, row_a, row_b = call(
        start_body,
        (
            shape(slot, LANES),
            *(shape(batch, m, cols, C) for _ in range(2)),
        ),
        scratch=(
            vm((taps_i, cs, taps_j), f32),
            *(vm((1, cs), f32) for _ in range(5)),
            vm((1, hs), f32),
            vm((hs, C), f32),
            vm((hs, C), f32),
            pltpu.SemaphoreType.DMA((11,)),
        ),
        size=10**6,
        limit=None,
        in_specs=[pl.BlockSpec(memory_space=pl.ANY)] * 10,
    )(features, conv_kernel.transpose(0, 2, 1), *vectors, w_in.T, in_bias.reshape(1, hs), w_out)

    wide_m = (m + 3) // 4 * 4
    edges = (shape(batch, rows + 2 * m, m, C), shape(batch, rows + 2 * m, wide_m, C))
    anywhere, in_vmem = pl.BlockSpec(memory_space=pl.ANY), pl.BlockSpec(memory_space=pltpu.VMEM)
    groups = groups_of(ms)
    order = [0]
    got_ra, got_rb = both_pairs(row_a, row_b, "row")
    parts = [block[None]]
    for n, group in enumerate(groups[:-1]):
        if n == 1:
            slots, edge_a, edge_b = call(
                functools.partial(first_join_body, ms),
                (shape(len(order), slot, LANES), *edges),
                scratch=[vm((batch, rows, m, C), f32) for _ in range(2)],
            )(features, got_ra, got_rb, *parts)
            got_cb = lax.ppermute(edge_b, "col", pairs(ms["col"], True))
        else:
            slots = jnp.concatenate(parts)
        parts = [slots] + [flip(slots, mask, count) for mask in masks(group)[1:]]
        order = [mask ^ x for mask in masks(group) for x in order]
    half = count // 2
    message = call(
        message_body,
        shape(half * slot + edges[0].shape[0] * edges[0].shape[1] * wide_m, LANES),
        in_specs=[anywhere] + [in_vmem] * (1 + len(parts)),
    )(got_cb, edge_a, *parts)
    last = groups[-1][0]
    order += [last ^ x for x in order]
    got = flip(message, last, count)
    tile = rows * cols
    src, dconv, d_row_a, d_row_b, d_edge_a, d_edge_b, grads, chan, small = call(
        functools.partial(mix_body, ms, order, factor, taps_i, taps_j, tile),
        (
            shape(batch, rows + 2 * m, wide, C),
            shape(batch, rows, cols, C),
            *(shape(batch, m, cols, C) for _ in range(2)),
            *(shape(batch, rows, m, C) for _ in range(2)),
            shape(count, 2 * hs, C),
            shape(8, hid),
            shape(LANES, C),
        ),
        scratch=(
            vm((batch, rows + 2 * m, wide, C), f32),
            vm((batch, rows, cols, C), f32),
            vm((C, LANES), f32),
            vm((taps, 8, C), f32),
            vm((hid, C), f32),
            vm((hid, C), f32),
            vm((hid, 3 * C), bf16),
            vm((hid, 3 * C), bf16),
            vm((2 * C, hid), bf16),
            vm((hid, LANES), f32),
            vm((hid, 2 * C), f32),
            vm((hid, 2 * C), f32),
            vm((hid, LANES), f32),
            vm((C, LANES), f32),
            vm((C, LANES), f32),
            vm((C, LANES), f32),
            vm((8, C), f32),
        ),
        flops=12 * 10**9,
        size=8 * 10**6,
        limit=24,
    )(features, got_ra, got_rb, got_cb, message, got, cotangent)

    d_got_ra, d_got_rb = both_pairs(d_row_a, d_row_b, "row")
    large_got = flip(grads[half:], last, count)
    smalls = call(
        functools.partial(kernel_grad_body, ms, order, factor, taps_i, taps_j, count),
        shape(count, 8, LANES),
        scratch=(
            vm((batch, rows + 2 * m, wide, C), f32),
            vm((batch, rows, cols + 8, C), f32),
            vm((taps, 8, C), f32),
            vm((LANES, C), f32),
        ),
        flops=4 * 10**9,
        size=4 * 10**6,
    )(src, dconv, chan)
    small_got = flip(smalls[half:], last, count)
    ways = len(masks(groups[-2]))
    *parts, edge_a, edge_b = call(
        functools.partial(back_join_body, ms),
        (*(shape(half // ways, slot, LANES) for _ in range(ways)), edges[1], edges[1]),
    )(d_edge_a, d_edge_b, d_got_ra, d_got_rb, grads, large_got, smalls, small_got)
    d_got_ca, d_got_cb = both_pairs(edge_a, edge_b, "col")
    for n, group in reversed(list(enumerate(groups[:-1]))):
        parts = [parts[0]] + [flip(part, mask, count) for part, mask in zip(parts[1:], masks(group)[1:])]
        if n:
            whole = parts[0]
            for part in parts[1:]:
                whole = whole + part
            ways = len(masks(groups[n - 1]))
            step = whole.shape[0] // ways
            parts = [whole[k * step : (k + 1) * step] for k in range(ways)]

    features_grad = call(
        functools.partial(features_grad_body, ms, taps_i, taps_j),
        shape(batch, rows, cols, C),
        scratch=(
            vm((batch, rows + 2 * m, wide, C), f32),
            vm((taps, 8, C), f32),
        ),
        flops=4 * 10**9,
        size=4 * 10**6,
    )(dconv, d_got_ra, d_got_rb, d_got_ca, d_got_cb, small, cotangent)

    outs = call(
        functools.partial(finish_body, taps_i, taps_j, cs, hs),
        (
            shape(taps_i, cs, taps_j),
            *(shape(1, cs) for _ in range(3)),
            shape(hs, C),
            shape(1, hs),
            shape(hs, C),
            *(shape(1, cs) for _ in range(2)),
        ),
        size=100000,
    )(*(p.reshape(slot, LANES) for p in parts))
    kernel_grad, cb, ng, ns, win, ib, wout, ob, ls = outs
    return (
        features_grad,
        kernel_grad.transpose(0, 2, 1),
        cb.reshape(cs),
        ng.reshape(cs),
        ns.reshape(cs),
        win.T,
        ib.reshape(hs),
        wout,
        ob.reshape(cs),
        ls.reshape(cs),
    )


def solution(mesh):
    both = P(AXES)
    tiles = P(None, "row", "col", None)
    in_specs = (
        tiles, tiles, P(None, None, AXES), both, both, both, P(None, AXES), both, P(AXES, None), both, both,
    )
    out_specs = (
        tiles, P(None, None, AXES), both, both, both, P(None, AXES), both, P(AXES, None), both, both,
    )
    return jax.shard_map(
        functools.partial(per_device, dict(mesh.shape)),
        mesh=mesh, in_specs=in_specs, out_specs=out_specs, check_vma=False,
    )
```

```python
import functools
import math

import jax
import jax.numpy as jnp
from jax import lax
from jax.experimental import pallas as pl
from jax.experimental.pallas import tpu as pltpu
from jax.sharding import PartitionSpec as P

norm_eps = 1e-06
inverse_root_twopi = 0.3989422804014327
half_log2e = 0.7213475204444817
tail_p = 0.275
tail_c = (
    0.1178092510180382,
    0.04211149421929024,
    0.3339322641039753,
    -0.33099338058058636,
    0.45199870802757525,
    -0.11485833206946416,
)
AXES = ("row", "col")
LANES = 128
LEFT = 8
NN = (((1,), (0,)), ((), ()))
NT = (((1,), (1,)), ((), ()))
f32, bf16 = jnp.float32, jnp.bfloat16


def ceil8(n):
    return (n + 7) // 8 * 8


def call(body, outs, scratch=(), flops=0, size=0, limit=8, **more):
    return pl.pallas_call(
        body,
        out_shape=outs,
        scratch_shapes=list(scratch),
        compiler_params=pltpu.CompilerParams(vmem_limit_bytes=limit and limit * 1024 * 1024),
        **more,
        cost_estimate=pl.CostEstimate(flops=flops, bytes_accessed=size, transcendentals=0),
    )


def shape(*dims):
    return jax.ShapeDtypeStruct(dims, f32)


def device_index(mesh_shape):
    return lax.axis_index("row") * mesh_shape["col"] + lax.axis_index("col")


def split(x):
    high = x.astype(bf16)
    return high, (x - high.astype(f32)).astype(bf16)


def dot(a, b, dims):
    return lax.dot_general(a, b, dims, preferred_element_type=f32)


def exchange_order(x, unit, count, me):
    rows = x.shape[0]
    index = lax.broadcasted_iota(jnp.int32, x.shape, 0)
    step = unit
    bit = 1
    while bit < count:
        up = pltpu.roll(x, step, 0)
        down = pltpu.roll(x, rows - step, 0)
        swapped = jnp.where((index & step) != 0, up, down)
        x = jnp.where((me & bit) != 0, swapped, x)
        step *= 2
        bit *= 2
    return x


def pairs(count, second):
    if not second:
        return [(i, i ^ 1) for i in range(count)]
    return [(i, (i + 1 if i % 2 else i - 1) % count) for i in range(count)]


def both_pairs(a, b, axis):
    count = lax.axis_size(axis)
    return lax.ppermute(a, axis, pairs(count, False)), lax.ppermute(b, axis, pairs(count, True))


def even(axis):
    return lax.axis_index(axis) % 2 == 0


def true_neighbour(ms, axis):
    i = lax.axis_index(axis)
    return jnp.where(i % 2 == 0, i > 0, i < ms[axis] - 1)


def start_body(feat, kernel_hbm, cb, ng, ns, ob, ls, win_hbm, ib, wout_hbm, out_ref, row_a, row_b,
               kernel_scr, v0, v1, v2, v3, v4, ib_scr, win_scr, wout_scr, sems):
    batch, rows, cols, C = feat.shape
    taps_i, cs, taps_j = kernel_hbm.shape
    hs = win_hbm.shape[0]
    taps = taps_i * taps_j
    m = taps_i // 2
    even_r = even("row")
    far = jnp.where(even_r, rows - m, 0)
    near = jnp.where(even_r, 0, rows - m)
    vectors = (v0, v1, v2, v3, v4)
    moves = [(kernel_hbm, kernel_scr), (win_hbm, win_scr), (wout_hbm, wout_scr), (ib, ib_scr)]
    moves += list(zip((cb, ng, ns, ob, ls), vectors))
    moves += [(feat.at[:, pl.ds(far, m)], row_a), (feat.at[:, pl.ds(near, m)], row_b)]
    copies = [pltpu.make_async_copy(src, dst, sems.at[n]) for n, (src, dst) in enumerate(moves)]
    for copy in copies:
        copy.start()
    out_ref[...] = jnp.zeros_like(out_ref)
    for copy in copies:
        copy.wait()
    out_ref[0:hs, :] = win_scr[...]
    out_ref[hs : 2 * hs, :] = wout_scr[...]
    base = 2 * hs
    for i in range(taps_i):
        out_ref[base : base + cs, i * taps_j : (i + 1) * taps_j] = kernel_scr[i]
    for n, ref in enumerate(vectors):
        column = jnp.broadcast_to(ref[...], (8, cs)).T
        out_ref[base : base + cs, taps + n : taps + n + 1] = column[:, 0:1]
    out_ref[base + cs : base + cs + 1, 0:hs] = ib_scr[...]


def with_corners(ms, edge_a, edge_b, got_a, got_b, out_a, out_b):
    batch, rows, m, C = edge_a.shape
    cols = got_a.shape[2]
    even_r, even_c = even("row"), even("col")
    out_a[:, m : m + rows, 0:m] = edge_a[...]
    out_b[:, m : m + rows, 0:m] = edge_b[...]
    true_r = true_neighbour(ms, "row")
    for got, end, keep in ((got_a, even_r, None), (got_b, jnp.logical_not(even_r), true_r)):
        at = jnp.where(end, rows + m, 0)
        last, first = got[:, :, cols - m :], got[:, :, 0:m]
        x, y = jnp.where(even_c, last, first), jnp.where(even_c, first, last)
        if keep is not None:
            x, y = jnp.where(keep, x, 0.0), jnp.where(keep, y, 0.0)
        out_a[:, pl.ds(at, m), 0:m] = x
        out_b[:, pl.ds(at, m), 0:m] = y


def first_join_body(ms, inner, got_a, got_b, *refs):
    parts, (slots, out_a, out_b, edge_a, edge_b) = refs[:-5], refs[-5:]
    cols, m = inner.shape[2], got_a.shape[1]
    even_c = even("col")
    first, last = inner[:, :, 0:m], inner[:, :, cols - m :]
    edge_a[...] = jnp.where(even_c, last, first)
    edge_b[...] = jnp.where(even_c, first, last)
    with_corners(ms, edge_a, edge_b, got_a, got_b, out_a, out_b)
    n = 0
    for part in parts:
        slots[n : n + part.shape[0]] = part[...]
        n += part.shape[0]


def message_body(waited, halo, *refs):
    parts, message = refs[:-1], refs[-1]
    n = 0
    for part in parts:
        for k in range(part.shape[0]):
            message[n : n + part.shape[1], :] = part[k]
            n += part.shape[1]
    batch, rows, m, _ = halo.shape
    step = (message.shape[0] - n) // (batch * rows)
    for b in range(batch):
        for r in range(rows):
            message[n : n + m, :] = halo[b, r]
            n += step


def back_join_body(ms, edge_a, edge_b, got_a, got_b, large, large_got, small, small_got, *refs):
    out_a, out_b = refs[-2:]
    rows = large.shape[1]
    n = 0
    for out in refs[:-2]:
        count = out.shape[0]
        out[:, 0:rows] = large[n : n + count] + large_got[n : n + count]
        out[:, rows:] = small[n : n + count] + small_got[n : n + count]
        n += count
    with_corners(ms, edge_a, edge_b, got_a, got_b, out_a, out_b)


def depthwise_block(read, weight, rows, taps_i, taps_j, start):
    acc = start
    for j in range(taps_j):
        w = [weight(i, j) for i in range(taps_i)]
        for r in range(rows + taps_i - 1):
            s = read(r, j)
            for i in range(taps_i):
                p = r - i
                if 0 <= p < rows:
                    term = w[i] * s
                    acc[p] = term if acc[p] is None else acc[p] + term
    return acc


def fill(ms, dst, inner, row_a, row_b, col_a, col_b):
    batch, rows, cols, _ = inner.shape
    m = row_a.shape[1]
    even_r, even_c = even("row"), even("col")
    true_r, true_c = true_neighbour(ms, "row"), true_neighbour(ms, "col")
    at_a = jnp.where(even_r, rows + m, 0)
    at_b = jnp.where(even_r, 0, rows + m)
    for b in range(batch):
        dst[b, m : m + rows, LEFT : LEFT + cols, :] = inner[b]
        dst[b, pl.ds(at_a, m), LEFT : LEFT + cols, :] = row_a[b]
        dst[b, pl.ds(at_b, m), LEFT : LEFT + cols, :] = jnp.where(true_r, row_b[b], 0.0)
        for r in range(rows + 2 * m):
            x, y = col_a(b, r), jnp.where(true_c, col_b[b, r, 0:m], 0.0)
            dst[b, r, LEFT - m : LEFT, :] = jnp.where(even_c, y, x)
            dst[b, r, LEFT + cols : LEFT + cols + m, :] = jnp.where(even_c, x, y)


def small_columns(read, hs, cs, count, me, order, scratch):
    for s in range(count):
        scratch[order[s] * cs : (order[s] + 1) * cs, :] = read(s, 2 * hs, cs)
    return exchange_order(scratch[...], cs, count, me)


def mix_body(
    ms, order, factor, taps_i, taps_j, tile,
    feat, got_ra, got_rb, got_cb, kept, got, cot_ref,
    src_out, dconv_ref, row_a, row_b, edge_a, edge_b, grads_ref, chan_ref, small_ref,
    src_ref, conv_scr, cols_scr, kb_scr, win_scr, wout_scr, w1_scr, w2_scr, w4_scr, bias_scr, bias_rows,
    gw1_scr, gw2_scr, gb_scr, gg_scr, gs_scr, gc_scr, cot_sum,
):
    batch, rows, cols, C = feat.shape
    count = len(order)
    cs = C // count
    taps = taps_i * taps_j
    m = taps_i // 2
    hid = win_scr.shape[0]
    hs = hid // count
    me = device_index(ms)
    half = count // 2
    slot = 2 * hs + 8
    step_rows = (got.shape[0] - half * slot) // (batch * (rows + 2 * m))

    def read(s, first, size):
        at = (s % half) * slot + first
        return (kept if s < half else got)[at : at + size, :]

    def col_a(b, r):
        at = half * slot + (b * (rows + 2 * m) + r) * step_rows
        return got[at : at + m, :]

    fill(ms, src_ref, feat, got_ra, got_rb, col_a, got_cb)
    src_out[...] = src_ref[...]
    columns = small_columns(read, hs, cs, count, me, order, cols_scr)
    cols_scr[...] = columns
    rows_form = columns.T
    small_ref[...] = rows_form
    for t in range(taps):
        kb_scr[t] = jnp.broadcast_to(rows_form[t : t + 1, :], (8, C))
    conv_bias = jnp.broadcast_to(rows_form[taps : taps + 1, :], (8, C))

    for s in range(count):
        win_scr[s * hs : (s + 1) * hs, :] = read(s, 0, hs)
        wout_scr[s * hs : (s + 1) * hs, :] = read(s, hs, hs)
        bias_rows[s : s + 1, :] = read(s, 2 * hs + cs, 1)
    bias_columns = bias_rows[...].T
    for s in range(count):
        bias_scr[s * hs : (s + 1) * hs, :] = jnp.broadcast_to(bias_columns[0:hs, s : s + 1], (hs, LANES))

    scale_row = rows_form[taps + 4 : taps + 5, :]
    wh, wl = split(win_scr[...])
    w1_scr[:, 0:C] = wh
    w1_scr[:, C : 2 * C] = wl
    w1_scr[:, 2 * C : 3 * C] = wh
    oh, ol = split(wout_scr[...] * scale_row)
    w2_scr[:, 0:C] = oh
    w2_scr[:, C : 2 * C] = ol
    w2_scr[:, 2 * C : 3 * C] = oh
    th, tl = split(win_scr[...].T)
    w4_scr[0:C, :] = th
    w4_scr[C : 2 * C, :] = tl

    def conv_block(b, q):
        acc = depthwise_block(
            lambda r, j: src_ref[b, r, LEFT - m + q + j : LEFT - m + q + j + 8, :],
            lambda i, j: kb_scr[i * taps_j + j],
            rows, taps_i, taps_j, [conv_bias] * rows,
        )
        for p in range(rows):
            conv_scr[b, p, q : q + 8, :] = acc[p]

    for ref in (gw1_scr, gw2_scr, gb_scr, gg_scr, gs_scr, gc_scr, cot_sum):
        ref[...] = jnp.zeros_like(ref)
    gain = cols_scr[:, taps + 1 : taps + 2]
    shift = cols_scr[:, taps + 2 : taps + 3]

    def lanes_sum(x):
        total = x[:, 0:LANES]
        for k in range(LANES, x.shape[1], LANES):
            total = total + x[:, k : k + LANES]
        return total

    def image(b):
        x = conv_scr[b].reshape(tile, C).T
        mean = jnp.mean(x, axis=0, keepdims=True)
        centred = x - mean
        variance = jnp.mean(centred * centred, axis=0, keepdims=True)
        inverse = lax.rsqrt(variance + norm_eps)
        normed = centred * inverse
        lin = normed * gain + shift
        lh, ll = split(lin)
        cot = cot_ref[b].reshape(tile, C)
        ch, cl = split(cot)
        yield
        act = dot(w1_scr[...], jnp.concatenate([lh, lh, ll], axis=0), NN)
        d_hid = dot(w2_scr[...], jnp.concatenate([ch, ch, cl], axis=1), NT)
        yield
        bias = bias_scr[...]
        act = act + jnp.concatenate([bias] * (tile // LANES), axis=1)
        e = jnp.exp2((act * act) * (-half_log2e))
        d = 1.0 + tail_p * jnp.abs(act)
        r = pltpu.reciprocal(d, approx=True)
        r = r * (2.0 - d * r)
        q = tail_c[5] * r + tail_c[4]
        for k in (3, 2, 1, 0):
            q = q * r + tail_c[k]
        q = q * r * e
        phi = jnp.where(act > 0, 1.0 - q, q)
        hidden = act * phi
        d_act = d_hid * (phi + act * e * inverse_root_twopi)
        yield
        hh, hl = split(hidden)
        dh, dl = split(d_act)
        gb_scr[...] += lanes_sum(d_act)
        both = dot(w4_scr[...], dh, NN)
        d_lin = both[0:C] + both[C : 2 * C] + dot(w4_scr[0:C, :], dl, NN)
        yield
        gw1_scr[...] += dot(dh, jnp.concatenate([lh, ll], axis=0), NT)
        gw1_scr[:, 0:C] += dot(dl, lh, NT)
        gw2_scr[...] += dot(hh, jnp.concatenate([ch, cl], axis=1), NN)
        gw2_scr[:, 0:C] += dot(hl, ch, NN)
        yield
        gg_scr[...] += lanes_sum(d_lin * normed)
        gs_scr[...] += lanes_sum(d_lin)
        d_norm = d_lin * gain
        d_conv = inverse * (
            d_norm
            - jnp.mean(d_norm, axis=0, keepdims=True)
            - normed * jnp.mean(d_norm * normed, axis=0, keepdims=True)
        )
        gc_scr[...] += lanes_sum(d_conv)
        dconv_ref[b] = d_conv.T.reshape(rows, cols, C)
        cot_sum[...] += jnp.sum(cot.reshape(tile // 8, 8, C), axis=0)

    blocks = list(range(0, cols, 8))
    for q in blocks:
        conv_block(0, q)
    for b in range(batch):
        ahead = list(blocks) if b + 1 < batch else []
        stages = 5
        share = -(-len(ahead) // stages)
        for _ in image(b):
            for q in ahead[:share]:
                conv_block(b + 1, q)
            ahead = ahead[share:]
        for q in ahead:
            conv_block(b + 1, q)

    even_r, even_c = even("row"), even("col")
    row_a[...] = dconv_ref[:, pl.ds(jnp.where(even_r, rows - m, 0), m)]
    row_b[...] = dconv_ref[:, pl.ds(jnp.where(even_r, 0, rows - m), m)]
    first, last = dconv_ref[:, :, 0:m], dconv_ref[:, :, cols - m : cols]
    edge_a[...] = jnp.where(even_c, last, first)
    edge_b[...] = jnp.where(even_c, first, last)

    h = gw2_scr[:, 0:C] + gw2_scr[:, C : 2 * C]
    gw1 = (gw1_scr[:, 0:C] + gw1_scr[:, C : 2 * C]) * factor
    gw2 = h * (scale_row * factor)
    gb = (jnp.sum(gb_scr[...].T, axis=0, keepdims=True)) * factor
    for s in range(count):
        grads_ref[s, 0:hs, :] = gw1[s * hs : (s + 1) * hs, :]
        grads_ref[s, hs : 2 * hs, :] = gw2[s * hs : (s + 1) * hs, :]
    total = jnp.sum(cot_sum[...], axis=0, keepdims=True)
    outb = rows_form[taps + 3 : taps + 4, :]
    scale_grad = jnp.sum(h * wout_scr[...], axis=0, keepdims=True) + outb * total
    chan_ref[...] = jnp.zeros_like(chan_ref)
    chan_ref[0:1, 0:C] = jnp.sum(gc_scr[...].T, axis=0, keepdims=True) * factor
    chan_ref[1:2, 0:C] = jnp.sum(gg_scr[...].T, axis=0, keepdims=True) * factor
    chan_ref[2:3, 0:C] = jnp.sum(gs_scr[...].T, axis=0, keepdims=True) * factor
    chan_ref[3:4, 0:C] = total * scale_row * factor
    chan_ref[4:5, 0:C] = scale_grad * factor
    chan_ref[5:6, :] = gb


def kernel_grad_body(ms, order, factor, taps_i, taps_j, count, src_in, dconv_in, chan_ref, out_ref, src_ref, dconv_ref, acc_scr, rows_scr):
    batch, rows, cols, C = dconv_in.shape
    m = taps_i // 2
    taps = taps_i * taps_j
    cs = C // count
    me = device_index(ms)
    src_ref[...] = src_in[...]
    dconv_ref[:, :, 0:cols, :] = dconv_in[...]
    acc_scr[...] = jnp.zeros_like(acc_scr)

    def step(b, _):
        for j in range(taps_j):
            acc = [acc_scr[i * taps_j + j] for i in range(taps_i)]
            for q in range(0, cols, 8):
                d = [dconv_ref[b, p, q : q + 8, :] for p in range(rows)]
                for r in range(rows + taps_i - 1):
                    s = src_ref[b, r, LEFT - m + q + j : LEFT - m + q + j + 8, :]
                    for i in range(taps_i):
                        p = r - i
                        if 0 <= p < rows:
                            acc[i] = acc[i] + d[p] * s
            for i in range(taps_i):
                acc_scr[i * taps_j + j] = acc[i]
        return 0

    lax.fori_loop(0, batch, step, 0)
    rows_scr[...] = jnp.zeros_like(rows_scr)
    for t in range(taps):
        rows_scr[t : t + 1, :] = jnp.sum(acc_scr[t], axis=0, keepdims=True) * factor
    rows_scr[taps : taps + 5, :] = chan_ref[0:5, 0:C]
    columns = exchange_order(rows_scr[...].T, cs, count, me)
    out_ref[...] = jnp.zeros_like(out_ref)
    hs = chan_ref.shape[1] // count
    for s in range(count):
        out_ref[s, 0:cs, :] = columns[order[s] * cs : (order[s] + 1) * cs, :]
        out_ref[s, cs : cs + 1, 0:hs] = chan_ref[5:6, s * hs : (s + 1) * hs]


def features_grad_body(ms, taps_i, taps_j, inner, got_ra, got_rb, got_ca, got_cb, small_ref, cot_ref, out_ref, ext_scr, kb_scr):
    batch, rows, cols, C = inner.shape
    m = taps_i // 2
    taps = taps_i * taps_j
    fill(ms, ext_scr, inner, got_ra, got_rb, lambda b, r: got_ca[b, r, 0 : taps_i // 2], got_cb)
    for t in range(taps):
        kb_scr[t] = jnp.broadcast_to(small_ref[t : t + 1, :], (8, C))

    def step(b, _):
        for q in range(0, cols, 8):
            acc = depthwise_block(
                lambda r, j: ext_scr[b, r, LEFT - m + q + j : LEFT - m + q + j + 8, :],
                lambda i, j: kb_scr[taps - 1 - (i * taps_j + j)],
                rows, taps_i, taps_j, [cot_ref[b, p, q : q + 8, :] for p in range(rows)],
            )
            for p in range(rows):
                out_ref[b, p, q : q + 8, :] = acc[p]
        return 0

    lax.fori_loop(0, batch, step, 0)


def finish_body(taps_i, taps_j, cs, hs, *refs):
    parts, outs = refs[:-9], refs[-9:]
    total = parts[0][...]
    for part in parts[1:]:
        total = total + part[...]
    kernel_out, cb, ng, ns, win_out, ib, wout_out, ob, ls = outs
    taps = taps_i * taps_j
    win_out[...] = total[0:hs, :]
    wout_out[...] = total[hs : 2 * hs, :]
    small = total[2 * hs : 2 * hs + 8, :]
    for i in range(taps_i):
        kernel_out[i] = small[0:cs, i * taps_j : (i + 1) * taps_j]
    flipped = small.T
    for n, ref in enumerate((cb, ng, ns, ob, ls)):
        ref[...] = flipped[taps + n : taps + n + 1, 0:cs]
    ib[...] = small[cs : cs + 1, 0:hs]


def flip(x, mask, count):
    return lax.ppermute(x, AXES, [(i, i ^ mask) for i in range(count)])


def groups_of(ms):
    bits_col = ms["col"].bit_length() - 1
    bits_row = ms["row"].bit_length() - 1
    col = [1 << k for k in range(bits_col)]
    row = [1 << (k + bits_col) for k in range(bits_row)]
    rest = col[1:]
    out = [rest[k : k + 2] for k in range(0, len(rest), 2)]
    out += [row[k : k + 2] for k in range(0, len(row), 2)]
    return out + [col[:1]]


def masks(group):
    out = [0]
    for bit in group:
        out += [bit ^ x for x in out]
    return out


def per_device(ms, features, cotangent, conv_kernel, conv_bias, norm_gain, norm_shift, w_in, in_bias, w_out, out_bias, layer_scale):
    batch, rows, cols, C = features.shape
    taps_i, taps_j, cs = conv_kernel.shape
    hs = w_out.shape[0]
    count = ms["row"] * ms["col"]
    hid = hs * count
    m = taps_i // 2
    taps = taps_i * taps_j
    cells = batch * rows * cols * count
    factor = 1.0 / math.sqrt(cells)
    slot = 2 * hs + 8
    wide = ceil8(LEFT + cols + m)

    vm = pltpu.VMEM
    vectors = [v.reshape(1, cs) for v in (conv_bias, norm_gain, norm_shift, out_bias, layer_scale)]
    block, row_a, row_b = call(
        start_body,
        (
            shape(slot, LANES),
            *(shape(batch, m, cols, C) for _ in range(2)),
        ),
        scratch=(
            vm((taps_i, cs, taps_j), f32),
            *(vm((1, cs), f32) for _ in range(5)),
            vm((1, hs), f32),
            vm((hs, C), f32),
            vm((hs, C), f32),
            pltpu.SemaphoreType.DMA((11,)),
        ),
        size=10**6,
        limit=None,
        in_specs=[pl.BlockSpec(memory_space=pl.ANY)] * 10,
    )(features, conv_kernel.transpose(0, 2, 1), *vectors, w_in.T, in_bias.reshape(1, hs), w_out)

    wide_m = (m + 3) // 4 * 4
    edges = (shape(batch, rows + 2 * m, m, C), shape(batch, rows + 2 * m, wide_m, C))
    anywhere, in_vmem = pl.BlockSpec(memory_space=pl.ANY), pl.BlockSpec(memory_space=pltpu.VMEM)
    groups = groups_of(ms)
    order = [0]
    got_ra, got_rb = both_pairs(row_a, row_b, "row")
    parts = [block[None]]
    for n, group in enumerate(groups[:-1]):
        if n == 1:
            slots, edge_a, edge_b = call(
                functools.partial(first_join_body, ms),
                (shape(len(order), slot, LANES), *edges),
                scratch=[vm((batch, rows, m, C), f32) for _ in range(2)],
            )(features, got_ra, got_rb, *parts)
            got_cb = lax.ppermute(edge_b, "col", pairs(ms["col"], True))
        else:
            slots = jnp.concatenate(parts)
        parts = [slots] + [flip(slots, mask, count) for mask in masks(group)[1:]]
        order = [mask ^ x for mask in masks(group) for x in order]
    half = count // 2
    message = call(
        message_body,
        shape(half * slot + edges[0].shape[0] * edges[0].shape[1] * wide_m, LANES),
        in_specs=[anywhere] + [in_vmem] * (1 + len(parts)),
    )(got_cb, edge_a, *parts)
    last = groups[-1][0]
    order += [last ^ x for x in order]
    got = flip(message, last, count)
    tile = rows * cols
    src, dconv, d_row_a, d_row_b, d_edge_a, d_edge_b, grads, chan, small = call(
        functools.partial(mix_body, ms, order, factor, taps_i, taps_j, tile),
        (
            shape(batch, rows + 2 * m, wide, C),
            shape(batch, rows, cols, C),
            *(shape(batch, m, cols, C) for _ in range(2)),
            *(shape(batch, rows, m, C) for _ in range(2)),
            shape(count, 2 * hs, C),
            shape(8, hid),
            shape(LANES, C),
        ),
        scratch=(
            vm((batch, rows + 2 * m, wide, C), f32),
            vm((batch, rows, cols, C), f32),
            vm((C, LANES), f32),
            vm((taps, 8, C), f32),
            vm((hid, C), f32),
            vm((hid, C), f32),
            vm((hid, 3 * C), bf16),
            vm((hid, 3 * C), bf16),
            vm((2 * C, hid), bf16),
            vm((hid, LANES), f32),
            vm((ceil8(max(count, LANES)), LANES), f32),
            vm((hid, 2 * C), f32),
            vm((hid, 2 * C), f32),
            vm((hid, LANES), f32),
            vm((C, LANES), f32),
            vm((C, LANES), f32),
            vm((C, LANES), f32),
            vm((8, C), f32),
        ),
        flops=12 * 10**9,
        size=8 * 10**6,
        limit=24,
    )(features, got_ra, got_rb, got_cb, message, got, cotangent)

    d_got_ra, d_got_rb = both_pairs(d_row_a, d_row_b, "row")
    large_got = flip(grads[half:], last, count)
    smalls = call(
        functools.partial(kernel_grad_body, ms, order, factor, taps_i, taps_j, count),
        shape(count, 8, LANES),
        scratch=(
            vm((batch, rows + 2 * m, wide, C), f32),
            vm((batch, rows, cols + 8, C), f32),
            vm((taps, 8, C), f32),
            vm((LANES, C), f32),
        ),
        flops=4 * 10**9,
        size=4 * 10**6,
    )(src, dconv, chan)
    small_got = flip(smalls[half:], last, count)
    ways = len(masks(groups[-2]))
    *parts, edge_a, edge_b = call(
        functools.partial(back_join_body, ms),
        (*(shape(half // ways, slot, LANES) for _ in range(ways)), edges[1], edges[1]),
    )(d_edge_a, d_edge_b, d_got_ra, d_got_rb, grads, large_got, smalls, small_got)
    d_got_ca, d_got_cb = both_pairs(edge_a, edge_b, "col")
    for n, group in reversed(list(enumerate(groups[:-1]))):
        parts = [parts[0]] + [flip(part, mask, count) for part, mask in zip(parts[1:], masks(group)[1:])]
        if n:
            whole = parts[0]
            for part in parts[1:]:
                whole = whole + part
            ways = len(masks(groups[n - 1]))
            step = whole.shape[0] // ways
            parts = [whole[k * step : (k + 1) * step] for k in range(ways)]

    features_grad = call(
        functools.partial(features_grad_body, ms, taps_i, taps_j),
        shape(batch, rows, cols, C),
        scratch=(
            vm((batch, rows + 2 * m, wide, C), f32),
            vm((taps, 8, C), f32),
        ),
        flops=4 * 10**9,
        size=4 * 10**6,
    )(dconv, d_got_ra, d_got_rb, d_got_ca, d_got_cb, small, cotangent)

    outs = call(
        functools.partial(finish_body, taps_i, taps_j, cs, hs),
        (
            shape(taps_i, cs, taps_j),
            *(shape(1, cs) for _ in range(3)),
            shape(hs, C),
            shape(1, hs),
            shape(hs, C),
            *(shape(1, cs) for _ in range(2)),
        ),
        size=100000,
    )(*(p.reshape(slot, LANES) for p in parts))
    kernel_grad, cb, ng, ns, win, ib, wout, ob, ls = outs
    return (
        features_grad,
        kernel_grad.transpose(0, 2, 1),
        cb.reshape(cs),
        ng.reshape(cs),
        ns.reshape(cs),
        win.T,
        ib.reshape(hs),
        wout,
        ob.reshape(cs),
        ls.reshape(cs),
    )


def solution(mesh):
    both = P(AXES)
    tiles = P(None, "row", "col", None)
    in_specs = (
        tiles, tiles, P(None, None, AXES), both, both, both, P(None, AXES), both, P(AXES, None), both, both,
    )
    out_specs = (
        tiles, P(None, None, AXES), both, both, both, P(None, AXES), both, P(AXES, None), both, both,
    )
    return jax.shard_map(
        functools.partial(per_device, dict(mesh.shape)),
        mesh=mesh, in_specs=in_specs, out_specs=out_specs, check_vma=False,
    )
```
